512 devices in a mesh: dp: 64 (over z, x, y_hi), mp: 8 (over y_lo, core).
Axes of the slice: x: 4, y: 8 (y_hi: 2, y_lo: 4; y = y_hi * 4 + y_lo), z: 8, core: 2. Of those that a mesh axis runs over, the one named last changes fastest.
Arguments:
- query_emb: bfloat16 [512, 4096], P('dp', 'mp'), as said below
- item_emb: bfloat16 [512, 4096], P('dp', 'mp'), as said below
- pair_index: int32 [512], P('dp'), may hold values from 0 to 511, each once
- hard_index: int32 [512, 4], P('dp'), may hold values from 0 to 511
- hidden_in: bfloat16 [2, 64, 152, 4096], P(None, 'dp', None, 'mp'), may hold values from -24 to 24
- lengths: int32 [2, 64], P(None, 'dp'), may hold values from 76 to 152
- w_query: bfloat16 [4096, 4096], P('dp', 'mp'), as said below
- key_weight_matrix: bfloat16 [4096, 1024], P(None, 'mp'), as said below
- value_weight_matrix: bfloat16 [4096, 1024], P(None, 'mp'), may hold values from -0.09375 to 0.09375
- w_out: bfloat16 [4096, 4096], P('mp', 'dp'), may hold values from -0.09375 to 0.09375
- key_down_matrix: bfloat16 [4096, 16], replicated, may hold values from -0.09375 to 0.09375
- key_up_matrix: bfloat16 [16, 1024], P(None, 'mp'), may hold values from -0.29882812 to 0.29882812
- value_down: bfloat16 [4096, 16], replicated, may hold values from -0.09375 to 0.09375
- value_up_matrix: bfloat16 [16, 1024], P(None, 'mp'), may hold values from -0.29882812 to 0.29882812
Outputs:
- mean_loss: float32 [], replicated
- query_grad: bfloat16 [512, 4096], P('dp', 'mp')
- item_grad: bfloat16 [512, 4096], P('dp', 'mp')
- input_grad: bfloat16 [2, 64, 152, 4096], P(None, 'dp', None, 'mp')
- key_down_grad: float32 [4096, 16], replicated
- value_down_grad: float32 [4096, 16], replicated
- key_up_grad: float32 [16, 1024], P(None, 'mp')
- value_up_grad: float32 [16, 1024], P(None, 'mp')
The draws below stay inside these ranges and needn't reach their ends.
Inputs may be any that keep to these rules, and one draw needn't show every extreme that they name: `query_emb`: entries within 10 / sqrt(4096) in magnitude. `item_emb`: entries within 10 / sqrt(4096) in magnitude. `w_query`: entries within 16 / sqrt(4096) in magnitude. `key_weight_matrix`: entries within 6 / sqrt(4096) in magnitude.
All inputs are finite; a program needn't handle non-finite values.
Results may differ from the reference program's by a relative error of at most 0.025.
The reference program's roundings to bfloat16 on the way count: a program that leaves them out, or rounds other values in their place, can miss the bound.
Values may be sent and summed in bfloat16 or wider, within the bound.
No kernel may reach another device: no remote copies, remote signals or barrier semaphores. Data moves between devices by JAX's collectives and lax.ppermute only.
A program may use at most 64 MiB of HBM per device.

```python
import math
import jax
import jax.numpy as jnp
from jax import lax

D = 4096
HEADS = 32
KV_HEADS = 8
HEAD_DIM = 128
RANK = 16
HARD = 4
SUBS = 2
B_DEV = 8
LEN = 152
BATCH = 512
SEQS = 64
N_MP = 8


def draw_rows(base_key):
    normal_part = jnp.clip(jax.random.normal(jax.random.fold_in(base_key, 1), (BATCH, D)), -6.0, 6.0)
    return normal_part / math.sqrt(D)


def embed_pair(key):
    queries = draw_rows(jax.random.fold_in(key, 11))
    items = draw_rows(jax.random.fold_in(key, 12))
    anchors = jnp.array([0, BATCH // 3, 2 * BATCH // 3, BATCH - 1], dtype=jnp.int32)
    for offset, lowered in ((1, 0.0), (BATCH // 2, 0.04)):
        targets = (anchors + offset) % BATCH
        blended = items[targets]
        items = items.at[targets].set(blended)
    return (queries, items)


def draw_query_emb(key, part):
    queries, items = embed_pair(key)
    return queries.astype(jnp.bfloat16)


def draw_item_emb(key, part):
    queries, items = embed_pair(key)
    return items.astype(jnp.bfloat16)


def key_basis(key):
    return jnp.clip(jax.random.normal(jax.random.fold_in(key, 21), (D, KV_HEADS * HEAD_DIM)), -6.0, 6.0)


def draw_key_weight_matrix(key, part):
    basis = key_basis(key)
    return (basis / math.sqrt(D)).astype(jnp.bfloat16)


def draw_w_query(key, part):
    key = jax.random.fold_in(key, 6)
    own_part = jnp.clip(jax.random.normal(key, (D, HEADS * HEAD_DIM)), -6.0, 6.0)
    mixed = own_part
    return (mixed / math.sqrt(D)).astype(jnp.bfloat16)


def draw_hidden_in(key, part):
    key = jax.random.fold_in(key, 7)
    extent = (SUBS, SEQS, LEN, D)
    normal_part = jnp.clip(jax.random.normal(jax.random.fold_in(key, 1), extent), -6.0, 6.0)
    seq_order = jnp.arange(SEQS, dtype=jnp.int32)[None, :] * SUBS + jnp.arange(SUBS, dtype=jnp.int32)[:, None]
    heavy_column = (seq_order % D).reshape(SUBS, SEQS, 1, 1)
    feature_ids = jnp.arange(D, dtype=jnp.int32).reshape(1, 1, 1, D)
    heavy = 14.0 * (feature_ids == heavy_column).astype(jnp.float32)
    mixed = normal_part + heavy
    return jnp.clip(mixed, -24.0, 24.0).astype(jnp.bfloat16)


def draw_lengths(key, part):
    key = jax.random.fold_in(key, 9)
    drawn = jax.random.randint(key, (SUBS, SEQS), LEN // 2, LEN + 1)
    return drawn.at[0, 0].set(LEN).astype(jnp.int32)


def set_ends(entries, rng, least, largest):
    longest = entries.shape.index(max(entries.shape))
    spots = []
    for shift in (0, 1):
        where = [jax.random.randint(jax.random.fold_in(rng, axis), (), 0, length) for axis, length in enumerate(entries.shape)]
        where[longest] = (where[longest] + shift) % entries.shape[longest]
        spots.append(tuple(where))
    return entries.at[spots[0]].set(least).at[spots[1]].set(largest)


def shard_levels(stream_key, dims, pieces, least, top_value):
    gain = 1.0
    for position, shards_of in pieces:
        heights = jax.random.uniform(jax.random.fold_in(jax.random.fold_in(stream_key, 6), position), (shards_of,), jnp.float32, least / len(pieces), top_value / len(pieces))
        gain = gain * jnp.repeat(jnp.exp(heights), dims[position] // shards_of).reshape((-1,) + (1,) * (len(dims) - 1 - position))
    return gain


def noise(stream_key, shape, scale, reach, shards=(), kind=jnp.bfloat16):
    values = scale * jax.random.normal(stream_key, shape, jnp.float32)
    if shards:
        values = values * shard_levels(stream_key, shape, shards, -0.22, 0.18)
    return jnp.clip(values, -reach, reach).astype(kind)


def setup_inputs(seed: int = 0) -> dict:
    key_of = jax.random.split(jax.random.key(seed), 15)
    query_emb = draw_query_emb(jax.random.fold_in(key_of[14], 71), 0)
    item_emb = draw_item_emb(jax.random.fold_in(key_of[14], 71), 0)
    pair_index = jax.random.permutation(key_of[2], BATCH).astype(jnp.int32)
    hard_index = set_ends(jax.random.randint(key_of[3], (BATCH, HARD), 0, BATCH), jax.random.fold_in(key_of[3], 1), 0, BATCH - 1).astype(jnp.int32)
    hidden_in = draw_hidden_in(jax.random.fold_in(key_of[14], 71), 0)
    lengths = draw_lengths(jax.random.fold_in(key_of[14], 71), 0)
    w_query = draw_w_query(jax.random.fold_in(key_of[14], 71), 0)
    key_weight_matrix = draw_key_weight_matrix(jax.random.fold_in(key_of[14], 71), 0)
    value_weight_matrix = noise(key_of[8], (D, KV_HEADS * HEAD_DIM), D ** -0.5, 0.09375, ((1, 8),))
    w_out = noise(key_of[9], (HEADS * HEAD_DIM, D), (HEADS * HEAD_DIM) ** -0.5, 0.09375, ((0, 8), (1, 64)))
    key_down_matrix = noise(key_of[10], (D, RANK), D ** -0.5, 0.09375)
    key_up_matrix = noise(key_of[11], (RANK, KV_HEADS * HEAD_DIM), 0.05, 0.29882812, ((1, 8),))
    value_down = noise(key_of[12], (D, RANK), D ** -0.5, 0.09375)
    value_up_matrix = noise(key_of[13], (RANK, KV_HEADS * HEAD_DIM), 0.05, 0.29882812, ((1, 8),))
    return {"query_emb": query_emb, "item_emb": item_emb, "pair_index": pair_index, "hard_index": hard_index, "hidden_in": hidden_in, "lengths": lengths, "w_query": w_query, "key_weight_matrix": key_weight_matrix, "value_weight_matrix": value_weight_matrix, "w_out": w_out, "key_down_matrix": key_down_matrix, "key_up_matrix": key_up_matrix, "value_down": value_down, "value_up_matrix": value_up_matrix}


INV_TEMP = 50.0
HARD_NEGATIVE_ADD = 4.0
ADAPTER_SCALE = 2.0

def final_product(left_side, right_side):
    return lax.dot_general(left_side, right_side, (((1,), (1,)), ((), ())), preferred_element_type=jnp.float32)

def first_product(left_side, right_side):
    return lax.dot_general(left_side, right_side, (((0,), (0,)), ((), ())), preferred_element_type=jnp.float32)

def rounded(value):
    return lax.optimization_barrier(value.astype(jnp.bfloat16)).astype(jnp.float32)

def reference(query_emb, item_emb, pair_index, hard_index, hidden_in, lengths, w_query, key_weight_matrix, value_weight_matrix, w_out, key_down_matrix, key_up_matrix, value_down, value_up_matrix):
    columns = jnp.arange(BATCH, dtype=jnp.int32)
    pair_scores = final_product(query_emb, item_emb) * INV_TEMP
    hard_negative_count = lax.optimization_barrier(jnp.sum((hard_index[:, :, None] == columns[None, None, :]).astype(jnp.float32), axis=1))
    score_logits = pair_scores + HARD_NEGATIVE_ADD * hard_negative_count
    row_top = lax.optimization_barrier(jnp.max(score_logits, axis=1, keepdims=True))
    log_total = row_top[:, 0] + jnp.log(lax.optimization_barrier(jnp.sum(jnp.exp(score_logits - row_top), axis=1)))
    target = (pair_index[:, None] == columns[None, :]).astype(jnp.float32)
    picked = lax.optimization_barrier(jnp.sum(target * score_logits, axis=1))
    mean_loss = jnp.sum(log_total - picked) / BATCH
    residual = (jnp.exp(score_logits - log_total[:, None]) - target).astype(jnp.bfloat16)
    query_grad = (jnp.dot(residual, item_emb, preferred_element_type=jnp.float32) * INV_TEMP).astype(jnp.bfloat16)
    item_grad = (first_product(residual, query_emb) * INV_TEMP).astype(jnp.bfloat16)
    group_size = HEADS // KV_HEADS
    key_width = KV_HEADS * HEAD_DIM // N_MP
    query_width = HEADS * HEAD_DIM // N_MP
    score_scale = 1.0 / math.sqrt(HEAD_DIM)
    flat_x = hidden_in.reshape(SUBS * SEQS, LEN, D)
    flat_len = lengths.reshape(SUBS * SEQS)
    seq_ids = jnp.arange(SUBS * SEQS, dtype=jnp.int32)
    item_rows = seq_ids % SEQS * B_DEV + seq_ids // SEQS
    cotangents = jnp.take(item_grad, item_rows, axis=0)
    key_down_float = key_down_matrix.astype(jnp.float32)
    value_down_float = value_down.astype(jnp.float32)

    def one_sequence(state_sum, packed):
        token_inputs, length, cotangent = packed
        reduced_key = jnp.dot(token_inputs, key_down_matrix, preferred_element_type=jnp.float32).astype(jnp.bfloat16)
        reduced_value = jnp.dot(token_inputs, value_down, preferred_element_type=jnp.float32).astype(jnp.bfloat16)
        key_rows = (jnp.dot(token_inputs, key_weight_matrix, preferred_element_type=jnp.float32) + ADAPTER_SCALE * jnp.dot(reduced_key, key_up_matrix, preferred_element_type=jnp.float32)).astype(jnp.bfloat16)
        value_rows = (jnp.dot(token_inputs, value_weight_matrix, preferred_element_type=jnp.float32) + ADAPTER_SCALE * jnp.dot(reduced_value, value_up_matrix, preferred_element_type=jnp.float32)).astype(jnp.bfloat16)
        last_tokens = lax.dynamic_slice_in_dim(token_inputs, (length - 1).astype(jnp.int32), 1, 0)
        query = jnp.dot(last_tokens, w_query, preferred_element_type=jnp.float32).astype(jnp.bfloat16)
        q_heads = query.reshape(KV_HEADS, group_size, HEAD_DIM).astype(jnp.float32)
        k_heads = key_rows.reshape(LEN, KV_HEADS, HEAD_DIM).astype(jnp.float32)
        v_heads = value_rows.reshape(LEN, KV_HEADS, HEAD_DIM).astype(jnp.float32)
        raw_scores = jnp.einsum('kgd,jkd->kgj', q_heads, k_heads) * score_scale
        live_mask = jnp.arange(LEN, dtype=jnp.int32) < length
        raw_scores = jnp.where(live_mask[None, None, :], raw_scores, -jnp.inf)
        row_peak = lax.optimization_barrier(jnp.max(raw_scores, axis=-1, keepdims=True))
        weights = jnp.exp(raw_scores - row_peak)
        softmax_probs = weights / lax.optimization_barrier(jnp.sum(weights, axis=-1, keepdims=True))
        attn_grad = final_product(cotangent[None, :], w_out).astype(jnp.bfloat16)
        grad_heads = attn_grad.reshape(KV_HEADS, group_size, HEAD_DIM).astype(jnp.float32)
        prob_grad = jnp.einsum('kgd,jkd->kgj', grad_heads, v_heads)
        score_grad = rounded(softmax_probs * (prob_grad - lax.optimization_barrier(jnp.sum(softmax_probs * prob_grad, axis=-1, keepdims=True))) * score_scale)
        query_delta = jnp.einsum('kgj,jkd->kgd', score_grad, k_heads).astype(jnp.bfloat16).reshape(1, HEADS * HEAD_DIM)
        key_adapter_change = jnp.einsum('kgj,kgd->jkd', score_grad, q_heads).astype(jnp.bfloat16).reshape(LEN, KV_HEADS * HEAD_DIM)
        value_adapter_change = jnp.einsum('kgj,kgd->jkd', rounded(softmax_probs), grad_heads).astype(jnp.bfloat16).reshape(LEN, KV_HEADS * HEAD_DIM)
        grad_sum = jnp.zeros((LEN, D), jnp.float32)
        key_down_total, value_down_total, key_up_total, value_up_total = state_sum
        for shard_index in range(N_MP):
            key_start = shard_index * key_width
            key_stop = key_start + key_width
            query_start = shard_index * query_width
            query_stop = query_start + query_width
            key_coefficient = final_product(key_adapter_change[:, key_start:key_stop], key_up_matrix[:, key_start:key_stop]).astype(jnp.bfloat16)
            value_coefficient = final_product(value_adapter_change[:, key_start:key_stop], value_up_matrix[:, key_start:key_stop]).astype(jnp.bfloat16)
            portion_total = final_product(key_adapter_change[:, key_start:key_stop], key_weight_matrix[:, key_start:key_stop]) + final_product(value_adapter_change[:, key_start:key_stop], value_weight_matrix[:, key_start:key_stop])
            portion_total = portion_total + ADAPTER_SCALE * (final_product(key_coefficient.astype(jnp.float32), key_down_float) + final_product(value_coefficient.astype(jnp.float32), value_down_float))
            last_part = final_product(query_delta[:, query_start:query_stop], w_query[:, query_start:query_stop])
            portion_total = portion_total.at[length - 1].add(last_part[0])
            grad_sum = grad_sum + rounded(portion_total)
            key_down_total = key_down_total + ADAPTER_SCALE * first_product(token_inputs, key_coefficient)
            value_down_total = value_down_total + ADAPTER_SCALE * first_product(token_inputs, value_coefficient)
        grad_sum = grad_sum.at[length - 1].add(cotangent.astype(jnp.float32))
        key_up_total = key_up_total + ADAPTER_SCALE * first_product(reduced_key, key_adapter_change)
        value_up_total = value_up_total + ADAPTER_SCALE * first_product(reduced_value, value_adapter_change)
        return ((key_down_total, value_down_total, key_up_total, value_up_total), grad_sum.astype(jnp.bfloat16))
    start_state = (jnp.zeros((D, RANK), jnp.float32), jnp.zeros((D, RANK), jnp.float32), jnp.zeros((RANK, KV_HEADS * HEAD_DIM), jnp.float32), jnp.zeros((RANK, KV_HEADS * HEAD_DIM), jnp.float32))
    final_state, grad_rows = lax.scan(one_sequence, start_state, (flat_x, flat_len, cotangents))
    input_grad = grad_rows.reshape(SUBS, SEQS, LEN, D)
    return (mean_loss, query_grad, item_grad, input_grad, final_state[0], final_state[1], final_state[2], final_state[3])
```

```python
import math

import jax
import jax.numpy as jnp
from jax import lax
from jax.sharding import Mesh
from jax.sharding import PartitionSpec as P

HEADS = 32
KV_HEADS = 8
HEAD_DIM = 128

INV_TEMP = 50.0
HARD_NEGATIVE_ADD = 4.0
ADAPTER_SCALE = 2.0

DP = ("z", "x", "h")


def final_product(left_side, right_side):
    return lax.dot_general(
        left_side, right_side, (((1,), (1,)), ((), ())), preferred_element_type=jnp.float32
    )


def first_product(left_side, right_side):
    return lax.dot_general(
        left_side, right_side, (((0,), (0,)), ((), ())), preferred_element_type=jnp.float32
    )


def spread(block, axes):
    count = lax.axis_size(axes)
    copies = jnp.broadcast_to(block[None], (count,) + block.shape)
    return lax.all_to_all(copies, axes, split_axis=0, concat_axis=0, tiled=True)


def swap(blocks, axes):
    return lax.all_to_all(blocks, axes, split_axis=0, concat_axis=0, tiled=True)


def local(
    query_emb,
    item_emb,
    pair_index,
    hard_index,
    hidden_in,
    lengths,
    w_query,
    key_weight_matrix,
    value_weight_matrix,
    w_out,
    key_down_matrix,
    key_up_matrix,
    value_down,
    value_up_matrix,
):
    dp_count = lax.axis_size(DP)
    mp_count = lax.axis_size("mp")
    local_rows = query_emb.shape[0]
    batch_size = local_rows * dp_count
    feature_width = query_emb.shape[1]

    sub_count = hidden_in.shape[0]
    seq_len = hidden_in.shape[2]
    full_rows = lax.all_gather(hidden_in, "mp", axis=3, tiled=True)
    model_width = full_rows.shape[3]
    token_inputs = full_rows.reshape(sub_count * seq_len, model_width)
    seq_lengths = lengths[:, 0]
    last_rows = jnp.arange(sub_count, dtype=jnp.int32) * seq_len + seq_lengths - 1
    last_tokens = jnp.take(token_inputs, last_rows, axis=0)

    rows_here, query_width = w_query.shape
    both = jnp.stack([w_query, w_out.T])
    both = lax.all_gather(both, "h", axis=0, tiled=False)
    both = spread(both, "x")
    plane_rows = both.shape[0] * both.shape[1] * rows_here
    wq_plane = both[:, :, 0].reshape(plane_rows, query_width)
    wo_plane = both[:, :, 1].reshape(plane_rows, query_width)
    wq_full = lax.all_gather(wq_plane, "z", axis=0, tiled=True)
    wo_full = lax.all_gather(wo_plane, "z", axis=0, tiled=True)

    emb_all = spread(jnp.concatenate([item_emb, query_emb], axis=0), DP)
    items_all = emb_all[:, :local_rows].reshape(batch_size, feature_width)
    queries_all = emb_all[:, local_rows:].reshape(batch_size, feature_width)
    partial_scores = final_product(query_emb, items_all)
    pair_scores = jnp.sum(spread(partial_scores, "mp"), axis=0) * INV_TEMP
    columns = jnp.arange(batch_size, dtype=jnp.int32)
    hard_negative_count = jnp.sum(
        (hard_index[:, :, None] == columns[None, None, :]).astype(jnp.float32), axis=1
    )
    score_logits = pair_scores + HARD_NEGATIVE_ADD * hard_negative_count
    row_top = jnp.max(score_logits, axis=1, keepdims=True)
    log_total = row_top[:, 0] + jnp.log(jnp.sum(jnp.exp(score_logits - row_top), axis=1))
    target = (pair_index[:, None] == columns[None, :]).astype(jnp.float32)
    picked = jnp.sum(target * score_logits, axis=1)
    loss_part = jnp.sum(log_total - picked)
    residual = (jnp.exp(score_logits - log_total[:, None]) - target).astype(jnp.bfloat16)
    residual_columns = swap(
        residual.reshape(local_rows, dp_count, local_rows).transpose(1, 0, 2), DP
    ).reshape(batch_size, local_rows)
    item_grad = (first_product(residual_columns, queries_all) * INV_TEMP).astype(jnp.bfloat16)
    query_grad = (
        jnp.dot(residual, items_all, preferred_element_type=jnp.float32) * INV_TEMP
    ).astype(jnp.bfloat16)
    cot_local = item_grad[:sub_count]
    cot_full = spread(cot_local, "mp").transpose(1, 0, 2).reshape(sub_count, model_width)

    adapter_rank = key_down_matrix.shape[1]
    down_both = jnp.concatenate([key_down_matrix, value_down], axis=1)
    reduced_pair = jnp.dot(token_inputs, down_both, preferred_element_type=jnp.float32).astype(
        jnp.bfloat16
    )
    reduced_key = reduced_pair[:, :adapter_rank]
    reduced_value = reduced_pair[:, adapter_rank:]
    key_rows = (
        jnp.dot(token_inputs, key_weight_matrix, preferred_element_type=jnp.float32)
        + ADAPTER_SCALE * jnp.dot(reduced_key, key_up_matrix, preferred_element_type=jnp.float32)
    ).astype(jnp.bfloat16)
    value_rows = (
        jnp.dot(token_inputs, value_weight_matrix, preferred_element_type=jnp.float32)
        + ADAPTER_SCALE
        * jnp.dot(reduced_value, value_up_matrix, preferred_element_type=jnp.float32)
    ).astype(jnp.bfloat16)
    query = jnp.dot(last_tokens, wq_full, preferred_element_type=jnp.float32).astype(jnp.bfloat16)
    attn_grad = jnp.dot(cot_full, wo_full, preferred_element_type=jnp.float32).astype(jnp.bfloat16)
    group_size = HEADS // KV_HEADS
    kv_local = key_rows.shape[1] // HEAD_DIM
    score_scale = 1.0 / math.sqrt(HEAD_DIM)
    q_heads = query.reshape(sub_count, kv_local, group_size, HEAD_DIM)
    k_heads = key_rows.reshape(sub_count, seq_len, kv_local, HEAD_DIM)
    v_heads = value_rows.reshape(sub_count, seq_len, kv_local, HEAD_DIM)
    raw_scores = (
        jnp.einsum("bkgd,bjkd->bkgj", q_heads, k_heads, preferred_element_type=jnp.float32)
        * score_scale
    )
    live_mask = jnp.arange(seq_len, dtype=jnp.int32)[None, :] < seq_lengths[:, None]
    raw_scores = jnp.where(live_mask[:, None, None, :], raw_scores, -jnp.inf)
    row_peak = jnp.max(raw_scores, axis=-1, keepdims=True)
    weights = jnp.exp(raw_scores - row_peak)
    softmax_probs = weights / jnp.sum(weights, axis=-1, keepdims=True)
    prob_half = softmax_probs.astype(jnp.bfloat16)
    grad_heads = attn_grad.reshape(sub_count, kv_local, group_size, HEAD_DIM)
    prob_grad = jnp.einsum(
        "bkgd,bjkd->bkgj", grad_heads, v_heads, preferred_element_type=jnp.float32
    )
    score_grad = (
        softmax_probs
        * (prob_grad - jnp.sum(softmax_probs * prob_grad, axis=-1, keepdims=True))
        * score_scale
    ).astype(jnp.bfloat16)
    query_delta = (
        jnp.einsum("bkgj,bjkd->bkgd", score_grad, k_heads, preferred_element_type=jnp.float32)
        .astype(jnp.bfloat16)
        .reshape(sub_count, query_width)
    )
    key_adapter_change = (
        jnp.einsum("bkgj,bkgd->bjkd", score_grad, q_heads, preferred_element_type=jnp.float32)
        .astype(jnp.bfloat16)
        .reshape(sub_count * seq_len, kv_local * HEAD_DIM)
    )
    value_adapter_change = (
        jnp.einsum("bkgj,bkgd->bjkd", prob_half, grad_heads, preferred_element_type=jnp.float32)
        .astype(jnp.bfloat16)
        .reshape(sub_count * seq_len, kv_local * HEAD_DIM)
    )
    last_part = final_product(query_delta, wq_full)
    key_coefficient = final_product(key_adapter_change, key_up_matrix).astype(jnp.bfloat16)
    value_coefficient = final_product(value_adapter_change, value_up_matrix).astype(jnp.bfloat16)
    input_portion = final_product(key_adapter_change, key_weight_matrix) + final_product(
        value_adapter_change, value_weight_matrix
    )
    input_portion = input_portion + ADAPTER_SCALE * (
        final_product(key_coefficient, key_down_matrix)
        + final_product(value_coefficient, value_down)
    )
    input_portion = input_portion.at[last_rows].add(last_part)
    input_sum = lax.psum_scatter(
        input_portion.astype(jnp.bfloat16), "mp", scatter_dimension=1, tiled=True
    ).astype(jnp.float32)
    input_sum = input_sum.at[last_rows].add(cot_local.astype(jnp.float32))
    input_grad = input_sum.astype(jnp.bfloat16).reshape(hidden_in.shape)

    own_rows = hidden_in.reshape(sub_count * seq_len, feature_width)
    coefficients = spread(jnp.concatenate([key_coefficient, value_coefficient], axis=1), "mp")
    coefficient_sum = jnp.sum(coefficients.astype(jnp.float32), axis=0)
    down_part = ADAPTER_SCALE * lax.dot_general(
        coefficient_sum,
        own_rows.astype(jnp.float32),
        (((0,), (0,)), ((), ())),
        precision=lax.Precision.HIGHEST,
        preferred_element_type=jnp.float32,
    )
    up_part = ADAPTER_SCALE * jnp.concatenate(
        [
            first_product(reduced_key, key_adapter_change),
            first_product(reduced_value, value_adapter_change),
        ],
        axis=0,
    )
    down_cut = down_part.size // dp_count
    up_cut = up_part.size // dp_count
    shares = jnp.concatenate(
        [
            down_part.reshape(dp_count, down_cut),
            up_part.reshape(dp_count, up_cut),
            jnp.broadcast_to(loss_part, (dp_count, HEAD_DIM - up_cut)),
        ],
        axis=1,
    )
    share_sum = jnp.sum(swap(shares, DP), axis=0)
    mean_loss = share_sum[down_cut + up_cut] / batch_size
    summed = spread(share_sum, DP)
    up_grad = summed[:, down_cut : down_cut + up_cut].reshape(up_part.shape)
    down_slice = summed[:, :down_cut].reshape(down_part.shape)
    down_grad = spread(down_slice, "mp").transpose(1, 0, 2).reshape(-1, model_width).T
    return (
        mean_loss,
        query_grad,
        item_grad,
        input_grad,
        down_grad[:, :adapter_rank],
        down_grad[:, adapter_rank:],
        up_grad[:adapter_rank],
        up_grad[adapter_rank:],
    )


def solution(mesh):
    fine = Mesh(
        mesh.devices.reshape(8, 4, 2, mesh.devices.shape[1]), ("z", "x", "h", "mp")
    )
    in_specs = (
        P(DP, "mp"),
        P(DP, "mp"),
        P(DP),
        P(DP, None),
        P(None, DP, None, "mp"),
        P(None, DP),
        P(DP, "mp"),
        P(None, "mp"),
        P(None, "mp"),
        P("mp", DP),
        P(),
        P(None, "mp"),
        P(),
        P(None, "mp"),
    )
    out_specs = (
        P(),
        P(DP, "mp"),
        P(DP, "mp"),
        P(None, DP, None, "mp"),
        P(),
        P(),
        P(None, "mp"),
        P(None, "mp"),
    )
    return jax.shard_map(local, mesh=fine, in_specs=in_specs, out_specs=out_specs, check_vma=False)
```

```python
import math

import jax
import jax.numpy as jnp
from jax import lax
from jax.sharding import Mesh
from jax.sharding import PartitionSpec as P

HEADS = 32
KV_HEADS = 8
HEAD_DIM = 128

INV_TEMP = 50.0
HARD_NEGATIVE_ADD = 4.0
ADAPTER_SCALE = 2.0

PLANE = ("x", "h")
DP = ("z", "x", "h")


def final_product(left_side, right_side):
    return lax.dot_general(
        left_side, right_side, (((1,), (1,)), ((), ())), preferred_element_type=jnp.float32
    )


def first_product(left_side, right_side):
    return lax.dot_general(
        left_side, right_side, (((0,), (0,)), ((), ())), preferred_element_type=jnp.float32
    )


def spread(block, axes):
    count = lax.axis_size(axes)
    copies = jnp.broadcast_to(block[None], (count,) + block.shape)
    return lax.all_to_all(copies, axes, split_axis=0, concat_axis=0, tiled=True)


def swap(blocks, axes):
    return lax.all_to_all(blocks, axes, split_axis=0, concat_axis=0, tiled=True)


def local(
    query_emb,
    item_emb,
    pair_index,
    hard_index,
    hidden_in,
    lengths,
    w_query,
    key_weight_matrix,
    value_weight_matrix,
    w_out,
    key_down_matrix,
    key_up_matrix,
    value_down,
    value_up_matrix,
):
    z_count = lax.axis_size("z")
    plane_count = lax.axis_size(PLANE)
    dp_count = z_count * plane_count
    mp_count = lax.axis_size("mp")
    local_rows = query_emb.shape[0]
    batch_size = local_rows * dp_count
    feature_width = query_emb.shape[1]

    sub_count = hidden_in.shape[0]
    seq_len = hidden_in.shape[2]
    token_count = sub_count * seq_len
    full_rows = lax.all_gather(hidden_in, "mp", axis=3, tiled=True)
    model_width = full_rows.shape[3]
    token_inputs = full_rows.reshape(token_count, model_width)
    seq_lengths = lengths[:, 0]
    last_rows = jnp.arange(sub_count, dtype=jnp.int32) * seq_len + seq_lengths - 1
    last_tokens = jnp.concatenate(
        [
            lax.dynamic_slice_in_dim(token_inputs, last_rows[sub], 1, 0)
            for sub in range(sub_count)
        ],
        axis=0,
    )

    rows_here, query_width = w_query.shape
    both = jnp.stack([w_query, w_out.T])
    other = lax.ppermute(both, "h", [(0, 1), (1, 0)])
    lower = lax.axis_index("h") == 0
    both = jnp.stack([jnp.where(lower, both, other), jnp.where(lower, other, both)])
    both = spread(both, "x")
    plane_rows = plane_count * rows_here
    wq_plane = both[:, :, 0].reshape(plane_rows, query_width)
    wo_plane = both[:, :, 1].reshape(plane_rows, query_width)
    wq_full = lax.all_gather(wq_plane, "z", axis=0, tiled=True)

    query_slices = spread(query_emb, "mp")
    chunks = jnp.concatenate(
        [
            jnp.broadcast_to(item_emb[None], query_slices.shape),
            query_slices,
        ],
        axis=1,
    )
    chunks = jnp.broadcast_to(
        chunks[:, None], (z_count, plane_count) + chunks.shape[1:]
    ).reshape((dp_count,) + chunks.shape[1:])
    emb_all = swap(chunks, DP)
    items_all = emb_all[:, :local_rows].reshape(batch_size, feature_width)
    queries_all = emb_all[:, local_rows:].reshape(batch_size, feature_width)
    partial_scores = final_product(query_emb, items_all)
    score_parts = spread(partial_scores, "mp")

    adapter_rank = key_down_matrix.shape[1]
    down_both = jnp.concatenate([key_down_matrix, value_down], axis=1)
    reduced_pair = jnp.dot(token_inputs, down_both, preferred_element_type=jnp.float32).astype(
        jnp.bfloat16
    )
    reduced_key = reduced_pair[:, :adapter_rank]
    reduced_value = reduced_pair[:, adapter_rank:]
    key_rows = (
        jnp.dot(token_inputs, key_weight_matrix, preferred_element_type=jnp.float32)
        + ADAPTER_SCALE * jnp.dot(reduced_key, key_up_matrix, preferred_element_type=jnp.float32)
    ).astype(jnp.bfloat16)
    value_rows = (
        jnp.dot(token_inputs, value_weight_matrix, preferred_element_type=jnp.float32)
        + ADAPTER_SCALE
        * jnp.dot(reduced_value, value_up_matrix, preferred_element_type=jnp.float32)
    ).astype(jnp.bfloat16)
    score_parts, key_rows, value_rows = lax.optimization_barrier(
        (score_parts, key_rows, value_rows)
    )

    pair_scores = jnp.sum(score_parts, axis=0) * INV_TEMP
    columns = jnp.arange(batch_size, dtype=jnp.int32)
    hard_negative_count = jnp.sum(
        (hard_index[:, :, None] == columns[None, None, :]).astype(jnp.float32), axis=1
    )
    score_logits = pair_scores + HARD_NEGATIVE_ADD * hard_negative_count
    row_top = jnp.max(score_logits, axis=1, keepdims=True)
    log_total = row_top[:, 0] + jnp.log(jnp.sum(jnp.exp(score_logits - row_top), axis=1))
    target = (pair_index[:, None] == columns[None, :]).astype(jnp.float32)
    residual = (jnp.exp(score_logits - log_total[:, None]) - target).astype(jnp.bfloat16)
    plane_columns = (
        residual.reshape(local_rows, z_count, plane_count, local_rows)
        .transpose(2, 0, 1, 3)
        .reshape(1, plane_count, local_rows, z_count * local_rows)
    )
    plane_columns = jnp.broadcast_to(plane_columns, (z_count,) + plane_columns.shape[1:])
    column_rows = swap(
        plane_columns.reshape((dp_count,) + plane_columns.shape[2:]), DP
    ).reshape(batch_size, z_count * local_rows)
    column_grads = (
        (first_product(column_rows, queries_all) * INV_TEMP)
        .astype(jnp.bfloat16)
        .reshape(z_count, local_rows, feature_width)
    )
    cotangents = column_grads[:, :sub_count].reshape(z_count * sub_count, feature_width)
    attn_parts = jnp.dot(cotangents, wo_plane, preferred_element_type=jnp.float32)
    attn_parts = swap(attn_parts.reshape(z_count, sub_count, query_width), "z")
    attn_grad = jnp.sum(attn_parts, axis=0).astype(jnp.bfloat16)
    item_grad = lax.ppermute(
        lax.dynamic_index_in_dim(column_grads, lax.axis_index("mp"), 0, keepdims=False),
        ("z", "mp"),
        [(a * mp_count + b, b * mp_count + a) for a in range(z_count) for b in range(mp_count)],
    )
    picked = jnp.sum(target * score_logits, axis=1)
    loss_part = jnp.sum(log_total - picked)
    query_grad = (
        jnp.dot(residual, items_all, preferred_element_type=jnp.float32) * INV_TEMP
    ).astype(jnp.bfloat16)

    query = jnp.dot(last_tokens, wq_full, preferred_element_type=jnp.float32).astype(jnp.bfloat16)
    group_size = HEADS // KV_HEADS
    kv_local = key_rows.shape[1] // HEAD_DIM
    score_scale = 1.0 / math.sqrt(HEAD_DIM)
    q_heads = query.reshape(sub_count, kv_local, group_size, HEAD_DIM)
    k_heads = key_rows.reshape(sub_count, seq_len, kv_local, HEAD_DIM)
    v_heads = value_rows.reshape(sub_count, seq_len, kv_local, HEAD_DIM)
    raw_scores = (
        jnp.einsum("bkgd,bjkd->bkgj", q_heads, k_heads, preferred_element_type=jnp.float32)
        * score_scale
    )
    live_mask = jnp.arange(seq_len, dtype=jnp.int32)[None, :] < seq_lengths[:, None]
    raw_scores = jnp.where(live_mask[:, None, None, :], raw_scores, -jnp.inf)
    row_peak = jnp.max(raw_scores, axis=-1, keepdims=True)
    weights = jnp.exp(raw_scores - row_peak)
    softmax_probs = weights / jnp.sum(weights, axis=-1, keepdims=True)
    prob_half = softmax_probs.astype(jnp.bfloat16)
    grad_heads = attn_grad.reshape(sub_count, kv_local, group_size, HEAD_DIM)
    prob_grad = jnp.einsum(
        "bkgd,bjkd->bkgj", grad_heads, v_heads, preferred_element_type=jnp.float32
    )
    score_grad = (
        softmax_probs
        * (prob_grad - jnp.sum(softmax_probs * prob_grad, axis=-1, keepdims=True))
        * score_scale
    ).astype(jnp.bfloat16)
    query_delta = (
        jnp.einsum("bkgj,bjkd->bkgd", score_grad, k_heads, preferred_element_type=jnp.float32)
        .astype(jnp.bfloat16)
        .reshape(sub_count, query_width)
    )
    key_adapter_change = (
        jnp.einsum("bkgj,bkgd->bjkd", score_grad, q_heads, preferred_element_type=jnp.float32)
        .astype(jnp.bfloat16)
        .reshape(token_count, kv_local * HEAD_DIM)
    )
    value_adapter_change = (
        jnp.einsum("bkgj,bkgd->bjkd", prob_half, grad_heads, preferred_element_type=jnp.float32)
        .astype(jnp.bfloat16)
        .reshape(token_count, kv_local * HEAD_DIM)
    )
    key_coefficient = final_product(key_adapter_change, key_up_matrix).astype(jnp.bfloat16)
    value_coefficient = final_product(value_adapter_change, value_up_matrix).astype(jnp.bfloat16)

    own_rows = hidden_in.reshape(token_count, feature_width)
    coefficients = spread(jnp.concatenate([key_coefficient, value_coefficient], axis=1), "mp")
    coefficient_sum = jnp.sum(coefficients.astype(jnp.float32), axis=0)
    down_part = ADAPTER_SCALE * lax.dot_general(
        coefficient_sum,
        own_rows.astype(jnp.float32),
        (((0,), (0,)), ((), ())),
        precision=lax.Precision.HIGHEST,
        preferred_element_type=jnp.float32,
    )
    up_part = ADAPTER_SCALE * jnp.concatenate(
        [
            first_product(reduced_key, key_adapter_change),
            first_product(reduced_value, value_adapter_change),
        ],
        axis=0,
    )
    up_width = up_part.shape[1]
    shares = jnp.concatenate(
        [down_part, up_part, jnp.broadcast_to(loss_part, up_part.shape)], axis=1
    )
    shares = shares.reshape(z_count, -1, shares.shape[1])

    shares, key_adapter_change, value_adapter_change, query_delta = lax.optimization_barrier(
        (shares, key_adapter_change, value_adapter_change, query_delta)
    )
    last_part = final_product(query_delta, wq_full)
    input_portion = final_product(key_adapter_change, key_weight_matrix) + final_product(
        value_adapter_change, value_weight_matrix
    )
    input_portion = input_portion + ADAPTER_SCALE * (
        final_product(key_coefficient, key_down_matrix)
        + final_product(value_coefficient, value_down)
    )
    row_ids = jnp.arange(token_count, dtype=jnp.int32)[:, None]
    for sub in range(sub_count):
        input_portion = input_portion + jnp.where(
            row_ids == last_rows[sub], last_part[sub][None, :], 0.0
        )
    input_sum = lax.psum_scatter(
        input_portion.astype(jnp.bfloat16), "mp", scatter_dimension=1, tiled=True
    ).astype(jnp.float32)
    for sub in range(sub_count):
        input_sum = input_sum + jnp.where(
            row_ids == last_rows[sub], item_grad[sub][None, :].astype(jnp.float32), 0.0
        )
    input_grad = input_sum.astype(jnp.bfloat16).reshape(hidden_in.shape)

    share_sum = jnp.sum(swap(shares, "z"), axis=0)
    share_sum = jnp.sum(spread(share_sum, PLANE), axis=0)
    mean_loss = share_sum[0, feature_width + up_width] / batch_size
    summed = spread(share_sum[:, : feature_width + up_width], "z")
    summed = summed.reshape(2 * adapter_rank, feature_width + up_width)
    up_grad = summed[:, feature_width:]
    down_slice = summed[:, :feature_width].astype(jnp.bfloat16)
    down_grad = (
        spread(down_slice, "mp").transpose(1, 0, 2).reshape(-1, model_width).astype(jnp.float32).T
    )
    return (
        mean_loss,
        query_grad,
        item_grad,
        input_grad,
        down_grad[:, :adapter_rank],
        down_grad[:, adapter_rank:],
        up_grad[:adapter_rank],
        up_grad[adapter_rank:],
    )


def solution(mesh):
    fine = Mesh(
        mesh.devices.reshape(8, 4, 2, mesh.devices.shape[1]), ("z", "x", "h", "mp")
    )
    in_specs = (
        P(DP, "mp"),
        P(DP, "mp"),
        P(DP),
        P(DP, None),
        P(None, DP, None, "mp"),
        P(None, DP),
        P(DP, "mp"),
        P(None, "mp"),
        P(None, "mp"),
        P("mp", DP),
        P(),
        P(None, "mp"),
        P(),
        P(None, "mp"),
    )
    out_specs = (
        P(),
        P(DP, "mp"),
        P(DP, "mp"),
        P(None, DP, None, "mp"),
        P(),
        P(),
        P(None, "mp"),
        P(None, "mp"),
    )
    return jax.shard_map(local, mesh=fine, in_specs=in_specs, out_specs=out_specs, check_vma=False)
```

```python
import functools
import math

import jax
import jax.numpy as jnp
from jax import lax
from jax.experimental import pallas as pl
from jax.experimental.pallas import tpu as pltpu
from jax.sharding import Mesh
from jax.sharding import PartitionSpec as P

HEADS = 32
KV_HEADS = 8
HEAD_DIM = 128
LANES = 128

INV_TEMP = 50.0
HARD_NEGATIVE_ADD = 4.0
ADAPTER_SCALE = 2.0

PLANE = ("x", "h")
DP = ("z", "x", "h")


def final_product(left_side, right_side):
    return lax.dot_general(
        left_side, right_side, (((1,), (1,)), ((), ())), preferred_element_type=jnp.float32
    )


def first_product(left_side, right_side):
    return lax.dot_general(
        left_side, right_side, (((0,), (0,)), ((), ())), preferred_element_type=jnp.float32
    )


def spread(block, axes):
    count = lax.axis_size(axes)
    copies = jnp.broadcast_to(block[None], (count,) + block.shape)
    return lax.all_to_all(copies, axes, split_axis=0, concat_axis=0, tiled=True)


def swap(blocks, axes):
    return lax.all_to_all(blocks, axes, split_axis=0, concat_axis=0, tiled=True)


def call(kernel, out_shape, flops):
    return pl.pallas_call(
        kernel,
        out_shape=out_shape,
        compiler_params=pltpu.CompilerParams(vmem_limit_bytes=32 * 1024 * 1024),
        cost_estimate=pl.CostEstimate(flops=flops, bytes_accessed=2**20, transcendentals=4096),
    )


def residual_kernel(z_count, plane_count, parts, hard, pair, chunks, residual_out, loss_out):
    rows = parts.shape[1]
    batch_size = parts.shape[2]
    pair_scores = parts[0]
    for part in range(1, parts.shape[0]):
        pair_scores = pair_scores + parts[part]
    column = lax.broadcasted_iota(jnp.int32, (rows, batch_size), 1)
    inner = column % rows
    outer = column // rows
    item = ((outer % z_count) * plane_count + outer // z_count) * rows + inner
    count = jnp.zeros((rows, batch_size), jnp.float32)
    for choice in range(hard.shape[1]):
        count = count + jnp.where(hard[:, choice : choice + 1] == item, 1.0, 0.0)
    logits = pair_scores * INV_TEMP + HARD_NEGATIVE_ADD * count
    top = jnp.max(logits, axis=1, keepdims=True)
    log_total = top + jnp.log(jnp.sum(jnp.exp(logits - top), axis=1, keepdims=True))
    target = jnp.where(pair[...] == item, 1.0, 0.0)
    picked = jnp.sum(target * logits, axis=1, keepdims=True)
    loss = jnp.sum(log_total - picked, axis=0, keepdims=True)
    loss_out[...] = jnp.broadcast_to(loss, loss_out.shape)
    residual = jnp.exp(logits - log_total) - target
    residual_out[...] = residual.astype(jnp.bfloat16)
    width = z_count * rows
    pad = jnp.zeros((rows, chunks.shape[2] - width), jnp.float32)
    for plane in range(plane_count):
        block = jnp.concatenate([residual[:, plane * width : (plane + 1) * width], pad], axis=1)
        block = block.astype(jnp.bfloat16)
        for z in range(z_count):
            chunks[z * plane_count + plane] = block


def gradient_kernel(
    z_count, subs, columns, queries, wo_plane, wq_plane, last_tokens, item_out, parts_out
):
    item_rows = item_out.shape[0]
    every = lax.dot_general(
        columns[...], queries[...], (((0,), (0,)), ((), ())), preferred_element_type=jnp.float32
    )
    grads = (every[:item_rows] * INV_TEMP).astype(jnp.bfloat16)
    item_out[...] = grads
    row = lax.broadcasted_iota(jnp.int32, (subs * z_count, item_rows), 0)
    column = lax.broadcasted_iota(jnp.int32, (subs * z_count, item_rows), 1)
    per_z = item_rows // z_count
    wanted = jnp.where((row // subs) * per_z + row % subs == column, 1.0, 0.0)
    cotangents = jnp.dot(
        wanted.astype(jnp.bfloat16), grads, preferred_element_type=jnp.float32
    ).astype(jnp.bfloat16)
    attn = jnp.dot(cotangents, wo_plane[...], preferred_element_type=jnp.float32)
    query = jnp.dot(last_tokens[...], wq_plane[...], preferred_element_type=jnp.float32)
    for z in range(z_count):
        parts_out[z, :subs] = attn[z * subs : (z + 1) * subs]
        parts_out[z, subs:] = query[z * subs : (z + 1) * subs]


def attention_kernel(
    lengths,
    parts,
    keys,
    values,
    key_up,
    value_up,
    reduced,
    query_delta_out,
    key_change_out,
    value_change_out,
    coef_out,
    up_out,
):
    subs = parts.shape[1] // 2
    width = parts.shape[2]
    token_count = keys.shape[0]
    seq_len = token_count // subs
    group = width // HEAD_DIM
    both = parts[0]
    for part in range(1, parts.shape[0]):
        both = both + parts[part]
    both = both.astype(jnp.bfloat16).astype(jnp.float32)

    def heads(first):
        return jnp.concatenate(
            [
                both[first + sub : first + sub + 1, head * HEAD_DIM : (head + 1) * HEAD_DIM]
                for sub in range(subs)
                for head in range(group)
            ],
            axis=0,
        )

    grad_heads = heads(0)
    q_heads = heads(subs)
    score_scale = 1.0 / math.sqrt(HEAD_DIM)
    raw = final_product(q_heads.astype(jnp.bfloat16), keys[...]) * score_scale
    row_sub = lax.broadcasted_iota(jnp.int32, raw.shape, 0) // group
    token = lax.broadcasted_iota(jnp.int32, raw.shape, 1)
    live = jnp.zeros(raw.shape, jnp.bool_)
    for sub in range(subs):
        first = sub * seq_len
        inside = (token >= first) & (token < first + lengths[sub, 0])
        live = live | (inside & (row_sub == sub))
    raw = jnp.where(live, raw, -jnp.inf)
    weights = jnp.exp(raw - jnp.max(raw, axis=1, keepdims=True))
    probs = weights / jnp.sum(weights, axis=1, keepdims=True)
    prob_half = probs.astype(jnp.bfloat16).astype(jnp.float32)
    prob_grad = final_product(grad_heads.astype(jnp.bfloat16), values[...])
    score_grad = (
        probs * (prob_grad - jnp.sum(probs * prob_grad, axis=1, keepdims=True)) * score_scale
    )
    score_grad = score_grad.astype(jnp.bfloat16)
    delta = jnp.dot(score_grad, keys[...], preferred_element_type=jnp.float32)
    for sub in range(subs):
        for head in range(group):
            row = sub * group + head
            query_delta_out[sub : sub + 1, head * HEAD_DIM : (head + 1) * HEAD_DIM] = delta[
                row : row + 1
            ]
    score_grad = score_grad.astype(jnp.float32)
    key_change = first_product(score_grad, q_heads).astype(jnp.bfloat16)
    value_change = first_product(prob_half, grad_heads).astype(jnp.bfloat16)
    key_change_out[...] = key_change
    value_change_out[...] = value_change
    key_coef = final_product(key_change, key_up[...])
    value_coef = final_product(value_change, value_up[...])
    coef = jnp.concatenate([key_coef, value_coef], axis=1).astype(jnp.bfloat16)
    for copy in range(coef_out.shape[0]):
        coef_out[copy] = coef
    rank = key_up.shape[0]
    up_out[:rank] = ADAPTER_SCALE * first_product(reduced[...], key_change)[:rank]
    up_out[rank:] = ADAPTER_SCALE * first_product(reduced[...], value_change)[rank:]


def share_kernel(coefs, tokens, ups, loss, deltas, wq_plane, out):
    total = coefs[0].astype(jnp.float32)
    for part in range(1, coefs.shape[0]):
        total = total + coefs[part].astype(jnp.float32)
    upper = total.astype(jnp.bfloat16)
    lower = (total - upper.astype(jnp.float32)).astype(jnp.bfloat16)
    down = ADAPTER_SCALE * (first_product(upper, tokens[...]) + first_product(lower, tokens[...]))
    last = final_product(deltas[...], wq_plane[...])
    z_count, rows, _ = out.shape
    subs = deltas.shape[0] // z_count
    feature_width = tokens.shape[1]
    up_end = feature_width + ups.shape[1]
    loss_end = up_end + loss.shape[1]
    for z in range(z_count):
        mine = slice(z * rows, (z + 1) * rows)
        out[z, :, :feature_width] = down[mine]
        out[z, :, feature_width:up_end] = ups[mine]
        out[z, :, up_end:loss_end] = loss[:rows]
        out[z, :subs, loss_end:] = last[z * subs : (z + 1) * subs]
        out[z, subs:, loss_end:] = jnp.zeros((rows - subs, feature_width), jnp.float32)


def local(
    query_emb,
    item_emb,
    pair_index,
    hard_index,
    hidden_in,
    lengths,
    w_query,
    key_weight_matrix,
    value_weight_matrix,
    w_out,
    key_down_matrix,
    key_up_matrix,
    value_down,
    value_up_matrix,
):
    z_count = lax.axis_size("z")
    plane_count = lax.axis_size(PLANE)
    dp_count = z_count * plane_count
    mp_count = lax.axis_size("mp")
    local_rows = query_emb.shape[0]
    batch_size = local_rows * dp_count
    feature_width = query_emb.shape[1]
    turn = [(a * mp_count + b, b * mp_count + a) for a in range(z_count) for b in range(mp_count)]

    sub_count = hidden_in.shape[0]
    seq_len = hidden_in.shape[2]
    token_count = sub_count * seq_len
    full_rows = lax.all_gather(hidden_in, "mp", axis=3, tiled=True)
    model_width = full_rows.shape[3]
    token_inputs = full_rows.reshape(token_count, model_width)
    seq_lengths = lengths[:, 0]
    last_rows = jnp.arange(sub_count, dtype=jnp.int32) * seq_len + seq_lengths - 1

    turned = lax.ppermute(query_emb, ("z", "mp"), turn)
    queries_all = spread(turned, PLANE + ("mp",))
    queries_all = (
        queries_all.reshape(plane_count, mp_count, local_rows, feature_width)
        .transpose(1, 0, 2, 3)
        .reshape(batch_size, feature_width)
    )
    items_all = (
        spread(item_emb, DP)
        .reshape(z_count, plane_count, local_rows, feature_width)
        .transpose(1, 0, 2, 3)
        .reshape(batch_size, feature_width)
    )
    partial_scores = final_product(query_emb, items_all)
    score_parts = spread(partial_scores, "mp")

    rows_here, query_width = w_query.shape
    both = jnp.stack([w_query, w_out.T])
    both, partial_scores = lax.optimization_barrier((both, partial_scores))
    other = lax.ppermute(both, "h", [(0, 1), (1, 0)])
    lower = lax.axis_index("h") == 0
    both = jnp.stack([jnp.where(lower, both, other), jnp.where(lower, other, both)])
    both = spread(both, "x")
    plane_rows = plane_count * rows_here
    wq_plane = both[:, :, 0].reshape(plane_rows, query_width)
    wo_plane = both[:, :, 1].reshape(plane_rows, query_width)

    last_tokens = jnp.concatenate(
        [
            lax.dynamic_slice_in_dim(token_inputs, last_rows[sub], 1, 0)
            for sub in range(sub_count)
        ],
        axis=0,
    )
    last_slices = swap(
        last_tokens.reshape(sub_count, z_count, feature_width).transpose(1, 0, 2), "z"
    ).reshape(z_count * sub_count, feature_width)

    adapter_rank = key_down_matrix.shape[1]
    down_both = jnp.concatenate([key_down_matrix, value_down], axis=1)
    reduced_pair = jnp.dot(token_inputs, down_both, preferred_element_type=jnp.float32).astype(
        jnp.bfloat16
    )
    reduced_key = reduced_pair[:, :adapter_rank]
    reduced_value = reduced_pair[:, adapter_rank:]
    key_rows = (
        jnp.dot(token_inputs, key_weight_matrix, preferred_element_type=jnp.float32)
        + ADAPTER_SCALE * jnp.dot(reduced_key, key_up_matrix, preferred_element_type=jnp.float32)
    ).astype(jnp.bfloat16)
    value_rows = (
        jnp.dot(token_inputs, value_weight_matrix, preferred_element_type=jnp.float32)
        + ADAPTER_SCALE
        * jnp.dot(reduced_value, value_up_matrix, preferred_element_type=jnp.float32)
    ).astype(jnp.bfloat16)

    bf16, f32 = jnp.bfloat16, jnp.float32
    chunks, residual, loss_part = call(
        functools.partial(residual_kernel, z_count, plane_count),
        (
            jax.ShapeDtypeStruct((dp_count, local_rows, LANES), bf16),
            jax.ShapeDtypeStruct((local_rows, batch_size), bf16),
            jax.ShapeDtypeStruct((local_rows, LANES), f32),
        ),
        2**24,
    )(score_parts, hard_index, pair_index[:, None])
    column_rows = swap(chunks, DP).reshape(batch_size, LANES)
    column_rows, key_rows, value_rows = lax.optimization_barrier(
        (column_rows, key_rows, value_rows)
    )
    column_grads, parts = call(
        functools.partial(gradient_kernel, z_count, sub_count),
        (
            jax.ShapeDtypeStruct((z_count * local_rows, feature_width), bf16),
            jax.ShapeDtypeStruct((z_count, 2 * sub_count, query_width), f32),
        ),
        2**26,
    )(column_rows, queries_all, wo_plane, wq_plane, last_slices)
    parts = swap(parts, "z")
    own_grads = lax.dynamic_index_in_dim(
        column_grads.reshape(z_count, local_rows, feature_width),
        lax.axis_index("mp"),
        0,
        keepdims=False,
    )
    item_grad = lax.ppermute(own_grads, ("z", "mp"), turn)
    query_grad = (
        jnp.dot(residual, items_all, preferred_element_type=jnp.float32) * INV_TEMP
    ).astype(jnp.bfloat16)

    query_delta, key_change, value_change, coef_copies, up_part = call(
        attention_kernel,
        (
            jax.ShapeDtypeStruct((sub_count, query_width), f32),
            jax.ShapeDtypeStruct(key_rows.shape, bf16),
            jax.ShapeDtypeStruct(value_rows.shape, bf16),
            jax.ShapeDtypeStruct((mp_count, token_count, 2 * adapter_rank), bf16),
            jax.ShapeDtypeStruct((2 * adapter_rank, key_rows.shape[1]), f32),
        ),
        2**24,
    )(lengths, parts, key_rows, value_rows, key_up_matrix, value_up_matrix, reduced_pair)
    coefficients = swap(coef_copies, "mp")
    query_deltas = spread(query_delta.astype(bf16), "z").reshape(-1, query_width)

    own_rows = hidden_in.reshape(token_count, feature_width)
    up_width = up_part.shape[1]
    share_rows = 2 * adapter_rank // z_count
    loss_end = feature_width + up_width + LANES
    shares = call(
        share_kernel,
        jax.ShapeDtypeStruct((z_count, share_rows, loss_end + feature_width), f32),
        2**26,
    )(coefficients, own_rows, up_part, loss_part, query_deltas, wq_plane)
    shares = swap(shares, "z")
    last_part = (
        shares[:, :sub_count, loss_end:].transpose(1, 0, 2).reshape(sub_count, model_width)
    )

    key_coefficient = coef_copies[0, :, :adapter_rank]
    value_coefficient = coef_copies[0, :, adapter_rank:]
    input_portion = final_product(key_change, key_weight_matrix) + final_product(
        value_change, value_weight_matrix
    )
    input_portion = input_portion + ADAPTER_SCALE * (
        final_product(key_coefficient, key_down_matrix)
        + final_product(value_coefficient, value_down)
    )
    row_ids = jnp.arange(token_count, dtype=jnp.int32)[:, None]
    for sub in range(sub_count):
        input_portion = input_portion + jnp.where(
            row_ids == last_rows[sub], last_part[sub][None, :], 0.0
        )
    input_sum = lax.psum_scatter(
        input_portion.astype(jnp.bfloat16), "mp", scatter_dimension=1, tiled=True
    ).astype(jnp.float32)
    for sub in range(sub_count):
        input_sum = input_sum + jnp.where(
            row_ids == last_rows[sub], item_grad[sub][None, :].astype(jnp.float32), 0.0
        )
    input_grad = input_sum.astype(jnp.bfloat16).reshape(hidden_in.shape)

    share_sum = jnp.sum(shares[:, :, :loss_end], axis=0)
    share_sum = jnp.sum(spread(share_sum, PLANE), axis=0)
    mean_loss = share_sum[0, feature_width + up_width] / batch_size
    summed = spread(share_sum[:, : feature_width + up_width], "z")
    summed = summed.reshape(2 * adapter_rank, feature_width + up_width)
    up_grad = summed[:, feature_width:]
    down_slice = summed[:, :feature_width].astype(jnp.bfloat16)
    down_grad = (
        spread(down_slice, "mp").transpose(1, 0, 2).reshape(-1, model_width).astype(jnp.float32).T
    )
    return (
        mean_loss,
        query_grad,
        item_grad,
        input_grad,
        down_grad[:, :adapter_rank],
        down_grad[:, adapter_rank:],
        up_grad[:adapter_rank],
        up_grad[adapter_rank:],
    )


def solution(mesh):
    fine = Mesh(
        mesh.devices.reshape(8, 4, 2, mesh.devices.shape[1]), ("z", "x", "h", "mp")
    )
    in_specs = (
        P(DP, "mp"),
        P(DP, "mp"),
        P(DP),
        P(DP, None),
        P(None, DP, None, "mp"),
        P(None, DP),
        P(DP, "mp"),
        P(None, "mp"),
        P(None, "mp"),
        P("mp", DP),
        P(),
        P(None, "mp"),
        P(),
        P(None, "mp"),
    )
    out_specs = (
        P(),
        P(DP, "mp"),
        P(DP, "mp"),
        P(None, DP, None, "mp"),
        P(),
        P(),
        P(None, "mp"),
        P(None, "mp"),
    )
    return jax.shard_map(local, mesh=fine, in_specs=in_specs, out_specs=out_specs, check_vma=False)
```

```python
import functools
import math

import jax
import jax.numpy as jnp
from jax import lax
from jax.experimental import pallas as pl
from jax.experimental.pallas import tpu as pltpu
from jax.sharding import Mesh
from jax.sharding import PartitionSpec as P

HEADS = 32
KV_HEADS = 8
HEAD_DIM = 128
LANES = 128

INV_TEMP = 50.0
HARD_NEGATIVE_ADD = 4.0
ADAPTER_SCALE = 2.0

PLANE = ("x", "h")
DP = ("z", "x", "h")


def final_product(left_side, right_side):
    return lax.dot_general(
        left_side, right_side, (((1,), (1,)), ((), ())), preferred_element_type=jnp.float32
    )


def first_product(left_side, right_side):
    return lax.dot_general(
        left_side, right_side, (((0,), (0,)), ((), ())), preferred_element_type=jnp.float32
    )


def spread(block, axes):
    count = lax.axis_size(axes)
    copies = jnp.broadcast_to(block[None], (count,) + block.shape)
    return lax.all_to_all(copies, axes, split_axis=0, concat_axis=0, tiled=True)


def swap(blocks, axes):
    return lax.all_to_all(blocks, axes, split_axis=0, concat_axis=0, tiled=True)


def call(kernel, out_shape, flops, **layout):
    return pl.pallas_call(
        kernel,
        out_shape=out_shape,
        compiler_params=pltpu.CompilerParams(vmem_limit_bytes=32 * 1024 * 1024),
        cost_estimate=pl.CostEstimate(flops=flops, bytes_accessed=2**20, transcendentals=4096),
        **layout,
    )


def residual_kernel(
    z_count, plane_count, parts, hard, pair, tokens, chunks, residual_out, loss_out
):
    rows = parts.shape[1]
    batch_size = parts.shape[2]
    pair_scores = parts[0]
    for part in range(1, parts.shape[0]):
        pair_scores = pair_scores + parts[part]
    column = lax.broadcasted_iota(jnp.int32, (rows, batch_size), 1)
    inner = column % rows
    outer = column // rows
    item = ((outer % z_count) * plane_count + outer // z_count) * rows + inner
    count = jnp.zeros((rows, batch_size), jnp.float32)
    for choice in range(hard.shape[1]):
        count = count + jnp.where(hard[:, choice : choice + 1] == item, 1.0, 0.0)
    logits = pair_scores * INV_TEMP + HARD_NEGATIVE_ADD * count
    top = jnp.max(logits, axis=1, keepdims=True)
    log_total = top + jnp.log(jnp.sum(jnp.exp(logits - top), axis=1, keepdims=True))
    target = jnp.where(pair[...] == item, 1.0, 0.0)
    picked = jnp.sum(target * logits, axis=1, keepdims=True)
    loss = jnp.sum(log_total - picked, axis=0, keepdims=True)
    loss_out[...] = jnp.broadcast_to(loss, loss_out.shape)
    residual = jnp.exp(logits - log_total) - target
    residual_out[...] = residual.astype(jnp.bfloat16)
    width = z_count * rows
    pad = jnp.zeros((rows, LANES - width), jnp.float32)
    for plane in range(plane_count):
        block = jnp.concatenate([residual[:, plane * width : (plane + 1) * width], pad], axis=1)
        block = block.astype(jnp.bfloat16)
        for z in range(z_count):
            chunks[z * plane_count + plane, :, :LANES] = block
            chunks[z * plane_count + plane, :, LANES:] = tokens[z]


def gradient_kernel(z_count, subs, place, received, queries, loss, *rest):
    pieces, (item_out, parts_out) = rest[:-2], rest[-2:]
    item_rows = item_out.shape[0]
    count = len(pieces)
    width = queries.shape[1] // count
    every = lax.dot_general(
        received[:, :LANES],
        queries[...],
        (((0,), (0,)), ((), ())),
        preferred_element_type=jnp.float32,
    )
    grads = (every[:item_rows] * INV_TEMP).astype(jnp.bfloat16)
    item_out[...] = grads
    picks = subs * z_count
    row = lax.broadcasted_iota(jnp.int32, (picks, item_rows), 0)
    column = lax.broadcasted_iota(jnp.int32, (picks, item_rows), 1)
    per_z = item_rows // z_count
    wanted = jnp.where((row // subs) * per_z + row % subs == column, 1.0, 0.0)
    cotangents = jnp.dot(
        wanted.astype(jnp.bfloat16), grads, preferred_element_type=jnp.float32
    )
    senders = received.shape[0] // per_z
    planes = senders // z_count
    row = lax.broadcasted_iota(jnp.int32, (picks, received.shape[0]), 0)
    column = lax.broadcasted_iota(jnp.int32, (picks, received.shape[0]), 1)
    first = ((row // subs) * planes + place[1:2, 0:1]) * per_z + row % subs
    attn = query = None
    for turn, piece in enumerate(pieces):
        block = lax.rem(place[0:1, 0:1] + (count - turn), count)
        cot = jnp.zeros((picks, width), jnp.float32)
        for choice in range(count):
            cot = cot + jnp.where(
                block == choice, cotangents[:, choice * width : (choice + 1) * width], 0.0
            )
        chosen = jnp.where(first + block * subs == column, 1.0, 0.0).astype(jnp.bfloat16)
        token = jnp.dot(chosen, received[:, LANES:], preferred_element_type=jnp.float32)
        wq_rows = jnp.concatenate([piece[half, 0] for half in range(piece.shape[0])], axis=0)
        wo_rows = jnp.concatenate([piece[half, 1] for half in range(piece.shape[0])], axis=0)
        attn_term = jnp.dot(cot.astype(jnp.bfloat16), wo_rows, preferred_element_type=jnp.float32)
        query_term = jnp.dot(
            token.astype(jnp.bfloat16), wq_rows, preferred_element_type=jnp.float32
        )
        attn = attn_term if attn is None else attn + attn_term
        query = query_term if query is None else query + query_term
    end = attn.shape[1]
    for z in range(z_count):
        parts_out[z, :subs, :end] = attn[z * subs : (z + 1) * subs]
        parts_out[z, subs:, :end] = query[z * subs : (z + 1) * subs]
        parts_out[z, :, end:] = loss[: 2 * subs]


def attention_kernel(
    place,
    lengths,
    parts,
    keys,
    values,
    key_up,
    value_up,
    reduced,
    tokens,
    query_delta_out,
    key_change_out,
    value_change_out,
    coef_out,
    loss_out,
    shares_out,
):
    subs = parts.shape[1] // 2
    token_count = keys.shape[0]
    seq_len = token_count // subs
    group = parts.shape[2] // HEAD_DIM - 1
    total = parts[0]
    for part in range(1, parts.shape[0]):
        total = total + parts[part]
    loss_out[...] = total[:, group * HEAD_DIM :]
    both = total.astype(jnp.bfloat16).astype(jnp.float32)

    def heads(first):
        return jnp.concatenate(
            [
                both[first + sub : first + sub + 1, head * HEAD_DIM : (head + 1) * HEAD_DIM]
                for sub in range(subs)
                for head in range(group)
            ],
            axis=0,
        )

    grad_heads = heads(0)
    q_heads = heads(subs)
    score_scale = 1.0 / math.sqrt(HEAD_DIM)
    raw = final_product(q_heads.astype(jnp.bfloat16), keys[...]) * score_scale
    row_sub = lax.broadcasted_iota(jnp.int32, raw.shape, 0) // group
    token = lax.broadcasted_iota(jnp.int32, raw.shape, 1)
    live = jnp.zeros(raw.shape, jnp.bool_)
    for sub in range(subs):
        first = sub * seq_len
        inside = (token >= first) & (token < first + lengths[sub, 0])
        live = live | (inside & (row_sub == sub))
    raw = jnp.where(live, raw, -jnp.inf)
    weights = jnp.exp(raw - jnp.max(raw, axis=1, keepdims=True))
    probs = weights / jnp.sum(weights, axis=1, keepdims=True)
    prob_half = probs.astype(jnp.bfloat16).astype(jnp.float32)
    prob_grad = final_product(grad_heads.astype(jnp.bfloat16), values[...])
    score_grad = (
        probs * (prob_grad - jnp.sum(probs * prob_grad, axis=1, keepdims=True)) * score_scale
    )
    score_grad = score_grad.astype(jnp.bfloat16)
    delta = jnp.dot(score_grad, keys[...], preferred_element_type=jnp.float32)
    for sub in range(subs):
        for head in range(group):
            row = sub * group + head
            query_delta_out[sub : sub + 1, head * HEAD_DIM : (head + 1) * HEAD_DIM] = delta[
                row : row + 1
            ]
    score_grad = score_grad.astype(jnp.float32)
    key_change = first_product(score_grad, q_heads).astype(jnp.bfloat16)
    value_change = first_product(prob_half, grad_heads).astype(jnp.bfloat16)
    key_change_out[...] = key_change
    value_change_out[...] = value_change
    key_coef = final_product(key_change, key_up[...])
    value_coef = final_product(value_change, value_up[...])
    coef = jnp.concatenate([key_coef, value_coef], axis=1).astype(jnp.bfloat16)
    coef_out[...] = coef
    rank = key_up.shape[0]
    ups = ADAPTER_SCALE * jnp.concatenate(
        [
            first_product(reduced[...], key_change)[:rank],
            first_product(reduced[...], value_change)[rank:],
        ],
        axis=0,
    )
    downs = ADAPTER_SCALE * first_product(coef, tokens[...])
    z_count, mp_count, rows, chunk_width = shares_out.shape
    width = downs.shape[1] // mp_count
    for other in range(mp_count):
        kept = jnp.where(place[2:3, 0:1] == other, ups, 0.0)
        for z in range(z_count):
            mine = slice(z * rows, (z + 1) * rows)
            shares_out[z, other, :, :width] = downs[
                mine, other * width : (other + 1) * width
            ].astype(jnp.bfloat16)
            shares_out[z, other, :, width:] = kept[mine].astype(jnp.bfloat16)


def portion_kernel(
    seq_len, lengths, key_change, value_change, coef, last, key_weight, value_weight, down, out
):
    total = final_product(key_change[...], key_weight[...]) + final_product(
        value_change[...], value_weight[...]
    )
    total = total + ADAPTER_SCALE * jnp.dot(
        coef[...], down[...], preferred_element_type=jnp.float32
    )
    row = lax.broadcasted_iota(jnp.int32, total.shape, 0)
    for sub in range(last.shape[0]):
        chosen = row == sub * seq_len + lengths[sub, 0] - 1
        total = total + jnp.where(chosen, last[sub : sub + 1], 0.0)
    out[...] = total.astype(jnp.bfloat16)


def local(
    query_emb,
    item_emb,
    pair_index,
    hard_index,
    hidden_in,
    lengths,
    w_query,
    key_weight_matrix,
    value_weight_matrix,
    w_out,
    key_down_matrix,
    key_up_matrix,
    value_down,
    value_up_matrix,
):
    bf16, f32 = jnp.bfloat16, jnp.float32
    x_count = lax.axis_size("x")
    z_count = lax.axis_size("z")
    plane_count = lax.axis_size(PLANE)
    dp_count = z_count * plane_count
    mp_count = lax.axis_size("mp")
    local_rows = query_emb.shape[0]
    batch_size = local_rows * dp_count
    feature_width = query_emb.shape[1]
    place = jnp.broadcast_to(
        jnp.stack([lax.axis_index("x"), lax.axis_index(PLANE), lax.axis_index("mp")])[:, None],
        (3, LANES),
    ).astype(jnp.int32)

    sub_count = hidden_in.shape[0]
    seq_len = hidden_in.shape[2]
    token_count = sub_count * seq_len
    full_rows = lax.all_gather(hidden_in, "mp", axis=3, tiled=True)
    model_width = full_rows.shape[3]
    token_inputs = full_rows.reshape(token_count, model_width)
    seq_lengths = lengths[:, 0]
    last_rows = jnp.arange(sub_count, dtype=jnp.int32) * seq_len + seq_lengths - 1

    query_slices = spread(query_emb, "mp")
    chunks = jnp.concatenate(
        [jnp.broadcast_to(item_emb[None], query_slices.shape), query_slices], axis=1
    )
    chunks = jnp.broadcast_to(chunks[:, None], (z_count, plane_count) + chunks.shape[1:])
    received = swap(chunks.reshape((dp_count,) + chunks.shape[2:]), DP)
    queries_all = received[:, local_rows:].reshape(batch_size, feature_width)
    items_all = (
        received[:, :local_rows]
        .reshape(z_count, plane_count, local_rows, feature_width)
        .transpose(1, 0, 2, 3)
        .reshape(batch_size, feature_width)
    )
    partial_scores = final_product(query_emb, items_all)
    score_parts = spread(partial_scores, "mp")

    rows_here, query_width = w_query.shape
    both = jnp.stack([w_query, w_out.T])
    other = lax.ppermute(both, "h", [(0, 1), (1, 0)])
    lower = lax.axis_index("h") == 0
    both = jnp.stack([jnp.where(lower, both, other), jnp.where(lower, other, both)])
    pieces = [both] + [
        lax.ppermute(both, "x", [(a, (a + turn) % x_count) for a in range(x_count)])
        for turn in range(1, x_count)
    ]
    wq_plane = jnp.stack([piece[:, 0] for piece in pieces])
    wq_plane, partial_scores = lax.optimization_barrier((wq_plane, partial_scores))
    wq_full = lax.all_gather(
        wq_plane.reshape(plane_count * rows_here, query_width), "z", axis=0, tiled=True
    )

    last_tokens = jnp.concatenate(
        [
            lax.dynamic_slice_in_dim(token_inputs, last_rows[sub], 1, 0)
            for sub in range(sub_count)
        ],
        axis=0,
    )
    last_slices = (
        last_tokens.reshape(sub_count, z_count, x_count, feature_width // x_count)
        .transpose(1, 2, 0, 3)
        .reshape(z_count, x_count * sub_count, feature_width // x_count)
    )

    adapter_rank = key_down_matrix.shape[1]
    down_both = jnp.concatenate([key_down_matrix, value_down], axis=1)
    reduced_pair = jnp.dot(token_inputs, down_both, preferred_element_type=f32).astype(bf16)
    reduced_key = reduced_pair[:, :adapter_rank]
    reduced_value = reduced_pair[:, adapter_rank:]
    key_rows = (
        jnp.dot(token_inputs, key_weight_matrix, preferred_element_type=f32)
        + ADAPTER_SCALE * jnp.dot(reduced_key, key_up_matrix, preferred_element_type=f32)
    ).astype(bf16)
    value_rows = (
        jnp.dot(token_inputs, value_weight_matrix, preferred_element_type=f32)
        + ADAPTER_SCALE * jnp.dot(reduced_value, value_up_matrix, preferred_element_type=f32)
    ).astype(bf16)

    chunks, residual, loss_part = call(
        functools.partial(residual_kernel, z_count, plane_count),
        (
            jax.ShapeDtypeStruct((dp_count, local_rows, 2 * LANES), bf16),
            jax.ShapeDtypeStruct((local_rows, batch_size), bf16),
            jax.ShapeDtypeStruct((local_rows, LANES), f32),
        ),
        2**24,
    )(score_parts, hard_index, pair_index[:, None], last_slices)
    column_rows = swap(chunks, DP).reshape(batch_size, 2 * LANES)
    column_rows, key_rows, value_rows = lax.optimization_barrier(
        (column_rows, key_rows, value_rows)
    )
    column_grads, parts = call(
        functools.partial(gradient_kernel, z_count, sub_count),
        (
            jax.ShapeDtypeStruct((z_count * local_rows, feature_width), bf16),
            jax.ShapeDtypeStruct((z_count, 2 * sub_count, query_width + LANES), f32),
        ),
        2**26,
    )(place, column_rows, queries_all, loss_part, *pieces)
    parts = swap(parts, "z")
    own_grads = lax.dynamic_index_in_dim(
        column_grads.reshape(z_count, local_rows, feature_width),
        lax.axis_index("mp"),
        0,
        keepdims=False,
    )
    item_grad = lax.ppermute(
        own_grads,
        ("z", "mp"),
        [(a * mp_count + b, b * mp_count + a) for a in range(z_count) for b in range(mp_count)],
    )
    query_grad = (jnp.dot(residual, items_all, preferred_element_type=f32) * INV_TEMP).astype(bf16)

    share_rows = 2 * adapter_rank // z_count
    up_width = key_rows.shape[1]
    query_delta, key_change, value_change, coef, loss_part, shares = call(
        attention_kernel,
        (
            jax.ShapeDtypeStruct((sub_count, query_width), f32),
            jax.ShapeDtypeStruct(key_rows.shape, bf16),
            jax.ShapeDtypeStruct(value_rows.shape, bf16),
            jax.ShapeDtypeStruct((token_count, 2 * adapter_rank), bf16),
            jax.ShapeDtypeStruct((2 * sub_count, LANES), f32),
            jax.ShapeDtypeStruct((z_count, mp_count, share_rows, feature_width + up_width), bf16),
        ),
        2**26,
    )(
        place,
        lengths,
        parts,
        key_rows,
        value_rows,
        key_up_matrix,
        value_up_matrix,
        reduced_pair,
        token_inputs,
    )
    shares = swap(shares.reshape((-1,) + shares.shape[2:]), ("z", "mp"))

    last_part = final_product(query_delta.astype(bf16), wq_full)
    last_part = last_part.reshape(sub_count, z_count, x_count, -1)
    last_part = jnp.roll(last_part[:, :, (0,) + tuple(range(x_count - 1, 0, -1))], lax.axis_index("x"), axis=2)
    last_part = last_part.reshape(sub_count, model_width)
    block = model_width // mp_count
    whole = lambda array: pl.BlockSpec(array.shape, lambda step: (0, 0))
    along = lambda array: pl.BlockSpec((array.shape[0], block), lambda step: (0, step))
    down = lambda array: pl.BlockSpec((block, array.shape[1]), lambda step: (step, 0))
    down_rows = down_both.T
    portion = call(
        functools.partial(portion_kernel, seq_len),
        jax.ShapeDtypeStruct((token_count, model_width), bf16),
        2**29,
        grid=(mp_count,),
        in_specs=[
            whole(lengths),
            whole(key_change),
            whole(value_change),
            whole(coef),
            along(last_part),
            down(key_weight_matrix),
            down(value_weight_matrix),
            along(down_rows),
        ],
        out_specs=pl.BlockSpec((token_count, block), lambda step: (0, step)),
    )(
        lengths,
        key_change,
        value_change,
        coef,
        last_part,
        key_weight_matrix,
        value_weight_matrix,
        down_rows,
    )
    input_sum = lax.psum_scatter(portion, "mp", scatter_dimension=1, tiled=True).astype(f32)
    row_ids = jnp.arange(token_count, dtype=jnp.int32)[:, None]
    for sub in range(sub_count):
        input_sum = input_sum + jnp.where(
            row_ids == last_rows[sub], item_grad[sub][None, :].astype(f32), 0.0
        )
    input_grad = input_sum.astype(bf16).reshape(hidden_in.shape)

    share_sum = jnp.sum(shares.astype(f32), axis=0)
    share_sum = jnp.concatenate([share_sum, loss_part[:share_rows]], axis=1)
    share_sum = jnp.sum(spread(share_sum, PLANE), axis=0)
    mean_loss = share_sum[0, feature_width + up_width] / batch_size
    summed = spread(share_sum[:, : feature_width + up_width].astype(bf16), ("z", "mp"))
    summed, input_grad = lax.optimization_barrier((summed, input_grad))
    summed = summed.reshape(z_count, mp_count, share_rows, feature_width + up_width)
    up_grad = lax.dynamic_index_in_dim(
        summed[:, :, :, feature_width:], lax.axis_index("mp"), 1, keepdims=False
    )
    up_grad = up_grad.reshape(2 * adapter_rank, up_width).astype(f32)
    down_grad = (
        summed[:, :, :, :feature_width]
        .transpose(0, 2, 1, 3)
        .reshape(2 * adapter_rank, model_width)
        .astype(f32)
        .T
    )
    return (
        mean_loss,
        query_grad,
        item_grad,
        input_grad,
        down_grad[:, :adapter_rank],
        down_grad[:, adapter_rank:],
        up_grad[:adapter_rank],
        up_grad[adapter_rank:],
    )


def solution(mesh):
    fine = Mesh(
        mesh.devices.reshape(8, 4, 2, mesh.devices.shape[1]), ("z", "x", "h", "mp")
    )
    in_specs = (
        P(DP, "mp"),
        P(DP, "mp"),
        P(DP),
        P(DP, None),
        P(None, DP, None, "mp"),
        P(None, DP),
        P(DP, "mp"),
        P(None, "mp"),
        P(None, "mp"),
        P("mp", DP),
        P(),
        P(None, "mp"),
        P(),
        P(None, "mp"),
    )
    out_specs = (
        P(),
        P(DP, "mp"),
        P(DP, "mp"),
        P(None, DP, None, "mp"),
        P(),
        P(),
        P(None, "mp"),
        P(None, "mp"),
    )
    return jax.shard_map(local, mesh=fine, in_specs=in_specs, out_specs=out_specs, check_vma=False)
```

```python
import functools
import math

import jax
import jax.numpy as jnp
from jax import lax
from jax.experimental import pallas as pl
from jax.experimental.pallas import tpu as pltpu
from jax.sharding import Mesh
from jax.sharding import PartitionSpec as P

HEADS = 32
KV_HEADS = 8
HEAD_DIM = 128
LANES = 128

INV_TEMP = 50.0
HARD_NEGATIVE_ADD = 4.0
ADAPTER_SCALE = 2.0

PLANE = ("x", "h")
DP = ("z", "x", "h")


def final_product(left_side, right_side):
    return lax.dot_general(
        left_side, right_side, (((1,), (1,)), ((), ())), preferred_element_type=jnp.float32
    )


def first_product(left_side, right_side):
    return lax.dot_general(
        left_side, right_side, (((0,), (0,)), ((), ())), preferred_element_type=jnp.float32
    )


def spread(block, axes):
    count = lax.axis_size(axes)
    copies = jnp.broadcast_to(block[None], (count,) + block.shape)
    return lax.all_to_all(copies, axes, split_axis=0, concat_axis=0, tiled=True)


def swap(blocks, axes):
    return lax.all_to_all(blocks, axes, split_axis=0, concat_axis=0, tiled=True)


def call(kernel, out_shape, flops, **layout):
    return pl.pallas_call(
        kernel,
        out_shape=out_shape,
        compiler_params=pltpu.CompilerParams(vmem_limit_bytes=56 * 1024 * 1024),
        cost_estimate=pl.CostEstimate(flops=flops, bytes_accessed=2**20, transcendentals=4096),
        **layout,
    )


def residual_kernel(
    z_count, plane_count, parts, hard, pair, tokens, chunks, residual_out, loss_out
):
    rows = parts.shape[1]
    batch_size = parts.shape[2]
    pair_scores = parts[0]
    for part in range(1, parts.shape[0]):
        pair_scores = pair_scores + parts[part]
    column = lax.broadcasted_iota(jnp.int32, (rows, batch_size), 1)
    inner = column % rows
    outer = column // rows
    item = ((outer % z_count) * plane_count + outer // z_count) * rows + inner
    count = jnp.zeros((rows, batch_size), jnp.float32)
    for choice in range(hard.shape[1]):
        count = count + jnp.where(hard[:, choice : choice + 1] == item, 1.0, 0.0)
    logits = pair_scores * INV_TEMP + HARD_NEGATIVE_ADD * count
    top = jnp.max(logits, axis=1, keepdims=True)
    log_total = top + jnp.log(jnp.sum(jnp.exp(logits - top), axis=1, keepdims=True))
    target = jnp.where(pair[...] == item, 1.0, 0.0)
    picked = jnp.sum(target * logits, axis=1, keepdims=True)
    loss = jnp.sum(log_total - picked, axis=0, keepdims=True)
    loss_out[...] = jnp.broadcast_to(loss, loss_out.shape)
    residual = jnp.exp(logits - log_total) - target
    residual_out[...] = residual.astype(jnp.bfloat16)
    width = z_count * rows
    pad = jnp.zeros((rows, LANES - width), jnp.float32)
    for plane in range(plane_count):
        block = jnp.concatenate([residual[:, plane * width : (plane + 1) * width], pad], axis=1)
        block = block.astype(jnp.bfloat16)
        for z in range(z_count):
            chunks[z * plane_count + plane, :, :LANES] = block
            chunks[z * plane_count + plane, :, LANES:] = tokens[z]


def gradient_kernel(z_count, subs, received, queries, loss, *rest):
    pieces, (item_out, parts_out) = rest[:-2], rest[-2:]
    item_rows = item_out.shape[0]
    count = len(pieces)
    width = queries.shape[1] // count
    every = lax.dot_general(
        received[:, :LANES],
        queries[...],
        (((0,), (0,)), ((), ())),
        preferred_element_type=jnp.float32,
    )
    grads = (every[:item_rows] * INV_TEMP).astype(jnp.bfloat16)
    item_out[...] = grads
    picks = subs * z_count
    row = lax.broadcasted_iota(jnp.int32, (picks, item_rows), 0)
    column = lax.broadcasted_iota(jnp.int32, (picks, item_rows), 1)
    per_z = item_rows // z_count
    wanted = jnp.where((row // subs) * per_z + row % subs == column, 1.0, 0.0)
    cotangents = jnp.dot(
        wanted.astype(jnp.bfloat16), grads, preferred_element_type=jnp.float32
    )
    senders = received.shape[0] // per_z
    planes = senders // z_count
    row = lax.broadcasted_iota(jnp.int32, (picks, received.shape[0]), 0)
    column = lax.broadcasted_iota(jnp.int32, (picks, received.shape[0]), 1)
    plane = lax.axis_index(PLANE)
    first = ((row // subs) * planes + plane) * per_z + row % subs
    attn = query = None
    for turn, piece in enumerate(pieces):
        block = lax.rem(lax.axis_index("x") + (count - turn), count)
        cot = jnp.zeros((picks, width), jnp.float32)
        for choice in range(count):
            cot = cot + jnp.where(
                block == choice, cotangents[:, choice * width : (choice + 1) * width], 0.0
            )
        chosen = jnp.where(first + block * subs == column, 1.0, 0.0).astype(jnp.bfloat16)
        token = jnp.dot(chosen, received[:, LANES:], preferred_element_type=jnp.float32)
        wq_rows = jnp.concatenate([piece[half, 0] for half in range(piece.shape[0])], axis=0)
        wo_rows = jnp.concatenate([piece[half, 1] for half in range(piece.shape[0])], axis=0)
        attn_term = jnp.dot(cot.astype(jnp.bfloat16), wo_rows, preferred_element_type=jnp.float32)
        query_term = jnp.dot(
            token.astype(jnp.bfloat16), wq_rows, preferred_element_type=jnp.float32
        )
        attn = attn_term if attn is None else attn + attn_term
        query = query_term if query is None else query + query_term
    end = attn.shape[1]
    for z in range(z_count):
        parts_out[z, :subs, :end] = attn[z * subs : (z + 1) * subs]
        parts_out[z, subs:, :end] = query[z * subs : (z + 1) * subs]
        parts_out[z, :, end:] = loss[: 2 * subs]


def attention_kernel(
    lengths,
    parts,
    keys,
    values,
    key_up,
    value_up,
    reduced,
    tokens,
    key_change_out,
    value_change_out,
    coef_out,
    loss_out,
    shares_out,
):
    subs = parts.shape[1] // 2
    token_count = keys.shape[0]
    seq_len = token_count // subs
    group = parts.shape[2] // HEAD_DIM - 1
    total = parts[0]
    for part in range(1, parts.shape[0]):
        total = total + parts[part]
    loss_out[...] = total[:, group * HEAD_DIM :]
    both = total.astype(jnp.bfloat16).astype(jnp.float32)

    def heads(first):
        return jnp.concatenate(
            [
                both[first + sub : first + sub + 1, head * HEAD_DIM : (head + 1) * HEAD_DIM]
                for sub in range(subs)
                for head in range(group)
            ],
            axis=0,
        )

    grad_heads = heads(0)
    q_heads = heads(subs)
    score_scale = 1.0 / math.sqrt(HEAD_DIM)
    raw = final_product(q_heads.astype(jnp.bfloat16), keys[...]) * score_scale
    row_sub = lax.broadcasted_iota(jnp.int32, raw.shape, 0) // group
    token = lax.broadcasted_iota(jnp.int32, raw.shape, 1)
    live = jnp.zeros(raw.shape, jnp.bool_)
    for sub in range(subs):
        first = sub * seq_len
        inside = (token >= first) & (token < first + lengths[sub, 0])
        live = live | (inside & (row_sub == sub))
    raw = jnp.where(live, raw, -jnp.inf)
    weights = jnp.exp(raw - jnp.max(raw, axis=1, keepdims=True))
    probs = weights / jnp.sum(weights, axis=1, keepdims=True)
    prob_half = probs.astype(jnp.bfloat16).astype(jnp.float32)
    prob_grad = final_product(grad_heads.astype(jnp.bfloat16), values[...])
    score_grad = (
        probs * (prob_grad - jnp.sum(probs * prob_grad, axis=1, keepdims=True)) * score_scale
    )
    score_grad = score_grad.astype(jnp.bfloat16)
    delta = jnp.dot(score_grad, keys[...], preferred_element_type=jnp.float32)
    score_grad = score_grad.astype(jnp.float32)
    key_change = first_product(score_grad, q_heads).astype(jnp.bfloat16)
    value_change = first_product(prob_half, grad_heads).astype(jnp.bfloat16)
    key_change_out[...] = key_change
    value_change_out[...] = value_change
    key_coef = final_product(key_change, key_up[...])
    value_coef = final_product(value_change, value_up[...])
    coef = jnp.concatenate([key_coef, value_coef], axis=1).astype(jnp.bfloat16)
    coef_out[...] = coef
    rank = key_up.shape[0]
    ups = ADAPTER_SCALE * jnp.concatenate(
        [
            first_product(reduced[...], key_change)[:rank],
            first_product(reduced[...], value_change)[rank:],
        ],
        axis=0,
    )
    downs = ADAPTER_SCALE * first_product(coef, tokens[...])
    z_count, mp_count, rows, chunk_width = shares_out.shape
    width = downs.shape[1] // mp_count
    up_end = width + ups.shape[1]
    deltas = jnp.concatenate(
        [
            jnp.concatenate(
                [delta[at : at + 1], delta[at + 1 : at + 2]], axis=1
            )
            for at in range(0, subs * group, 2)
        ],
        axis=0,
    )
    for other in range(mp_count):
        mine = lax.axis_index("mp") == other
        kept_ups = jnp.where(mine, ups, 0.0)
        kept_deltas = jnp.where(mine, deltas, 0.0).astype(jnp.bfloat16)
        for z in range(z_count):
            ranks = slice(z * rows, (z + 1) * rows)
            shares_out[z, other, :, :width] = downs[
                ranks, other * width : (other + 1) * width
            ].astype(jnp.bfloat16)
            shares_out[z, other, :, width:up_end] = kept_ups[ranks].astype(jnp.bfloat16)
            shares_out[z, other, :, up_end:] = kept_deltas


def home_kernel(subs, received, loss, *rest):
    pieces, (sums_out, last_out) = rest[:-2], rest[-2:]
    z_count, mp_count, rows, _ = received.shape
    copies, _, sum_width = sums_out.shape
    sum_width = sum_width - loss.shape[1]
    total = None
    deltas = []
    for z in range(z_count):
        column = None
        for other in range(mp_count):
            part = received[z, other].astype(jnp.float32)
            column = part if column is None else column + part
        delta = column[:, sum_width:]
        deltas = deltas + [
            jnp.concatenate([delta[at : at + 1], delta[at + 1 : at + 2]], axis=1)
            for at in range(0, rows, 2)
        ]
        column = column[:, :sum_width]
        total = column if total is None else total + column
    for copy in range(copies):
        sums_out[copy, :, :sum_width] = total
        sums_out[copy, :, sum_width:] = loss[:rows]
    deltas = jnp.concatenate(deltas, axis=0).astype(jnp.bfloat16)
    count = len(pieces)
    lasts = []
    for piece in pieces:
        wq_rows = jnp.concatenate([piece[half, 0] for half in range(piece.shape[0])], axis=0)
        lasts.append(final_product(deltas, wq_rows))
    for choice in range(count):
        turn = lax.rem(lax.axis_index("x") + (count - choice), count)
        block = jnp.zeros(lasts[0].shape, jnp.float32)
        for candidate in range(count):
            block = block + jnp.where(turn == candidate, lasts[candidate], 0.0)
        width = block.shape[1]
        for z in range(z_count):
            last_out[z, :, choice * width : (choice + 1) * width] = block[
                z * subs : (z + 1) * subs
            ]


def return_kernel(sums, last, chunks_out, loss_out):
    z_count, mp_count, rows, chunk_width = chunks_out.shape
    total = sums[0]
    for part in range(1, sums.shape[0]):
        total = total + sums[part]
    sum_width = total.shape[1] - loss_out.shape[1]
    loss_out[...] = total[:, sum_width:]
    total = total[:, :sum_width].astype(jnp.bfloat16)
    half = chunk_width - sum_width
    for z in range(z_count):
        value = last[z]
        value = jnp.concatenate(
            [
                value[sub : sub + 1, side * half : (side + 1) * half]
                for sub in range(value.shape[0])
                for side in range(value.shape[1] // half)
            ],
            axis=0,
        )
        for other in range(mp_count):
            chunks_out[z, other, :, :sum_width] = total
            chunks_out[z, other, :, sum_width:] = jnp.where(
                lax.axis_index("z") == other, value, 0.0
            ).astype(jnp.bfloat16)


def portion_kernel(key_change, value_change, coef, key_weight, value_weight, down, out):
    total = final_product(key_change[...], key_weight[...]) + final_product(
        value_change[...], value_weight[...]
    )
    total = total + ADAPTER_SCALE * jnp.dot(
        coef[...], down[...], preferred_element_type=jnp.float32
    )
    out[...] = total.astype(jnp.bfloat16)


def local(
    query_emb,
    item_emb,
    pair_index,
    hard_index,
    hidden_in,
    lengths,
    w_query,
    key_weight_matrix,
    value_weight_matrix,
    w_out,
    key_down_matrix,
    key_up_matrix,
    value_down,
    value_up_matrix,
):
    bf16, f32 = jnp.bfloat16, jnp.float32
    x_count = lax.axis_size("x")
    z_count = lax.axis_size("z")
    plane_count = lax.axis_size(PLANE)
    dp_count = z_count * plane_count
    mp_count = lax.axis_size("mp")
    local_rows = query_emb.shape[0]
    batch_size = local_rows * dp_count
    feature_width = query_emb.shape[1]
    sub_count = hidden_in.shape[0]
    seq_len = hidden_in.shape[2]
    token_count = sub_count * seq_len
    full_rows = lax.all_gather(hidden_in, "mp", axis=3, tiled=True)
    model_width = full_rows.shape[3]
    token_inputs = full_rows.reshape(token_count, model_width)
    seq_lengths = lengths[:, 0]
    last_rows = jnp.arange(sub_count, dtype=jnp.int32) * seq_len + seq_lengths - 1

    query_slices = spread(query_emb, "mp")
    chunks = jnp.concatenate(
        [jnp.broadcast_to(item_emb[None], query_slices.shape), query_slices], axis=1
    )
    chunks = jnp.broadcast_to(chunks[:, None], (z_count, plane_count) + chunks.shape[1:])
    received = swap(chunks.reshape((dp_count,) + chunks.shape[2:]), DP)
    queries_all = received[:, local_rows:].reshape(batch_size, feature_width)
    items_all = (
        received[:, :local_rows]
        .reshape(z_count, plane_count, local_rows, feature_width)
        .transpose(1, 0, 2, 3)
        .reshape(batch_size, feature_width)
    )
    partial_scores = final_product(query_emb, items_all)
    score_parts = spread(partial_scores, "mp")

    rows_here, query_width = w_query.shape
    both = jnp.stack([w_query, w_out.T])
    both, partial_scores = lax.optimization_barrier((both, partial_scores))
    other = lax.ppermute(both, "h", [(0, 1), (1, 0)])
    lower = lax.axis_index("h") == 0
    both = jnp.stack([jnp.where(lower, both, other), jnp.where(lower, other, both)])
    pieces = [both] + [
        lax.ppermute(both, "x", [(a, (a + turn) % x_count) for a in range(x_count)])
        for turn in range(1, x_count)
    ]

    last_tokens = jnp.concatenate(
        [
            lax.dynamic_slice_in_dim(token_inputs, last_rows[sub], 1, 0)
            for sub in range(sub_count)
        ],
        axis=0,
    )
    last_slices = (
        last_tokens.reshape(sub_count, z_count, x_count, feature_width // x_count)
        .transpose(1, 2, 0, 3)
        .reshape(z_count, x_count * sub_count, feature_width // x_count)
    )

    adapter_rank = key_down_matrix.shape[1]
    down_both = jnp.concatenate([key_down_matrix, value_down], axis=1)
    reduced_pair = jnp.dot(token_inputs, down_both, preferred_element_type=f32).astype(bf16)
    reduced_key = reduced_pair[:, :adapter_rank]
    reduced_value = reduced_pair[:, adapter_rank:]
    key_rows = (
        jnp.dot(token_inputs, key_weight_matrix, preferred_element_type=f32)
        + ADAPTER_SCALE * jnp.dot(reduced_key, key_up_matrix, preferred_element_type=f32)
    ).astype(bf16)
    value_rows = (
        jnp.dot(token_inputs, value_weight_matrix, preferred_element_type=f32)
        + ADAPTER_SCALE * jnp.dot(reduced_value, value_up_matrix, preferred_element_type=f32)
    ).astype(bf16)

    chunks, residual, loss_part = call(
        functools.partial(residual_kernel, z_count, plane_count),
        (
            jax.ShapeDtypeStruct((dp_count, local_rows, 2 * LANES), bf16),
            jax.ShapeDtypeStruct((local_rows, batch_size), bf16),
            jax.ShapeDtypeStruct((local_rows, LANES), f32),
        ),
        2**24,
    )(score_parts, hard_index, pair_index[:, None], last_slices)
    column_rows = swap(chunks, DP).reshape(batch_size, 2 * LANES)
    column_rows, key_rows, value_rows = lax.optimization_barrier(
        (column_rows, key_rows, value_rows)
    )
    column_grads, parts = call(
        functools.partial(gradient_kernel, z_count, sub_count),
        (
            jax.ShapeDtypeStruct((z_count * local_rows, feature_width), bf16),
            jax.ShapeDtypeStruct((z_count, 2 * sub_count, query_width + LANES), f32),
        ),
        2**26,
    )(column_rows, queries_all, loss_part, *pieces)
    parts = swap(parts, "z")
    own_grads = lax.dynamic_index_in_dim(
        column_grads.reshape(z_count, local_rows, feature_width),
        lax.axis_index("mp"),
        0,
        keepdims=False,
    )
    item_grad = lax.ppermute(
        own_grads,
        ("z", "mp"),
        [(a * mp_count + b, b * mp_count + a) for a in range(z_count) for b in range(mp_count)],
    )
    query_grad = (jnp.dot(residual, items_all, preferred_element_type=f32) * INV_TEMP).astype(bf16)

    share_rows = 2 * adapter_rank // z_count
    up_width = key_rows.shape[1]
    sum_width = feature_width + up_width
    chunk_width = sum_width + sub_count * query_width // share_rows
    key_change, value_change, coef, loss_part, shares = call(
        attention_kernel,
        (
            jax.ShapeDtypeStruct(key_rows.shape, bf16),
            jax.ShapeDtypeStruct(value_rows.shape, bf16),
            jax.ShapeDtypeStruct((token_count, 2 * adapter_rank), bf16),
            jax.ShapeDtypeStruct((2 * sub_count, LANES), f32),
            jax.ShapeDtypeStruct((z_count, mp_count, share_rows, chunk_width), bf16),
        ),
        2**26,
    )(lengths, parts, key_rows, value_rows, key_up_matrix, value_up_matrix, reduced_pair, token_inputs)
    grid_shape = shares.shape
    shares = swap(shares.reshape((-1,) + grid_shape[2:]), ("z", "mp")).reshape(grid_shape)

    block = model_width // mp_count
    whole = lambda array: pl.BlockSpec(array.shape, lambda step: (0, 0))
    along = lambda array: pl.BlockSpec((array.shape[0], block), lambda step: (0, step))
    down = lambda array: pl.BlockSpec((block, array.shape[1]), lambda step: (step, 0))
    down_rows = down_both.T
    portion = call(
        portion_kernel,
        jax.ShapeDtypeStruct((token_count, model_width), bf16),
        2**29,
        grid=(mp_count,),
        in_specs=[
            whole(key_change),
            whole(value_change),
            whole(coef),
            down(key_weight_matrix),
            down(value_weight_matrix),
            along(down_rows),
        ],
        out_specs=pl.BlockSpec((token_count, block), lambda step: (0, step)),
    )(key_change, value_change, coef, key_weight_matrix, value_weight_matrix, down_rows)
    input_sum = lax.psum_scatter(portion, "mp", scatter_dimension=1, tiled=True).astype(f32)
    sums, last_part = call(
        functools.partial(home_kernel, sub_count),
        (
            jax.ShapeDtypeStruct((plane_count, share_rows, sum_width + LANES), f32),
            jax.ShapeDtypeStruct((z_count, sub_count, feature_width), f32),
        ),
        2**24,
    )(shares, loss_part, *pieces)
    chunks, loss_sum = call(
        return_kernel,
        (
            jax.ShapeDtypeStruct(grid_shape, bf16),
            jax.ShapeDtypeStruct((share_rows, LANES), f32),
        ),
        2**24,
    )(swap(sums, PLANE), last_part)
    mean_loss = loss_sum[0, 0] / batch_size
    summed = swap(chunks.reshape((-1,) + grid_shape[2:]), ("z", "mp")).reshape(grid_shape)
    own = lax.axis_index("mp")
    up_grad = lax.dynamic_index_in_dim(
        summed[:, :, :, feature_width:sum_width], own, 1, keepdims=False
    )
    up_grad = up_grad.reshape(2 * adapter_rank, up_width).astype(f32)
    last_rows_grad = jnp.sum(
        lax.dynamic_index_in_dim(
            summed[:, :, :, sum_width:], own, 0, keepdims=False
        ).astype(f32),
        axis=0,
    ).reshape(sub_count, feature_width) + item_grad[:sub_count].astype(f32)
    row_ids = jnp.arange(token_count, dtype=jnp.int32)[:, None]
    for sub in range(sub_count):
        input_sum = input_sum + jnp.where(
            row_ids == last_rows[sub], last_rows_grad[sub][None, :], 0.0
        )
    input_grad = input_sum.astype(bf16).reshape(hidden_in.shape)
    down_grad = (
        summed[:, :, :, :feature_width]
        .transpose(0, 2, 1, 3)
        .reshape(2 * adapter_rank, model_width)
        .astype(f32)
        .T
    )
    return (
        mean_loss,
        query_grad,
        item_grad,
        input_grad,
        down_grad[:, :adapter_rank],
        down_grad[:, adapter_rank:],
        up_grad[:adapter_rank],
        up_grad[adapter_rank:],
    )


def solution(mesh):
    fine = Mesh(
        mesh.devices.reshape(8, 4, 2, mesh.devices.shape[1]), ("z", "x", "h", "mp")
    )
    in_specs = (
        P(DP, "mp"),
        P(DP, "mp"),
        P(DP),
        P(DP, None),
        P(None, DP, None, "mp"),
        P(None, DP),
        P(DP, "mp"),
        P(None, "mp"),
        P(None, "mp"),
        P("mp", DP),
        P(),
        P(None, "mp"),
        P(),
        P(None, "mp"),
    )
    out_specs = (
        P(),
        P(DP, "mp"),
        P(DP, "mp"),
        P(None, DP, None, "mp"),
        P(),
        P(),
        P(None, "mp"),
        P(None, "mp"),
    )
    return jax.shard_map(local, mesh=fine, in_specs=in_specs, out_specs=out_specs, check_vma=False)
```

```python
import functools
import math

import jax
import jax.numpy as jnp
from jax import lax
from jax.experimental import pallas as pl
from jax.experimental.pallas import tpu as pltpu
from jax.sharding import Mesh
from jax.sharding import PartitionSpec as P

HEADS = 32
KV_HEADS = 8
HEAD_DIM = 128
LANES = 128

INV_TEMP = 50.0
HARD_NEGATIVE_ADD = 4.0
ADAPTER_SCALE = 2.0

PLANE = ("x", "h")
DP = ("z", "x", "h")


def final_product(left_side, right_side):
    return lax.dot_general(
        left_side, right_side, (((1,), (1,)), ((), ())), preferred_element_type=jnp.float32
    )


def first_product(left_side, right_side):
    return lax.dot_general(
        left_side, right_side, (((0,), (0,)), ((), ())), preferred_element_type=jnp.float32
    )


def spread(block, axes):
    count = lax.axis_size(axes)
    copies = jnp.broadcast_to(block[None], (count,) + block.shape)
    return lax.all_to_all(copies, axes, split_axis=0, concat_axis=0, tiled=True)


def swap(blocks, axes):
    return lax.all_to_all(blocks, axes, split_axis=0, concat_axis=0, tiled=True)


def call(kernel, out_shape, flops, **layout):
    return pl.pallas_call(
        kernel,
        out_shape=out_shape,
        compiler_params=pltpu.CompilerParams(vmem_limit_bytes=56 * 1024 * 1024),
        cost_estimate=pl.CostEstimate(flops=flops, bytes_accessed=2**20, transcendentals=4096),
        **layout,
    )


def upright(line):
    count = line.shape[1]
    row = lax.broadcasted_iota(jnp.int32, (count, count), 0)
    column = lax.broadcasted_iota(jnp.int32, (count, count), 1)
    return jnp.sum(jnp.where(row == column, line, 0), axis=1, keepdims=True)


def residual_kernel(
    z_count, plane_count, parts, hard, pair, tokens, chunks, residual_out, loss_out
):
    rows = parts.shape[1]
    batch_size = parts.shape[2]
    pair_scores = parts[0]
    for part in range(1, parts.shape[0]):
        pair_scores = pair_scores + parts[part]
    column = lax.broadcasted_iota(jnp.int32, (rows, batch_size), 1)
    inner = column % rows
    outer = column // rows
    item = ((outer % z_count) * plane_count + outer // z_count) * rows + inner
    count = jnp.zeros((rows, batch_size), jnp.float32)
    for choice in range(hard.shape[0]):
        count = count + jnp.where(upright(hard[choice : choice + 1]) == item, 1.0, 0.0)
    logits = pair_scores * INV_TEMP + HARD_NEGATIVE_ADD * count
    top = jnp.max(logits, axis=1, keepdims=True)
    log_total = top + jnp.log(jnp.sum(jnp.exp(logits - top), axis=1, keepdims=True))
    target = jnp.where(upright(pair[...]) == item, 1.0, 0.0)
    picked = jnp.sum(target * logits, axis=1, keepdims=True)
    loss = jnp.sum(log_total - picked, axis=0, keepdims=True)
    loss_out[...] = jnp.broadcast_to(loss, loss_out.shape)
    residual = jnp.exp(logits - log_total) - target
    residual_out[...] = residual.astype(jnp.bfloat16)
    width = z_count * rows
    pad = jnp.zeros((rows, LANES - width), jnp.float32)
    for plane in range(plane_count):
        block = jnp.concatenate([residual[:, plane * width : (plane + 1) * width], pad], axis=1)
        block = block.astype(jnp.bfloat16)
        for z in range(z_count):
            chunks[z * plane_count + plane, :, :LANES] = block
            chunks[z * plane_count + plane, :, LANES:] = tokens[z]


def gradient_kernel(z_count, subs, received, queries, loss, *rest):
    pieces, (item_out, parts_out) = rest[:-2], rest[-2:]
    item_rows = item_out.shape[0]
    count = len(pieces)
    width = queries.shape[1] // count
    every = lax.dot_general(
        received[:, :LANES],
        queries[...],
        (((0,), (0,)), ((), ())),
        preferred_element_type=jnp.float32,
    )
    grads = (every[:item_rows] * INV_TEMP).astype(jnp.bfloat16)
    item_out[...] = grads
    picks = subs * z_count
    row = lax.broadcasted_iota(jnp.int32, (picks, item_rows), 0)
    column = lax.broadcasted_iota(jnp.int32, (picks, item_rows), 1)
    per_z = item_rows // z_count
    wanted = jnp.where((row // subs) * per_z + row % subs == column, 1.0, 0.0)
    cotangents = jnp.dot(
        wanted.astype(jnp.bfloat16), grads, preferred_element_type=jnp.float32
    )
    senders = received.shape[0] // per_z
    planes = senders // z_count
    row = lax.broadcasted_iota(jnp.int32, (picks, received.shape[0]), 0)
    column = lax.broadcasted_iota(jnp.int32, (picks, received.shape[0]), 1)
    plane = lax.axis_index(PLANE)
    first = ((row // subs) * planes + plane) * per_z + row % subs
    attn = query = None
    for turn, piece in enumerate(pieces):
        block = lax.rem(lax.axis_index("x") + (count - turn), count)
        cot = jnp.zeros((picks, width), jnp.float32)
        for choice in range(count):
            cot = cot + jnp.where(
                block == choice, cotangents[:, choice * width : (choice + 1) * width], 0.0
            )
        chosen = jnp.where(first + block * subs == column, 1.0, 0.0).astype(jnp.bfloat16)
        token = jnp.dot(chosen, received[:, LANES:], preferred_element_type=jnp.float32)
        wq_rows = jnp.concatenate([piece[half, 0] for half in range(piece.shape[0])], axis=0)
        wo_rows = jnp.concatenate([piece[half, 1] for half in range(piece.shape[0])], axis=0)
        attn_term = jnp.dot(cot.astype(jnp.bfloat16), wo_rows, preferred_element_type=jnp.float32)
        query_term = jnp.dot(
            token.astype(jnp.bfloat16), wq_rows, preferred_element_type=jnp.float32
        )
        attn = attn_term if attn is None else attn + attn_term
        query = query_term if query is None else query + query_term
    end = attn.shape[1]
    for z in range(z_count):
        parts_out[z, :subs, :end] = attn[z * subs : (z + 1) * subs]
        parts_out[z, subs:, :end] = query[z * subs : (z + 1) * subs]
        parts_out[z, :, end:] = loss[: 2 * subs]


def attention_kernel(
    lengths,
    parts,
    keys,
    values,
    key_up,
    value_up,
    reduced,
    tokens,
    key_weight,
    value_weight,
    down,
    portion_out,
    loss_out,
    shares_out,
):
    subs = parts.shape[1] // 2
    token_count = keys.shape[0]
    seq_len = token_count // subs
    group = parts.shape[2] // HEAD_DIM - 1
    total = parts[0]
    for part in range(1, parts.shape[0]):
        total = total + parts[part]
    loss_out[...] = total[:, group * HEAD_DIM :]
    both = total.astype(jnp.bfloat16).astype(jnp.float32)

    def heads(first):
        return jnp.concatenate(
            [
                both[first + sub : first + sub + 1, head * HEAD_DIM : (head + 1) * HEAD_DIM]
                for sub in range(subs)
                for head in range(group)
            ],
            axis=0,
        )

    grad_heads = heads(0)
    q_heads = heads(subs)
    score_scale = 1.0 / math.sqrt(HEAD_DIM)
    raw = final_product(q_heads.astype(jnp.bfloat16), keys[...]) * score_scale
    row_sub = lax.broadcasted_iota(jnp.int32, raw.shape, 0) // group
    token = lax.broadcasted_iota(jnp.int32, raw.shape, 1)
    live = jnp.zeros(raw.shape, jnp.bool_)
    for sub in range(subs):
        first = sub * seq_len
        inside = (token >= first) & (token < first + lengths[0, sub])
        live = live | (inside & (row_sub == sub))
    raw = jnp.where(live, raw, -jnp.inf)
    weights = jnp.exp(raw - jnp.max(raw, axis=1, keepdims=True))
    probs = weights / jnp.sum(weights, axis=1, keepdims=True)
    prob_half = probs.astype(jnp.bfloat16).astype(jnp.float32)
    prob_grad = final_product(grad_heads.astype(jnp.bfloat16), values[...])
    score_grad = (
        probs * (prob_grad - jnp.sum(probs * prob_grad, axis=1, keepdims=True)) * score_scale
    )
    score_grad = score_grad.astype(jnp.bfloat16)
    delta = jnp.dot(score_grad, keys[...], preferred_element_type=jnp.float32)
    score_grad = score_grad.astype(jnp.float32)
    key_change = first_product(score_grad, q_heads).astype(jnp.bfloat16)
    value_change = first_product(prob_half, grad_heads).astype(jnp.bfloat16)
    key_coef = final_product(key_change, key_up[...])
    value_coef = final_product(value_change, value_up[...])
    coef = jnp.concatenate([key_coef, value_coef], axis=1).astype(jnp.bfloat16)
    rank = key_up.shape[0]
    ups = ADAPTER_SCALE * jnp.concatenate(
        [
            first_product(reduced[...], key_change)[:rank],
            first_product(reduced[...], value_change)[rank:],
        ],
        axis=0,
    )
    downs = ADAPTER_SCALE * first_product(coef, tokens[...])
    z_count, mp_count, rows, chunk_width = shares_out.shape
    width = downs.shape[1] // mp_count
    up_end = width + ups.shape[1]
    deltas = jnp.concatenate(
        [
            jnp.concatenate(
                [delta[at : at + 1], delta[at + 1 : at + 2]], axis=1
            )
            for at in range(0, subs * group, 2)
        ],
        axis=0,
    )
    for other in range(mp_count):
        mine = lax.axis_index("mp") == other
        kept_ups = jnp.where(mine, ups, 0.0)
        kept_deltas = jnp.where(mine, deltas, 0.0).astype(jnp.bfloat16)
        for z in range(z_count):
            ranks = slice(z * rows, (z + 1) * rows)
            shares_out[z, other, :, :width] = downs[
                ranks, other * width : (other + 1) * width
            ].astype(jnp.bfloat16)
            shares_out[z, other, :, width:up_end] = kept_ups[ranks].astype(jnp.bfloat16)
            shares_out[z, other, :, up_end:] = kept_deltas
    for other in range(mp_count):
        features = slice(other * width, (other + 1) * width)
        portion = final_product(key_change, key_weight[features]) + final_product(
            value_change, value_weight[features]
        )
        portion = portion + ADAPTER_SCALE * jnp.dot(
            coef, down[:, features], preferred_element_type=jnp.float32
        )
        portion_out[:, features] = portion.astype(jnp.bfloat16)


def home_kernel(subs, received, loss, *rest):
    pieces, (sums_out, last_out) = rest[:-2], rest[-2:]
    z_count, mp_count, rows, _ = received.shape
    copies, _, sum_width = sums_out.shape
    sum_width = sum_width - loss.shape[1]
    total = None
    deltas = []
    for z in range(z_count):
        column = None
        for other in range(mp_count):
            part = received[z, other].astype(jnp.float32)
            column = part if column is None else column + part
        delta = column[:, sum_width:]
        deltas = deltas + [
            jnp.concatenate([delta[at : at + 1], delta[at + 1 : at + 2]], axis=1)
            for at in range(0, rows, 2)
        ]
        column = column[:, :sum_width]
        total = column if total is None else total + column
    for copy in range(copies):
        sums_out[copy, :, :sum_width] = total
        sums_out[copy, :, sum_width:] = loss[:rows]
    deltas = jnp.concatenate(deltas, axis=0).astype(jnp.bfloat16)
    count = len(pieces)
    lasts = []
    for piece in pieces:
        wq_rows = jnp.concatenate([piece[half, 0] for half in range(piece.shape[0])], axis=0)
        lasts.append(final_product(deltas, wq_rows))
    for choice in range(count):
        turn = lax.rem(lax.axis_index("x") + (count - choice), count)
        block = jnp.zeros(lasts[0].shape, jnp.float32)
        for candidate in range(count):
            block = block + jnp.where(turn == candidate, lasts[candidate], 0.0)
        width = block.shape[1]
        for z in range(z_count):
            last_out[z, :, choice * width : (choice + 1) * width] = block[
                z * subs : (z + 1) * subs
            ]


def return_kernel(sums, last, chunks_out, loss_out):
    z_count, mp_count, rows, chunk_width = chunks_out.shape
    total = sums[0]
    for part in range(1, sums.shape[0]):
        total = total + sums[part]
    sum_width = total.shape[1] - loss_out.shape[1]
    loss_out[...] = total[:, sum_width:]
    total = total[:, :sum_width].astype(jnp.bfloat16)
    half = chunk_width - sum_width
    for z in range(z_count):
        value = last[z]
        value = jnp.concatenate(
            [
                value[sub : sub + 1, side * half : (side + 1) * half]
                for sub in range(value.shape[0])
                for side in range(value.shape[1] // half)
            ],
            axis=0,
        )
        for other in range(mp_count):
            chunks_out[z, other, :, :sum_width] = total
            chunks_out[z, other, :, sum_width:] = jnp.where(
                lax.axis_index("z") == other, value, 0.0
            ).astype(jnp.bfloat16)


def local(
    query_emb,
    item_emb,
    pair_index,
    hard_index,
    hidden_in,
    lengths,
    w_query,
    key_weight_matrix,
    value_weight_matrix,
    w_out,
    key_down_matrix,
    key_up_matrix,
    value_down,
    value_up_matrix,
):
    bf16, f32 = jnp.bfloat16, jnp.float32
    x_count = lax.axis_size("x")
    z_count = lax.axis_size("z")
    plane_count = lax.axis_size(PLANE)
    dp_count = z_count * plane_count
    mp_count = lax.axis_size("mp")
    local_rows = query_emb.shape[0]
    batch_size = local_rows * dp_count
    feature_width = query_emb.shape[1]
    sub_count = hidden_in.shape[0]
    seq_len = hidden_in.shape[2]
    token_count = sub_count * seq_len
    full_rows = lax.all_gather(hidden_in, "mp", axis=3, tiled=True)
    model_width = full_rows.shape[3]
    token_inputs = full_rows.reshape(token_count, model_width)
    seq_lengths = lengths[:, 0]
    last_rows = jnp.arange(sub_count, dtype=jnp.int32) * seq_len + seq_lengths - 1

    lower = lax.axis_index("h") == 0

    def pair_up(block):
        other = lax.ppermute(block, "h", [(0, 1), (1, 0)])
        return jnp.stack([jnp.where(lower, block, other), jnp.where(lower, other, block)])

    emb_pair = pair_up(jnp.stack([item_emb, query_emb]))
    pair_rows = 2 * local_rows
    item_pair = emb_pair[:, 0].reshape(pair_rows, feature_width)
    query_pair = emb_pair[:, 1].reshape(pair_rows, feature_width)
    both = pair_up(jnp.stack([w_query, w_out.T]))

    query_slices = spread(query_pair, "mp")
    both, query_slices = lax.optimization_barrier((both, query_slices))
    chunks = jnp.concatenate(
        [jnp.broadcast_to(item_pair[None], query_slices.shape), query_slices], axis=1
    )
    chunks = jnp.broadcast_to(chunks[:, None], (z_count, x_count) + chunks.shape[1:])
    received = swap(chunks.reshape((z_count * x_count,) + chunks.shape[2:]), ("z", "x"))
    queries_all = received[:, pair_rows:].reshape(batch_size, feature_width)
    items_all = (
        received[:, :pair_rows]
        .reshape(z_count, plane_count, local_rows, feature_width)
        .transpose(1, 0, 2, 3)
        .reshape(batch_size, feature_width)
    )
    partial_scores = final_product(query_emb, items_all)
    score_parts = spread(partial_scores, "mp")

    query_width = w_query.shape[1]
    pieces = [both] + [
        lax.ppermute(both, "x", [(a, (a + turn) % x_count) for a in range(x_count)])
        for turn in range(1, x_count)
    ]

    last_tokens = jnp.concatenate(
        [
            lax.dynamic_slice_in_dim(token_inputs, last_rows[sub], 1, 0)
            for sub in range(sub_count)
        ],
        axis=0,
    )
    last_slices = (
        last_tokens.reshape(sub_count, z_count, x_count, feature_width // x_count)
        .transpose(1, 2, 0, 3)
        .reshape(z_count, x_count * sub_count, feature_width // x_count)
    )

    adapter_rank = key_down_matrix.shape[1]
    down_both = jnp.concatenate([key_down_matrix, value_down], axis=1)
    reduced_pair = jnp.dot(token_inputs, down_both, preferred_element_type=f32).astype(bf16)
    reduced_key = reduced_pair[:, :adapter_rank]
    reduced_value = reduced_pair[:, adapter_rank:]
    key_rows = (
        jnp.dot(token_inputs, key_weight_matrix, preferred_element_type=f32)
        + ADAPTER_SCALE * jnp.dot(reduced_key, key_up_matrix, preferred_element_type=f32)
    ).astype(bf16)
    value_rows = (
        jnp.dot(token_inputs, value_weight_matrix, preferred_element_type=f32)
        + ADAPTER_SCALE * jnp.dot(reduced_value, value_up_matrix, preferred_element_type=f32)
    ).astype(bf16)

    chunks, residual, loss_part = call(
        functools.partial(residual_kernel, z_count, plane_count),
        (
            jax.ShapeDtypeStruct((dp_count, local_rows, 2 * LANES), bf16),
            jax.ShapeDtypeStruct((local_rows, batch_size), bf16),
            jax.ShapeDtypeStruct((local_rows, LANES), f32),
        ),
        2**24,
    )(score_parts, hard_index.T, pair_index[None], last_slices)
    column_rows = swap(chunks, DP).reshape(batch_size, 2 * LANES)
    column_rows, key_rows, value_rows = lax.optimization_barrier(
        (column_rows, key_rows, value_rows)
    )
    column_grads, parts = call(
        functools.partial(gradient_kernel, z_count, sub_count),
        (
            jax.ShapeDtypeStruct((z_count * local_rows, feature_width), bf16),
            jax.ShapeDtypeStruct((z_count, 2 * sub_count, query_width + LANES), f32),
        ),
        2**26,
    )(column_rows, queries_all, loss_part, *pieces)
    parts = swap(parts, "z")
    own_grads = lax.dynamic_index_in_dim(
        column_grads.reshape(z_count, local_rows, feature_width),
        lax.axis_index("mp"),
        0,
        keepdims=False,
    )
    item_grad = lax.ppermute(
        own_grads,
        ("z", "mp"),
        [(a * mp_count + b, b * mp_count + a) for a in range(z_count) for b in range(mp_count)],
    )
    query_grad = (jnp.dot(residual, items_all, preferred_element_type=f32) * INV_TEMP).astype(bf16)

    share_rows = 2 * adapter_rank // z_count
    up_width = key_rows.shape[1]
    sum_width = feature_width + up_width
    chunk_width = sum_width + sub_count * query_width // share_rows
    portion, loss_part, shares = call(
        attention_kernel,
        (
            jax.ShapeDtypeStruct((token_count, model_width), bf16),
            jax.ShapeDtypeStruct((2 * sub_count, LANES), f32),
            jax.ShapeDtypeStruct((z_count, mp_count, share_rows, chunk_width), bf16),
        ),
        2**26,
    )(
        lengths.T,
        parts,
        key_rows,
        value_rows,
        key_up_matrix,
        value_up_matrix,
        reduced_pair,
        token_inputs,
        key_weight_matrix,
        value_weight_matrix,
        down_both.T,
    )
    grid_shape = shares.shape
    shares = swap(shares.reshape((-1,) + grid_shape[2:]), ("z", "mp")).reshape(grid_shape)

    input_sum = lax.psum_scatter(portion, "mp", scatter_dimension=1, tiled=True).astype(f32)
    sums, last_part = call(
        functools.partial(home_kernel, sub_count),
        (
            jax.ShapeDtypeStruct((plane_count, share_rows, sum_width + LANES), f32),
            jax.ShapeDtypeStruct((z_count, sub_count, feature_width), f32),
        ),
        2**24,
    )(shares, loss_part, *pieces)
    chunks, loss_sum = call(
        return_kernel,
        (
            jax.ShapeDtypeStruct(grid_shape, bf16),
            jax.ShapeDtypeStruct((share_rows, LANES), f32),
        ),
        2**24,
    )(swap(sums, PLANE), last_part)
    mean_loss = loss_sum[0, 0] / batch_size
    summed = swap(chunks.reshape((-1,) + grid_shape[2:]), ("z", "mp")).reshape(grid_shape)
    own = lax.axis_index("mp")
    up_grad = lax.dynamic_index_in_dim(
        summed[:, :, :, feature_width:sum_width], own, 1, keepdims=False
    )
    up_grad = up_grad.reshape(2 * adapter_rank, up_width).astype(f32)
    last_rows_grad = jnp.sum(
        lax.dynamic_index_in_dim(
            summed[:, :, :, sum_width:], own, 0, keepdims=False
        ).astype(f32),
        axis=0,
    ).reshape(sub_count, feature_width) + item_grad[:sub_count].astype(f32)
    row_ids = jnp.arange(token_count, dtype=jnp.int32)[:, None]
    for sub in range(sub_count):
        input_sum = input_sum + jnp.where(
            row_ids == last_rows[sub], last_rows_grad[sub][None, :], 0.0
        )
    input_grad = input_sum.astype(bf16).reshape(hidden_in.shape)
    down_grad = (
        summed[:, :, :, :feature_width]
        .transpose(0, 2, 1, 3)
        .reshape(2 * adapter_rank, model_width)
        .astype(f32)
        .T
    )
    return (
        mean_loss,
        query_grad,
        item_grad,
        input_grad,
        down_grad[:, :adapter_rank],
        down_grad[:, adapter_rank:],
        up_grad[:adapter_rank],
        up_grad[adapter_rank:],
    )


def solution(mesh):
    fine = Mesh(
        mesh.devices.reshape(8, 4, 2, mesh.devices.shape[1]), ("z", "x", "h", "mp")
    )
    in_specs = (
        P(DP, "mp"),
        P(DP, "mp"),
        P(DP),
        P(DP, None),
        P(None, DP, None, "mp"),
        P(None, DP),
        P(DP, "mp"),
        P(None, "mp"),
        P(None, "mp"),
        P("mp", DP),
        P(),
        P(None, "mp"),
        P(),
        P(None, "mp"),
    )
    out_specs = (
        P(),
        P(DP, "mp"),
        P(DP, "mp"),
        P(None, DP, None, "mp"),
        P(),
        P(),
        P(None, "mp"),
        P(None, "mp"),
    )
    return jax.shard_map(local, mesh=fine, in_specs=in_specs, out_specs=out_specs, check_vma=False)
```

```python
import functools
import math

import jax
import jax.numpy as jnp
from jax import lax
from jax.experimental import pallas as pl
from jax.experimental.pallas import tpu as pltpu
from jax.sharding import Mesh
from jax.sharding import PartitionSpec as P

HEADS = 32
KV_HEADS = 8
HEAD_DIM = 128
LANES = 128

INV_TEMP = 50.0
HARD_NEGATIVE_ADD = 4.0
ADAPTER_SCALE = 2.0

PLANE = ("x", "h")
MP = ("y", "c")
DP = ("z", "x", "h")


def final_product(left_side, right_side):
    return lax.dot_general(
        left_side, right_side, (((1,), (1,)), ((), ())), preferred_element_type=jnp.float32
    )


def first_product(left_side, right_side):
    return lax.dot_general(
        left_side, right_side, (((0,), (0,)), ((), ())), preferred_element_type=jnp.float32
    )


def spread(block, axes):
    count = lax.axis_size(axes)
    copies = jnp.broadcast_to(block[None], (count,) + block.shape)
    return lax.all_to_all(copies, axes, split_axis=0, concat_axis=0, tiled=True)


def swap(blocks, axes):
    return lax.all_to_all(blocks, axes, split_axis=0, concat_axis=0, tiled=True)


def feature_block(side, turn):
    y_count = lax.axis_size("y")
    core = lax.rem(lax.axis_index("c") + side, 2)
    return lax.rem(lax.axis_index("y") + (y_count - turn), y_count) * 2 + core


def call(kernel, out_shape, flops, **layout):
    return pl.pallas_call(
        kernel,
        out_shape=out_shape,
        compiler_params=pltpu.CompilerParams(vmem_limit_bytes=56 * 1024 * 1024),
        cost_estimate=pl.CostEstimate(flops=flops, bytes_accessed=2**20, transcendentals=4096),
        **layout,
    )


def upright(line):
    count = line.shape[1]
    row = lax.broadcasted_iota(jnp.int32, (count, count), 0)
    column = lax.broadcasted_iota(jnp.int32, (count, count), 1)
    return jnp.sum(jnp.where(row == column, line, 0), axis=1, keepdims=True)


def residual_kernel(
    z_count, plane_count, parts, hard, pair, tokens, chunks, residual_out, loss_out
):
    rows = parts.shape[1]
    batch_size = parts.shape[2]
    pair_scores = parts[0]
    for part in range(1, parts.shape[0]):
        pair_scores = pair_scores + parts[part]
    column = lax.broadcasted_iota(jnp.int32, (rows, batch_size), 1)
    inner = column % rows
    outer = column // rows
    item = ((outer % z_count) * plane_count + outer // z_count) * rows + inner
    count = jnp.zeros((rows, batch_size), jnp.float32)
    for choice in range(hard.shape[0]):
        count = count + jnp.where(upright(hard[choice : choice + 1]) == item, 1.0, 0.0)
    logits = pair_scores * INV_TEMP + HARD_NEGATIVE_ADD * count
    top = jnp.max(logits, axis=1, keepdims=True)
    log_total = top + jnp.log(jnp.sum(jnp.exp(logits - top), axis=1, keepdims=True))
    target = jnp.where(upright(pair[...]) == item, 1.0, 0.0)
    picked = jnp.sum(target * logits, axis=1, keepdims=True)
    loss = jnp.sum(log_total - picked, axis=0, keepdims=True)
    loss_out[...] = jnp.broadcast_to(loss, loss_out.shape)
    residual = jnp.exp(logits - log_total) - target
    residual_out[...] = residual.astype(jnp.bfloat16)
    width = z_count * rows
    pad = jnp.zeros((rows, LANES - width), jnp.float32)
    y_count = lax.axis_size("y")
    slices = []
    for z in range(z_count):
        side = lax.rem(lax.axis_index("c") + z, 2)
        turn = lax.rem(lax.axis_index("y") + (y_count - z // 2), y_count)
        slices.append(tokens[side * y_count + turn])
    for plane in range(plane_count):
        block = jnp.concatenate([residual[:, plane * width : (plane + 1) * width], pad], axis=1)
        block = block.astype(jnp.bfloat16)
        for z in range(z_count):
            chunks[z * plane_count + plane, :, :LANES] = block
            chunks[z * plane_count + plane, :, LANES:] = slices[z]


def token_kernel(
    mine, theirs, key_weight, value_weight, key_down, value_down, key_up, value_up, *outs
):
    low_key_out, low_value_out, keys_out, values_out = outs
    width = mine.shape[2]
    sums = [None] * 4
    for side, pieces in enumerate((mine, theirs)):
        for turn in range(pieces.shape[0]):
            start = pl.multiple_of(feature_block(side, turn) * width, width)
            rows = pl.ds(start, width)
            piece = pieces[turn]
            terms = [
                final_product(piece, key_down[:, rows]),
                final_product(piece, value_down[:, rows]),
                jnp.dot(piece, key_weight[rows], preferred_element_type=jnp.float32),
                jnp.dot(piece, value_weight[rows], preferred_element_type=jnp.float32),
            ]
            sums = [b if a is None else a + b for a, b in zip(sums, terms)]
    low_key, low_value = sums[0].astype(jnp.bfloat16), sums[1].astype(jnp.bfloat16)
    low_key_out[...] = low_key
    low_value_out[...] = low_value
    key_rise = jnp.dot(low_key, key_up[...], preferred_element_type=jnp.float32)
    value_rise = jnp.dot(low_value, value_up[...], preferred_element_type=jnp.float32)
    keys_out[...] = (sums[2] + ADAPTER_SCALE * key_rise).astype(jnp.bfloat16)
    values_out[...] = (sums[3] + ADAPTER_SCALE * value_rise).astype(jnp.bfloat16)


def gradient_kernel(z_count, subs, received, queries, loss, *rest):
    pieces, (item_out, parts_out) = rest[:-2], rest[-2:]
    item_rows = item_out.shape[0]
    count = len(pieces)
    width = queries.shape[1] // count
    every = lax.dot_general(
        received[:, :LANES],
        queries[...],
        (((0,), (0,)), ((), ())),
        preferred_element_type=jnp.float32,
    )
    grads = (every[:item_rows] * INV_TEMP).astype(jnp.bfloat16)
    item_out[...] = grads
    picks = subs * z_count
    row = lax.broadcasted_iota(jnp.int32, (picks, item_rows), 0)
    column = lax.broadcasted_iota(jnp.int32, (picks, item_rows), 1)
    per_z = item_rows // z_count
    wanted = jnp.where((row // subs) * per_z + row % subs == column, 1.0, 0.0)
    cotangents = jnp.dot(
        wanted.astype(jnp.bfloat16), grads, preferred_element_type=jnp.float32
    )
    senders = received.shape[0] // per_z
    planes = senders // z_count
    row = lax.broadcasted_iota(jnp.int32, (picks, received.shape[0]), 0)
    column = lax.broadcasted_iota(jnp.int32, (picks, received.shape[0]), 1)
    plane = lax.axis_index(PLANE)
    first = ((row // subs) * planes + plane) * per_z + row % subs
    attn = query = None
    for turn, piece in enumerate(pieces):
        block = lax.rem(lax.axis_index("x") + (count - turn), count)
        cot = jnp.zeros((picks, width), jnp.float32)
        for choice in range(count):
            cot = cot + jnp.where(
                block == choice, cotangents[:, choice * width : (choice + 1) * width], 0.0
            )
        chosen = jnp.where(first + block * subs == column, 1.0, 0.0).astype(jnp.bfloat16)
        token = jnp.dot(chosen, received[:, LANES:], preferred_element_type=jnp.float32)
        wq_rows = jnp.concatenate([piece[half, 0] for half in range(piece.shape[0])], axis=0)
        wo_rows = jnp.concatenate([piece[half, 1] for half in range(piece.shape[0])], axis=0)
        attn_term = jnp.dot(cot.astype(jnp.bfloat16), wo_rows, preferred_element_type=jnp.float32)
        query_term = jnp.dot(
            token.astype(jnp.bfloat16), wq_rows, preferred_element_type=jnp.float32
        )
        attn = attn_term if attn is None else attn + attn_term
        query = query_term if query is None else query + query_term
    end = attn.shape[1]
    for z in range(z_count):
        parts_out[z, :subs, :end] = attn[z * subs : (z + 1) * subs]
        parts_out[z, subs:, :end] = query[z * subs : (z + 1) * subs]
        parts_out[z, :, end:] = loss[: 2 * subs]


def attention_kernel(
    lengths,
    parts,
    keys,
    values,
    key_up,
    value_up,
    low_key,
    low_value,
    mine,
    theirs,
    key_change_out,
    value_change_out,
    coef_out,
    loss_out,
    shares_out,
):
    subs = parts.shape[1] // 2
    token_count = keys.shape[0]
    seq_len = token_count // subs
    group = parts.shape[2] // HEAD_DIM - 1
    total = parts[0]
    for part in range(1, parts.shape[0]):
        total = total + parts[part]
    loss_out[...] = total[:, group * HEAD_DIM :]
    both = total.astype(jnp.bfloat16).astype(jnp.float32)

    def heads(first):
        return jnp.concatenate(
            [
                both[first + sub : first + sub + 1, head * HEAD_DIM : (head + 1) * HEAD_DIM]
                for sub in range(subs)
                for head in range(group)
            ],
            axis=0,
        )

    grad_heads = heads(0)
    q_heads = heads(subs)
    score_scale = 1.0 / math.sqrt(HEAD_DIM)
    raw = final_product(q_heads.astype(jnp.bfloat16), keys[...]) * score_scale
    row_sub = lax.broadcasted_iota(jnp.int32, raw.shape, 0) // group
    token = lax.broadcasted_iota(jnp.int32, raw.shape, 1)
    live = jnp.zeros(raw.shape, jnp.bool_)
    for sub in range(subs):
        first = sub * seq_len
        inside = (token >= first) & (token < first + lengths[0, sub])
        live = live | (inside & (row_sub == sub))
    raw = jnp.where(live, raw, -jnp.inf)
    weights = jnp.exp(raw - jnp.max(raw, axis=1, keepdims=True))
    probs = weights / jnp.sum(weights, axis=1, keepdims=True)
    prob_half = probs.astype(jnp.bfloat16).astype(jnp.float32)
    prob_grad = final_product(grad_heads.astype(jnp.bfloat16), values[...])
    score_grad = (
        probs * (prob_grad - jnp.sum(probs * prob_grad, axis=1, keepdims=True)) * score_scale
    )
    score_grad = score_grad.astype(jnp.bfloat16)
    delta = jnp.dot(score_grad, keys[...], preferred_element_type=jnp.float32)
    score_grad = score_grad.astype(jnp.float32)
    key_change = first_product(score_grad, q_heads).astype(jnp.bfloat16)
    value_change = first_product(prob_half, grad_heads).astype(jnp.bfloat16)
    key_coef = final_product(key_change, key_up[...])
    value_coef = final_product(value_change, value_up[...])
    coef = jnp.concatenate([key_coef, value_coef], axis=1).astype(jnp.bfloat16)
    key_change_out[...] = key_change
    value_change_out[...] = value_change
    coef_out[...] = coef
    ups = ADAPTER_SCALE * jnp.concatenate(
        [first_product(low_key[...], key_change), first_product(low_value[...], value_change)],
        axis=0,
    )
    z_count, mp_count, rows, chunk_width = shares_out.shape
    width = mine.shape[2]
    up_end = width + ups.shape[1]
    deltas = jnp.concatenate(
        [
            jnp.concatenate(
                [delta[at : at + 1], delta[at + 1 : at + 2]], axis=1
            )
            for at in range(0, subs * group, 2)
        ],
        axis=0,
    )
    for other in range(mp_count):
        own = lax.axis_index(MP) == other
        kept_ups = jnp.where(own, ups, 0.0)
        kept_deltas = jnp.where(own, deltas, 0.0).astype(jnp.bfloat16)
        for z in range(z_count):
            ranks = slice(z * rows, (z + 1) * rows)
            shares_out[z, other, :, width:up_end] = kept_ups[ranks].astype(jnp.bfloat16)
            shares_out[z, other, :, up_end:] = kept_deltas
    for side, pieces in enumerate((mine, theirs)):
        for turn in range(pieces.shape[0]):
            block = feature_block(side, turn)
            downs = ADAPTER_SCALE * first_product(coef, pieces[turn])
            for z in range(z_count):
                ranks = slice(z * rows, (z + 1) * rows)
                shares_out[z, block, :, :width] = downs[ranks].astype(jnp.bfloat16)


def portion_kernel(
    key_change, value_change, coef, key_weight, value_weight, key_down, value_down, keep, give
):
    rank = key_down.shape[0]
    y_count, _, width = keep.shape
    for side, out in enumerate((keep, give)):
        for turn in range(y_count):
            block = feature_block(side, (y_count - turn) % y_count)
            start = pl.multiple_of(block * width, width)
            rows = pl.ds(start, width)
            portion = final_product(key_change[...], key_weight[rows]) + final_product(
                value_change[...], value_weight[rows]
            )
            lows = jnp.dot(
                coef[:, :rank], key_down[:, rows], preferred_element_type=jnp.float32
            ) + jnp.dot(coef[:, rank:], value_down[:, rows], preferred_element_type=jnp.float32)
            out[turn] = (portion + ADAPTER_SCALE * lows).astype(jnp.bfloat16)


def home_kernel(subs, received, loss, *rest):
    pieces, (sums_out, last_out) = rest[:-2], rest[-2:]
    z_count, mp_count, rows, _ = received.shape
    copies, _, sum_width = sums_out.shape
    sum_width = sum_width - loss.shape[1]
    total = None
    deltas = []
    for z in range(z_count):
        column = None
        for other in range(mp_count):
            part = received[z, other].astype(jnp.float32)
            column = part if column is None else column + part
        delta = column[:, sum_width:]
        deltas = deltas + [
            jnp.concatenate([delta[at : at + 1], delta[at + 1 : at + 2]], axis=1)
            for at in range(0, rows, 2)
        ]
        column = column[:, :sum_width]
        total = column if total is None else total + column
    for copy in range(copies):
        sums_out[copy, :, :sum_width] = total
        sums_out[copy, :, sum_width:] = loss[:rows]
    deltas = jnp.concatenate(deltas, axis=0).astype(jnp.bfloat16)
    count = len(pieces)
    lasts = []
    for piece in pieces:
        wq_rows = jnp.concatenate([piece[half, 0] for half in range(piece.shape[0])], axis=0)
        lasts.append(final_product(deltas, wq_rows))
    for choice in range(count):
        turn = lax.rem(lax.axis_index("x") + (count - choice), count)
        block = jnp.zeros(lasts[0].shape, jnp.float32)
        for candidate in range(count):
            block = block + jnp.where(turn == candidate, lasts[candidate], 0.0)
        width = block.shape[1]
        for z in range(z_count):
            last_out[z, :, choice * width : (choice + 1) * width] = block[
                z * subs : (z + 1) * subs
            ]


def return_kernel(sums, last, chunks_out, loss_out):
    z_count, mp_count, rows, chunk_width = chunks_out.shape
    total = sums[0]
    for part in range(1, sums.shape[0]):
        total = total + sums[part]
    sum_width = total.shape[1] - loss_out.shape[1]
    loss_out[...] = total[:, sum_width:]
    total = total[:, :sum_width].astype(jnp.bfloat16)
    half = chunk_width - sum_width
    for z in range(z_count):
        value = last[z]
        value = jnp.concatenate(
            [
                value[sub : sub + 1, side * half : (side + 1) * half]
                for sub in range(value.shape[0])
                for side in range(value.shape[1] // half)
            ],
            axis=0,
        )
        for other in range(mp_count):
            chunks_out[z, other, :, :sum_width] = total
            chunks_out[z, other, :, sum_width:] = jnp.where(
                lax.axis_index("z") == other, value, 0.0
            ).astype(jnp.bfloat16)


def local(
    query_emb,
    item_emb,
    pair_index,
    hard_index,
    hidden_in,
    lengths,
    w_query,
    key_weight_matrix,
    value_weight_matrix,
    w_out,
    key_down_matrix,
    key_up_matrix,
    value_down,
    value_up_matrix,
):
    bf16, f32 = jnp.bfloat16, jnp.float32
    x_count = lax.axis_size("x")
    z_count = lax.axis_size("z")
    plane_count = lax.axis_size(PLANE)
    dp_count = z_count * plane_count
    y_count = lax.axis_size("y")
    mp_count = lax.axis_size(MP)
    local_rows = query_emb.shape[0]
    batch_size = local_rows * dp_count
    feature_width = query_emb.shape[1]
    sub_count = hidden_in.shape[0]
    seq_len = hidden_in.shape[2]
    token_count = sub_count * seq_len
    model_width = feature_width * mp_count
    seq_lengths = lengths[:, 0]
    last_rows = jnp.arange(sub_count, dtype=jnp.int32) * seq_len + seq_lengths - 1

    lower = lax.axis_index("h") == 0

    def pair_up(block):
        other = lax.ppermute(block, "h", [(0, 1), (1, 0)])
        return jnp.stack([jnp.where(lower, block, other), jnp.where(lower, other, block)])

    both = pair_up(jnp.stack([w_query, w_out.T]))
    pair_rows = 2 * local_rows
    emb_pair = spread(jnp.concatenate([item_emb, query_emb], axis=0), ("h",) + MP)
    emb_pair = emb_pair.reshape(2, mp_count, pair_rows, feature_width)
    item_pair = lax.dynamic_index_in_dim(
        emb_pair[:, :, :local_rows], lax.axis_index(MP), 1, keepdims=False
    ).reshape(pair_rows, feature_width)

    query_slices = (
        emb_pair[:, :, local_rows:].transpose(1, 0, 2, 3).reshape(mp_count, pair_rows, -1)
    )
    own_tokens = hidden_in.reshape(token_count, feature_width)
    both, own_tokens, query_slices = lax.optimization_barrier((both, own_tokens, query_slices))
    chunks = jnp.concatenate(
        [jnp.broadcast_to(item_pair[None], query_slices.shape), query_slices], axis=1
    )
    chunks = jnp.broadcast_to(chunks[:, None], (z_count, x_count) + chunks.shape[1:])
    received = swap(chunks.reshape((z_count * x_count,) + chunks.shape[2:]), ("z", "x"))
    queries_all = received[:, pair_rows:].reshape(batch_size, feature_width)
    items_all = (
        received[:, :pair_rows]
        .reshape(z_count, plane_count, local_rows, feature_width)
        .transpose(1, 0, 2, 3)
        .reshape(batch_size, feature_width)
    )
    partial_scores = final_product(query_emb, items_all)
    score_parts = spread(partial_scores, MP)

    query_width = w_query.shape[1]
    def around(block, axis, turn):
        count = lax.axis_size(axis)
        return lax.ppermute(block, axis, [(a, (a + turn) % count) for a in range(count)])

    pieces = [both] + [around(both, "x", turn) for turn in range(1, x_count)]

    mine = jnp.stack(
        [own_tokens] + [around(own_tokens, "y", turn) for turn in range(1, y_count)]
    )
    theirs = around(mine, "c", 1)

    last_tokens = jnp.concatenate(
        [
            lax.dynamic_slice_in_dim(side, last_rows[sub], 1, 1)
            for side in (mine, theirs)
            for sub in range(sub_count)
        ],
        axis=1,
    )
    last_slices = (
        last_tokens.reshape(y_count, 2, sub_count, x_count, feature_width // x_count)
        .transpose(1, 0, 3, 2, 4)
        .reshape(mp_count, x_count * sub_count, feature_width // x_count)
    )

    chunks, residual, loss_part = call(
        functools.partial(residual_kernel, z_count, plane_count),
        (
            jax.ShapeDtypeStruct((dp_count, local_rows, 2 * LANES), bf16),
            jax.ShapeDtypeStruct((local_rows, batch_size), bf16),
            jax.ShapeDtypeStruct((local_rows, LANES), f32),
        ),
        2**24,
    )(score_parts, hard_index.T, pair_index[None], last_slices)
    column_rows = swap(chunks, DP).reshape(batch_size, 2 * LANES)
    adapter_rank = key_down_matrix.shape[1]
    up_width = key_up_matrix.shape[1]
    mine, theirs, residual = lax.optimization_barrier((mine, theirs, residual))
    low_shape = jax.ShapeDtypeStruct((token_count, adapter_rank), bf16)
    head_shape = jax.ShapeDtypeStruct((token_count, up_width), bf16)
    low_key, low_value, key_rows, value_rows = call(
        token_kernel, (low_shape, low_shape, head_shape, head_shape), 2**30
    )(
        mine,
        theirs,
        key_weight_matrix,
        value_weight_matrix,
        key_down_matrix.T,
        value_down.T,
        key_up_matrix,
        value_up_matrix,
    )
    column_rows, key_rows, value_rows = lax.optimization_barrier(
        (column_rows, key_rows, value_rows)
    )
    column_grads, parts = call(
        functools.partial(gradient_kernel, z_count, sub_count),
        (
            jax.ShapeDtypeStruct((z_count * local_rows, feature_width), bf16),
            jax.ShapeDtypeStruct((z_count, 2 * sub_count, query_width + LANES), f32),
        ),
        2**26,
    )(column_rows, queries_all, loss_part, *pieces)
    parts = swap(parts, "z")
    own_grads = lax.dynamic_index_in_dim(
        column_grads.reshape(z_count, local_rows, feature_width),
        lax.axis_index(MP),
        0,
        keepdims=False,
    )
    item_grad = lax.ppermute(
        own_grads,
        ("z",) + MP,
        [(a * mp_count + b, b * mp_count + a) for a in range(z_count) for b in range(mp_count)],
    )
    query_grad = (jnp.dot(residual, items_all, preferred_element_type=f32) * INV_TEMP).astype(bf16)

    share_rows = 2 * adapter_rank // z_count
    sum_width = feature_width + up_width
    chunk_width = sum_width + sub_count * query_width // share_rows
    key_change, value_change, coef, loss_part, shares = call(
        attention_kernel,
        (
            head_shape,
            head_shape,
            jax.ShapeDtypeStruct((token_count, 2 * adapter_rank), bf16),
            jax.ShapeDtypeStruct((2 * sub_count, LANES), f32),
            jax.ShapeDtypeStruct((z_count, mp_count, share_rows, chunk_width), bf16),
        ),
        2**26,
    )(
        lengths.T,
        parts,
        key_rows,
        value_rows,
        key_up_matrix,
        value_up_matrix,
        low_key,
        low_value,
        mine,
        theirs,
    )
    grid_shape = shares.shape
    shares = swap(shares.reshape((-1,) + grid_shape[2:]), ("z",) + MP).reshape(grid_shape)

    block_shape = jax.ShapeDtypeStruct((y_count, token_count, feature_width), bf16)
    keep, give = call(portion_kernel, (block_shape, block_shape), 2**30)(
        key_change,
        value_change,
        coef,
        key_weight_matrix,
        value_weight_matrix,
        key_down_matrix.T,
        value_down.T,
    )
    shares, got = lax.optimization_barrier((shares, around(give, "c", 1)))
    pair_sum = keep.astype(f32) + got.astype(f32)
    input_sum = pair_sum[0]
    pair_sum = pair_sum.astype(bf16)

    sums, last_part = call(
        functools.partial(home_kernel, sub_count),
        (
            jax.ShapeDtypeStruct((plane_count, share_rows, sum_width + LANES), f32),
            jax.ShapeDtypeStruct((z_count, sub_count, feature_width), f32),
        ),
        2**24,
    )(shares, loss_part, *pieces)
    arrived = [around(pair_sum[turn], "y", turn) for turn in range(1, y_count)]
    sums, arrived[1] = lax.optimization_barrier((swap(sums, PLANE), arrived[1]))
    for block in arrived:
        input_sum = input_sum + block.astype(f32)
    chunks, loss_sum = call(
        return_kernel,
        (
            jax.ShapeDtypeStruct(grid_shape, bf16),
            jax.ShapeDtypeStruct((share_rows, LANES), f32),
        ),
        2**24,
    )(sums, last_part)
    mean_loss = loss_sum[0, 0] / batch_size
    summed = swap(chunks.reshape((-1,) + grid_shape[2:]), ("z",) + MP).reshape(grid_shape)
    own = lax.axis_index(MP)
    up_grad = lax.dynamic_index_in_dim(
        summed[:, :, :, feature_width:sum_width], own, 1, keepdims=False
    )
    up_grad = up_grad.reshape(2 * adapter_rank, up_width).astype(f32)
    last_rows_grad = jnp.sum(
        lax.dynamic_index_in_dim(
            summed[:, :, :, sum_width:], own, 0, keepdims=False
        ).astype(f32),
        axis=0,
    ).reshape(sub_count, feature_width) + item_grad[:sub_count].astype(f32)
    row_ids = jnp.arange(token_count, dtype=jnp.int32)[:, None]
    for sub in range(sub_count):
        input_sum = input_sum + jnp.where(
            row_ids == last_rows[sub], last_rows_grad[sub][None, :], 0.0
        )
    input_grad = input_sum.astype(bf16).reshape(hidden_in.shape)
    down_grad = (
        summed[:, :, :, :feature_width]
        .transpose(0, 2, 1, 3)
        .reshape(2 * adapter_rank, model_width)
        .astype(f32)
        .T
    )
    return (
        mean_loss,
        query_grad,
        item_grad,
        input_grad,
        down_grad[:, :adapter_rank],
        down_grad[:, adapter_rank:],
        up_grad[:adapter_rank],
        up_grad[adapter_rank:],
    )


def solution(mesh):
    fine = Mesh(mesh.devices.reshape(8, 4, 2, 4, 2), DP + MP)
    in_specs = (
        P(DP, MP),
        P(DP, MP),
        P(DP),
        P(DP, None),
        P(None, DP, None, MP),
        P(None, DP),
        P(DP, MP),
        P(None, MP),
        P(None, MP),
        P(MP, DP),
        P(),
        P(None, MP),
        P(),
        P(None, MP),
    )
    out_specs = (
        P(),
        P(DP, MP),
        P(DP, MP),
        P(None, DP, None, MP),
        P(),
        P(),
        P(None, MP),
        P(None, MP),
    )
    return jax.shard_map(local, mesh=fine, in_specs=in_specs, out_specs=out_specs, check_vma=False)
```

```python
import functools
import math

import jax
import jax.numpy as jnp
from jax import lax
from jax.experimental import pallas as pl
from jax.experimental.pallas import tpu as pltpu
from jax.sharding import Mesh
from jax.sharding import PartitionSpec as P

HEADS = 32
KV_HEADS = 8
HEAD_DIM = 128
LANES = 128

INV_TEMP = 50.0
HARD_NEGATIVE_ADD = 4.0
ADAPTER_SCALE = 2.0

PLANE = ("x", "h")
DP = ("z", "x", "h")


def final_product(left_side, right_side):
    return lax.dot_general(
        left_side, right_side, (((1,), (1,)), ((), ())), preferred_element_type=jnp.float32
    )


def first_product(left_side, right_side):
    return lax.dot_general(
        left_side, right_side, (((0,), (0,)), ((), ())), preferred_element_type=jnp.float32
    )


def spread(block, axes):
    count = lax.axis_size(axes)
    copies = jnp.broadcast_to(block[None], (count,) + block.shape)
    return lax.all_to_all(copies, axes, split_axis=0, concat_axis=0, tiled=True)


def swap(blocks, axes):
    return lax.all_to_all(blocks, axes, split_axis=0, concat_axis=0, tiled=True)


def call(kernel, out_shape, flops, **layout):
    return pl.pallas_call(
        kernel,
        out_shape=out_shape,
        compiler_params=pltpu.CompilerParams(vmem_limit_bytes=56 * 1024 * 1024),
        cost_estimate=pl.CostEstimate(flops=flops, bytes_accessed=2**20, transcendentals=4096),
        **layout,
    )


def upright(line):
    count = line.shape[1]
    row = lax.broadcasted_iota(jnp.int32, (count, count), 0)
    column = lax.broadcasted_iota(jnp.int32, (count, count), 1)
    return jnp.sum(jnp.where(row == column, line, 0), axis=1, keepdims=True)


def residual_kernel(
    z_count, plane_count, parts, hard, pair, tokens, chunks, residual_out, loss_out
):
    rows = parts.shape[1]
    batch_size = parts.shape[2]
    pair_scores = parts[0]
    for part in range(1, parts.shape[0]):
        pair_scores = pair_scores + parts[part]
    column = lax.broadcasted_iota(jnp.int32, (rows, batch_size), 1)
    inner = column % rows
    outer = column // rows
    item = ((outer % z_count) * plane_count + outer // z_count) * rows + inner
    count = jnp.zeros((rows, batch_size), jnp.float32)
    for choice in range(hard.shape[0]):
        count = count + jnp.where(upright(hard[choice : choice + 1]) == item, 1.0, 0.0)
    logits = pair_scores * INV_TEMP + HARD_NEGATIVE_ADD * count
    top = jnp.max(logits, axis=1, keepdims=True)
    log_total = top + jnp.log(jnp.sum(jnp.exp(logits - top), axis=1, keepdims=True))
    target = jnp.where(upright(pair[...]) == item, 1.0, 0.0)
    picked = jnp.sum(target * logits, axis=1, keepdims=True)
    loss = jnp.sum(log_total - picked, axis=0, keepdims=True)
    loss_out[...] = jnp.broadcast_to(loss, loss_out.shape)
    residual = jnp.exp(logits - log_total) - target
    residual_out[...] = residual.astype(jnp.bfloat16)
    width = z_count * rows
    pad = jnp.zeros((rows, LANES - width), jnp.float32)
    for plane in range(plane_count):
        block = jnp.concatenate([residual[:, plane * width : (plane + 1) * width], pad], axis=1)
        block = block.astype(jnp.bfloat16)
        for z in range(z_count):
            chunks[z * plane_count + plane, :, :LANES] = block
            chunks[z * plane_count + plane, :, LANES:] = tokens[z]


def token_kernel(tokens, key_weight, value_weight, down, key_up, value_up, low, keys, values):
    rank = key_up.shape[0]
    lows = jnp.dot(tokens[...], down[...], preferred_element_type=jnp.float32)
    lows = lows.astype(jnp.bfloat16)
    low[...] = lows
    for side, (weight, up, out) in enumerate(
        ((key_weight, key_up, keys), (value_weight, value_up, values))
    ):
        base = jnp.dot(tokens[...], weight[...], preferred_element_type=jnp.float32)
        mine = lows[:, side * rank : (side + 1) * rank]
        rise = jnp.dot(mine, up[...], preferred_element_type=jnp.float32)
        out[...] = (base + ADAPTER_SCALE * rise).astype(jnp.bfloat16)


def gradient_kernel(
    z_count, subs, received, queries, loss, wq_plane, wo_plane, item_out, parts_out
):
    item_rows = item_out.shape[0]
    width = received.shape[1] - LANES
    count = queries.shape[1] // width
    every = lax.dot_general(
        received[:, :LANES],
        queries[...],
        (((0,), (0,)), ((), ())),
        preferred_element_type=jnp.float32,
    )
    grads = (every[:item_rows] * INV_TEMP).astype(jnp.bfloat16)
    item_out[...] = grads
    picks = subs * z_count
    row = lax.broadcasted_iota(jnp.int32, (picks, item_rows), 0)
    column = lax.broadcasted_iota(jnp.int32, (picks, item_rows), 1)
    per_z = item_rows // z_count
    wanted = jnp.where((row // subs) * per_z + row % subs == column, 1.0, 0.0)
    cotangents = jnp.dot(
        wanted.astype(jnp.bfloat16), grads, preferred_element_type=jnp.float32
    )
    senders = received.shape[0] // per_z
    planes = senders // z_count
    row = lax.broadcasted_iota(jnp.int32, (picks, received.shape[0]), 0)
    column = lax.broadcasted_iota(jnp.int32, (picks, received.shape[0]), 1)
    plane = lax.axis_index(PLANE)
    first = ((row // subs) * planes + plane) * per_z + row % subs
    attn = query = None
    for block in range(count):
        cot = cotangents[:, block * width : (block + 1) * width]
        chosen = jnp.where(first + block * subs == column, 1.0, 0.0).astype(jnp.bfloat16)
        token = jnp.dot(chosen, received[:, LANES:], preferred_element_type=jnp.float32)
        rows = slice(block * width, (block + 1) * width)
        wq_rows, wo_rows = wq_plane[rows], wo_plane[rows]
        attn_term = jnp.dot(cot.astype(jnp.bfloat16), wo_rows, preferred_element_type=jnp.float32)
        query_term = jnp.dot(
            token.astype(jnp.bfloat16), wq_rows, preferred_element_type=jnp.float32
        )
        attn = attn_term if attn is None else attn + attn_term
        query = query_term if query is None else query + query_term
    end = attn.shape[1]
    for z in range(z_count):
        parts_out[z, :subs, :end] = attn[z * subs : (z + 1) * subs]
        parts_out[z, subs:, :end] = query[z * subs : (z + 1) * subs]
        parts_out[z, :, end:] = loss[: 2 * subs]


def attention_kernel(
    lengths,
    parts,
    keys,
    values,
    key_up,
    value_up,
    reduced,
    tokens,
    key_change_out,
    value_change_out,
    coef_out,
    loss_out,
    shares_out,
):
    subs = parts.shape[1] // 2
    token_count = keys.shape[0]
    seq_len = token_count // subs
    group = parts.shape[2] // HEAD_DIM - 1
    total = parts[0]
    for part in range(1, parts.shape[0]):
        total = total + parts[part]
    loss_out[...] = total[:, group * HEAD_DIM :]
    both = total.astype(jnp.bfloat16).astype(jnp.float32)

    def heads(first):
        return jnp.concatenate(
            [
                both[first + sub : first + sub + 1, head * HEAD_DIM : (head + 1) * HEAD_DIM]
                for sub in range(subs)
                for head in range(group)
            ],
            axis=0,
        )

    grad_heads = heads(0)
    q_heads = heads(subs)
    score_scale = 1.0 / math.sqrt(HEAD_DIM)
    raw = final_product(q_heads.astype(jnp.bfloat16), keys[...]) * score_scale
    row_sub = lax.broadcasted_iota(jnp.int32, raw.shape, 0) // group
    token = lax.broadcasted_iota(jnp.int32, raw.shape, 1)
    live = jnp.zeros(raw.shape, jnp.bool_)
    for sub in range(subs):
        first = sub * seq_len
        inside = (token >= first) & (token < first + lengths[0, sub])
        live = live | (inside & (row_sub == sub))
    raw = jnp.where(live, raw, -jnp.inf)
    weights = jnp.exp(raw - jnp.max(raw, axis=1, keepdims=True))
    probs = weights / jnp.sum(weights, axis=1, keepdims=True)
    prob_half = probs.astype(jnp.bfloat16).astype(jnp.float32)
    prob_grad = final_product(grad_heads.astype(jnp.bfloat16), values[...])
    score_grad = (
        probs * (prob_grad - jnp.sum(probs * prob_grad, axis=1, keepdims=True)) * score_scale
    )
    score_grad = score_grad.astype(jnp.bfloat16)
    delta = jnp.dot(score_grad, keys[...], preferred_element_type=jnp.float32)
    score_grad = score_grad.astype(jnp.float32)
    key_change = first_product(score_grad, q_heads).astype(jnp.bfloat16)
    value_change = first_product(prob_half, grad_heads).astype(jnp.bfloat16)
    key_coef = final_product(key_change, key_up[...])
    value_coef = final_product(value_change, value_up[...])
    coef = jnp.concatenate([key_coef, value_coef], axis=1).astype(jnp.bfloat16)
    key_change_out[...] = key_change
    value_change_out[...] = value_change
    coef_out[...] = coef
    rank = key_up.shape[0]
    ups = ADAPTER_SCALE * jnp.concatenate(
        [
            first_product(reduced[...], key_change)[:rank],
            first_product(reduced[...], value_change)[rank:],
        ],
        axis=0,
    )
    downs = ADAPTER_SCALE * first_product(coef, tokens[...])
    z_count, mp_count, rows, chunk_width = shares_out.shape
    width = downs.shape[1] // mp_count
    up_end = width + ups.shape[1]
    deltas = jnp.concatenate(
        [
            jnp.concatenate(
                [delta[at : at + 1], delta[at + 1 : at + 2]], axis=1
            )
            for at in range(0, subs * group, 2)
        ],
        axis=0,
    )
    for other in range(mp_count):
        mine = lax.axis_index("mp") == other
        kept_ups = jnp.where(mine, ups, 0.0)
        kept_deltas = jnp.where(mine, deltas, 0.0).astype(jnp.bfloat16)
        for z in range(z_count):
            ranks = slice(z * rows, (z + 1) * rows)
            shares_out[z, other, :, :width] = downs[
                ranks, other * width : (other + 1) * width
            ].astype(jnp.bfloat16)
            shares_out[z, other, :, width:up_end] = kept_ups[ranks].astype(jnp.bfloat16)
            shares_out[z, other, :, up_end:] = kept_deltas

def portion_kernel(key_change, value_change, coef, key_weight, value_weight, down, out):
    width = 4 * LANES
    for start in range(0, out.shape[1], width):
        features = slice(start, start + width)
        portion = final_product(key_change[...], key_weight[features]) + final_product(
            value_change[...], value_weight[features]
        )
        portion = portion + ADAPTER_SCALE * jnp.dot(
            coef[...], down[:, features], preferred_element_type=jnp.float32
        )
        out[:, features] = portion.astype(jnp.bfloat16)


def home_kernel(subs, received, loss, wq_plane, sums_out, last_out):
    z_count, mp_count, rows, _ = received.shape
    copies, _, sum_width = sums_out.shape
    sum_width = sum_width - loss.shape[1]
    total = None
    deltas = []
    for z in range(z_count):
        column = None
        for other in range(mp_count):
            part = received[z, other].astype(jnp.float32)
            column = part if column is None else column + part
        delta = column[:, sum_width:]
        deltas = deltas + [
            jnp.concatenate([delta[at : at + 1], delta[at + 1 : at + 2]], axis=1)
            for at in range(0, rows, 2)
        ]
        column = column[:, :sum_width]
        total = column if total is None else total + column
    for copy in range(copies):
        sums_out[copy, :, :sum_width] = total
        sums_out[copy, :, sum_width:] = loss[:rows]
    deltas = jnp.concatenate(deltas, axis=0).astype(jnp.bfloat16)
    last = final_product(deltas, wq_plane[...])
    for z in range(z_count):
        last_out[z] = last[z * subs : (z + 1) * subs]


def return_kernel(sums, last, chunks_out, loss_out):
    z_count, mp_count, rows, chunk_width = chunks_out.shape
    total = sums[0]
    for part in range(1, sums.shape[0]):
        total = total + sums[part]
    sum_width = total.shape[1] - loss_out.shape[1]
    loss_out[...] = total[:, sum_width:]
    total = total[:, :sum_width].astype(jnp.bfloat16)
    half = chunk_width - sum_width
    for z in range(z_count):
        value = last[z]
        value = jnp.concatenate(
            [
                value[sub : sub + 1, side * half : (side + 1) * half]
                for sub in range(value.shape[0])
                for side in range(value.shape[1] // half)
            ],
            axis=0,
        )
        for other in range(mp_count):
            chunks_out[z, other, :, :sum_width] = total
            chunks_out[z, other, :, sum_width:] = jnp.where(
                lax.axis_index("z") == other, value, 0.0
            ).astype(jnp.bfloat16)


def local(
    query_emb,
    item_emb,
    pair_index,
    hard_index,
    hidden_in,
    lengths,
    w_query,
    key_weight_matrix,
    value_weight_matrix,
    w_out,
    key_down_matrix,
    key_up_matrix,
    value_down,
    value_up_matrix,
):
    bf16, f32 = jnp.bfloat16, jnp.float32
    x_count = lax.axis_size("x")
    z_count = lax.axis_size("z")
    plane_count = lax.axis_size(PLANE)
    dp_count = z_count * plane_count
    mp_count = lax.axis_size("mp")
    local_rows = query_emb.shape[0]
    batch_size = local_rows * dp_count
    feature_width = query_emb.shape[1]
    sub_count = hidden_in.shape[0]
    seq_len = hidden_in.shape[2]
    token_count = sub_count * seq_len
    full_rows = lax.all_gather(hidden_in, "mp", axis=3, tiled=True)
    model_width = full_rows.shape[3]
    token_inputs = full_rows.reshape(token_count, model_width)
    seq_lengths = lengths[:, 0]
    last_rows = jnp.arange(sub_count, dtype=jnp.int32) * seq_len + seq_lengths - 1

    lower = lax.axis_index("h") == 0

    def pair_up(block):
        other = lax.ppermute(block, "h", [(0, 1), (1, 0)])
        return jnp.stack([jnp.where(lower, block, other), jnp.where(lower, other, block)])

    both = pair_up(jnp.stack([w_query, w_out.T]))

    pair_rows = 2 * local_rows
    emb_pair = spread(jnp.concatenate([item_emb, query_emb], axis=0), ("h", "mp"))
    emb_pair = emb_pair.reshape(2, mp_count, pair_rows, feature_width)
    item_pair = lax.dynamic_index_in_dim(
        emb_pair[:, :, :local_rows], lax.axis_index("mp"), 1, keepdims=False
    ).reshape(pair_rows, feature_width)

    query_slices = (
        emb_pair[:, :, local_rows:].transpose(1, 0, 2, 3).reshape(mp_count, pair_rows, -1)
    )
    both, query_slices = lax.optimization_barrier((both, query_slices))
    chunks = jnp.concatenate(
        [jnp.broadcast_to(item_pair[None], query_slices.shape), query_slices], axis=1
    )
    chunks = jnp.broadcast_to(chunks[:, None], (z_count, x_count) + chunks.shape[1:])
    received = swap(chunks.reshape((z_count * x_count,) + chunks.shape[2:]), ("z", "x"))
    queries_all = received[:, pair_rows:].reshape(batch_size, feature_width)
    items_all = (
        received[:, :pair_rows]
        .reshape(z_count, plane_count, local_rows, feature_width)
        .transpose(1, 0, 2, 3)
        .reshape(batch_size, feature_width)
    )
    partial_scores = final_product(query_emb, items_all)
    score_parts = spread(partial_scores, "mp")

    query_width = w_query.shape[1]
    both = lax.all_gather(both, "x", axis=0, tiled=False)
    plane_shape = (feature_width, query_width)
    wq_plane = both[:, :, 0].reshape(plane_shape)
    wo_plane = both[:, :, 1].reshape(plane_shape)

    last_tokens = jnp.concatenate(
        [
            lax.dynamic_slice_in_dim(token_inputs, last_rows[sub], 1, 0)
            for sub in range(sub_count)
        ],
        axis=0,
    )
    last_slices = (
        last_tokens.reshape(sub_count, z_count, x_count, feature_width // x_count)
        .transpose(1, 2, 0, 3)
        .reshape(z_count, x_count * sub_count, feature_width // x_count)
    )

    chunks, residual, loss_part = call(
        functools.partial(residual_kernel, z_count, plane_count),
        (
            jax.ShapeDtypeStruct((dp_count, local_rows, 2 * LANES), bf16),
            jax.ShapeDtypeStruct((local_rows, batch_size), bf16),
            jax.ShapeDtypeStruct((local_rows, LANES), f32),
        ),
        2**24,
    )(score_parts, hard_index.T, pair_index[None], last_slices)
    column_rows = swap(chunks, DP).reshape(batch_size, 2 * LANES)
    adapter_rank = key_down_matrix.shape[1]
    up_width = key_up_matrix.shape[1]
    down_both = jnp.concatenate([key_down_matrix, value_down], axis=1)
    late_tokens, residual = lax.optimization_barrier((token_inputs, residual))
    head_shape = jax.ShapeDtypeStruct((token_count, up_width), bf16)
    low_shape = jax.ShapeDtypeStruct((token_count, 2 * adapter_rank), bf16)
    reduced_pair, key_rows, value_rows = call(
        token_kernel, (low_shape, head_shape, head_shape), 2**30
    )(
        late_tokens,
        key_weight_matrix,
        value_weight_matrix,
        down_both,
        key_up_matrix,
        value_up_matrix,
    )
    column_rows, key_rows, value_rows = lax.optimization_barrier(
        (column_rows, key_rows, value_rows)
    )
    column_grads, parts = call(
        functools.partial(gradient_kernel, z_count, sub_count),
        (
            jax.ShapeDtypeStruct((z_count * local_rows, feature_width), bf16),
            jax.ShapeDtypeStruct((z_count, 2 * sub_count, query_width + LANES), f32),
        ),
        2**26,
    )(column_rows, queries_all, loss_part, wq_plane, wo_plane)
    parts = swap(parts, "z")
    own_grads = lax.dynamic_index_in_dim(
        column_grads.reshape(z_count, local_rows, feature_width),
        lax.axis_index("mp"),
        0,
        keepdims=False,
    )
    item_grad = lax.ppermute(
        own_grads,
        ("z", "mp"),
        [(a * mp_count + b, b * mp_count + a) for a in range(z_count) for b in range(mp_count)],
    )
    query_grad = (jnp.dot(residual, items_all, preferred_element_type=f32) * INV_TEMP).astype(bf16)

    share_rows = 2 * adapter_rank // z_count
    sum_width = feature_width + up_width
    chunk_width = sum_width + sub_count * query_width // share_rows
    key_change, value_change, coef, loss_part, shares = call(
        attention_kernel,
        (
            head_shape,
            head_shape,
            low_shape,
            jax.ShapeDtypeStruct((2 * sub_count, LANES), f32),
            jax.ShapeDtypeStruct((z_count, mp_count, share_rows, chunk_width), bf16),
        ),
        2**26,
    )(
        lengths.T,
        parts,
        key_rows,
        value_rows,
        key_up_matrix,
        value_up_matrix,
        reduced_pair,
        token_inputs,
    )
    grid_shape = shares.shape
    shares = swap(shares.reshape((-1,) + grid_shape[2:]), ("z", "mp")).reshape(grid_shape)

    portion = call(portion_kernel, jax.ShapeDtypeStruct((token_count, model_width), bf16), 2**30)(
        key_change, value_change, coef, key_weight_matrix, value_weight_matrix, down_both.T
    )
    shares, portion = lax.optimization_barrier((shares, portion))
    input_sum = lax.psum_scatter(portion, "mp", scatter_dimension=1, tiled=True).astype(f32)
    sums, last_part = call(
        functools.partial(home_kernel, sub_count),
        (
            jax.ShapeDtypeStruct((plane_count, share_rows, sum_width + LANES), f32),
            jax.ShapeDtypeStruct((z_count, sub_count, feature_width), f32),
        ),
        2**24,
    )(shares, loss_part, wq_plane)
    chunks, loss_sum = call(
        return_kernel,
        (
            jax.ShapeDtypeStruct(grid_shape, bf16),
            jax.ShapeDtypeStruct((share_rows, LANES), f32),
        ),
        2**24,
    )(swap(sums, PLANE), last_part)
    mean_loss = loss_sum[0, 0] / batch_size
    summed = swap(chunks.reshape((-1,) + grid_shape[2:]), ("z", "mp")).reshape(grid_shape)
    own = lax.axis_index("mp")
    up_grad = lax.dynamic_index_in_dim(
        summed[:, :, :, feature_width:sum_width], own, 1, keepdims=False
    )
    up_grad = up_grad.reshape(2 * adapter_rank, up_width).astype(f32)
    last_rows_grad = jnp.sum(
        lax.dynamic_index_in_dim(
            summed[:, :, :, sum_width:], own, 0, keepdims=False
        ).astype(f32),
        axis=0,
    ).reshape(sub_count, feature_width) + item_grad[:sub_count].astype(f32)
    row_ids = jnp.arange(token_count, dtype=jnp.int32)[:, None]
    for sub in range(sub_count):
        input_sum = input_sum + jnp.where(
            row_ids == last_rows[sub], last_rows_grad[sub][None, :], 0.0
        )
    input_grad = input_sum.astype(bf16).reshape(hidden_in.shape)
    down_grad = (
        summed[:, :, :, :feature_width]
        .transpose(0, 2, 1, 3)
        .reshape(2 * adapter_rank, model_width)
        .astype(f32)
        .T
    )
    return (
        mean_loss,
        query_grad,
        item_grad,
        input_grad,
        down_grad[:, :adapter_rank],
        down_grad[:, adapter_rank:],
        up_grad[:adapter_rank],
        up_grad[adapter_rank:],
    )


def solution(mesh):
    fine = Mesh(
        mesh.devices.reshape(8, 4, 2, mesh.devices.shape[1]), ("z", "x", "h", "mp")
    )
    in_specs = (
        P(DP, "mp"),
        P(DP, "mp"),
        P(DP),
        P(DP, None),
        P(None, DP, None, "mp"),
        P(None, DP),
        P(DP, "mp"),
        P(None, "mp"),
        P(None, "mp"),
        P("mp", DP),
        P(),
        P(None, "mp"),
        P(),
        P(None, "mp"),
    )
    out_specs = (
        P(),
        P(DP, "mp"),
        P(DP, "mp"),
        P(None, DP, None, "mp"),
        P(),
        P(),
        P(None, "mp"),
        P(None, "mp"),
    )
    return jax.shard_map(local, mesh=fine, in_specs=in_specs, out_specs=out_specs, check_vma=False)
```

```python
import functools
import math

import jax
import jax.numpy as jnp
from jax import lax
from jax.experimental import pallas as pl
from jax.experimental.pallas import tpu as pltpu
from jax.sharding import Mesh
from jax.sharding import PartitionSpec as P

HEADS = 32
KV_HEADS = 8
HEAD_DIM = 128
LANES = 128

INV_TEMP = 50.0
HARD_NEGATIVE_ADD = 4.0
ADAPTER_SCALE = 2.0

PLANE = ("x", "h")
DP = ("z", "x", "h")


def final_product(left_side, right_side):
    return lax.dot_general(
        left_side, right_side, (((1,), (1,)), ((), ())), preferred_element_type=jnp.float32
    )


def first_product(left_side, right_side):
    return lax.dot_general(
        left_side, right_side, (((0,), (0,)), ((), ())), preferred_element_type=jnp.float32
    )


def spread(block, axes):
    count = lax.axis_size(axes)
    copies = jnp.broadcast_to(block[None], (count,) + block.shape)
    return lax.all_to_all(copies, axes, split_axis=0, concat_axis=0, tiled=True)


def swap(blocks, axes):
    return lax.all_to_all(blocks, axes, split_axis=0, concat_axis=0, tiled=True)


def call(kernel, out_shape, flops, **layout):
    return pl.pallas_call(
        kernel,
        out_shape=out_shape,
        compiler_params=pltpu.CompilerParams(vmem_limit_bytes=56 * 1024 * 1024),
        cost_estimate=pl.CostEstimate(flops=flops, bytes_accessed=2**20, transcendentals=4096),
        **layout,
    )


def upright(line):
    count = line.shape[1]
    row = lax.broadcasted_iota(jnp.int32, (count, count), 0)
    column = lax.broadcasted_iota(jnp.int32, (count, count), 1)
    return jnp.sum(jnp.where(row == column, line, 0), axis=1, keepdims=True)


def residual_kernel(
    z_count, plane_count, parts, hard, pair, tokens, chunks, residual_out, loss_out
):
    rows = parts.shape[1]
    batch_size = parts.shape[2]
    pair_scores = parts[0]
    for part in range(1, parts.shape[0]):
        pair_scores = pair_scores + parts[part]
    column = lax.broadcasted_iota(jnp.int32, (rows, batch_size), 1)
    inner = column % rows
    outer = column // rows
    item = ((outer % z_count) * plane_count + outer // z_count) * rows + inner
    count = jnp.zeros((rows, batch_size), jnp.float32)
    for choice in range(hard.shape[0]):
        count = count + jnp.where(upright(hard[choice : choice + 1]) == item, 1.0, 0.0)
    logits = pair_scores * INV_TEMP + HARD_NEGATIVE_ADD * count
    top = jnp.max(logits, axis=1, keepdims=True)
    log_total = top + jnp.log(jnp.sum(jnp.exp(logits - top), axis=1, keepdims=True))
    target = jnp.where(upright(pair[...]) == item, 1.0, 0.0)
    picked = jnp.sum(target * logits, axis=1, keepdims=True)
    loss = jnp.sum(log_total - picked, axis=0, keepdims=True)
    loss_out[...] = jnp.broadcast_to(loss, loss_out.shape)
    residual = jnp.exp(logits - log_total) - target
    residual_out[...] = residual.astype(jnp.bfloat16)
    width = z_count * rows
    pad = jnp.zeros((rows, LANES - width), jnp.float32)
    for plane in range(plane_count):
        block = jnp.concatenate([residual[:, plane * width : (plane + 1) * width], pad], axis=1)
        block = block.astype(jnp.bfloat16)
        for z in range(z_count):
            chunks[z * plane_count + plane, :, :LANES] = block
            chunks[z * plane_count + plane, :, LANES:] = tokens[z]


def token_kernel(tokens, key_weight, value_weight, down, key_up, value_up, low, keys, values):
    rank = key_up.shape[0]
    lows = jnp.dot(tokens[...], down[...], preferred_element_type=jnp.float32)
    lows = lows.astype(jnp.bfloat16)
    low[...] = lows
    for side, (weight, up, out) in enumerate(
        ((key_weight, key_up, keys), (value_weight, value_up, values))
    ):
        base = jnp.dot(tokens[...], weight[...], preferred_element_type=jnp.float32)
        mine = lows[:, side * rank : (side + 1) * rank]
        rise = jnp.dot(mine, up[...], preferred_element_type=jnp.float32)
        out[...] = (base + ADAPTER_SCALE * rise).astype(jnp.bfloat16)


def gradient_kernel(
    z_count, subs, received, queries, loss, wq_plane, wo_plane, item_out, parts_out
):
    item_rows = item_out.shape[0]
    width = received.shape[1] - LANES
    count = queries.shape[1] // width
    every = lax.dot_general(
        received[:, :LANES],
        queries[...],
        (((0,), (0,)), ((), ())),
        preferred_element_type=jnp.float32,
    )
    grads = (every[:item_rows] * INV_TEMP).astype(jnp.bfloat16)
    item_out[...] = grads
    picks = subs * z_count
    row = lax.broadcasted_iota(jnp.int32, (picks, item_rows), 0)
    column = lax.broadcasted_iota(jnp.int32, (picks, item_rows), 1)
    per_z = item_rows // z_count
    wanted = jnp.where((row // subs) * per_z + row % subs == column, 1.0, 0.0)
    cotangents = jnp.dot(
        wanted.astype(jnp.bfloat16), grads, preferred_element_type=jnp.float32
    )
    senders = received.shape[0] // per_z
    planes = senders // z_count
    row = lax.broadcasted_iota(jnp.int32, (picks, received.shape[0]), 0)
    column = lax.broadcasted_iota(jnp.int32, (picks, received.shape[0]), 1)
    plane = lax.axis_index(PLANE)
    first = ((row // subs) * planes + plane) * per_z + row % subs
    attn = query = None
    for block in range(count):
        cot = cotangents[:, block * width : (block + 1) * width]
        chosen = jnp.where(first + block * subs == column, 1.0, 0.0).astype(jnp.bfloat16)
        token = jnp.dot(chosen, received[:, LANES:], preferred_element_type=jnp.float32)
        rows = slice(block * width, (block + 1) * width)
        wq_rows, wo_rows = wq_plane[rows], wo_plane[rows]
        attn_term = jnp.dot(cot.astype(jnp.bfloat16), wo_rows, preferred_element_type=jnp.float32)
        query_term = jnp.dot(
            token.astype(jnp.bfloat16), wq_rows, preferred_element_type=jnp.float32
        )
        attn = attn_term if attn is None else attn + attn_term
        query = query_term if query is None else query + query_term
    end = attn.shape[1]
    for z in range(z_count):
        parts_out[z, :subs, :end] = attn[z * subs : (z + 1) * subs]
        parts_out[z, subs:, :end] = query[z * subs : (z + 1) * subs]
        parts_out[z, :, end:] = loss[: 2 * subs]


def attention_kernel(
    lengths,
    parts,
    keys,
    values,
    key_up,
    value_up,
    reduced,
    tokens,
    key_change_out,
    value_change_out,
    coef_out,
    loss_out,
    shares_out,
):
    subs = parts.shape[1] // 2
    token_count = keys.shape[0]
    seq_len = token_count // subs
    group = parts.shape[2] // HEAD_DIM - 1
    total = parts[0]
    for part in range(1, parts.shape[0]):
        total = total + parts[part]
    loss_out[...] = total[:, group * HEAD_DIM :]
    both = total.astype(jnp.bfloat16).astype(jnp.float32)

    def heads(first):
        return jnp.concatenate(
            [
                both[first + sub : first + sub + 1, head * HEAD_DIM : (head + 1) * HEAD_DIM]
                for sub in range(subs)
                for head in range(group)
            ],
            axis=0,
        )

    grad_heads = heads(0)
    q_heads = heads(subs)
    score_scale = 1.0 / math.sqrt(HEAD_DIM)
    raw = final_product(q_heads.astype(jnp.bfloat16), keys[...]) * score_scale
    row_sub = lax.broadcasted_iota(jnp.int32, raw.shape, 0) // group
    token = lax.broadcasted_iota(jnp.int32, raw.shape, 1)
    live = jnp.zeros(raw.shape, jnp.bool_)
    for sub in range(subs):
        first = sub * seq_len
        inside = (token >= first) & (token < first + lengths[0, sub])
        live = live | (inside & (row_sub == sub))
    raw = jnp.where(live, raw, -jnp.inf)
    weights = jnp.exp(raw - jnp.max(raw, axis=1, keepdims=True))
    probs = weights / jnp.sum(weights, axis=1, keepdims=True)
    prob_half = probs.astype(jnp.bfloat16).astype(jnp.float32)
    prob_grad = final_product(grad_heads.astype(jnp.bfloat16), values[...])
    score_grad = (
        probs * (prob_grad - jnp.sum(probs * prob_grad, axis=1, keepdims=True)) * score_scale
    )
    score_grad = score_grad.astype(jnp.bfloat16)
    delta = jnp.dot(score_grad, keys[...], preferred_element_type=jnp.float32)
    score_grad = score_grad.astype(jnp.float32)
    key_change = first_product(score_grad, q_heads).astype(jnp.bfloat16)
    value_change = first_product(prob_half, grad_heads).astype(jnp.bfloat16)
    key_coef = final_product(key_change, key_up[...])
    value_coef = final_product(value_change, value_up[...])
    coef = jnp.concatenate([key_coef, value_coef], axis=1).astype(jnp.bfloat16)
    key_change_out[...] = key_change
    value_change_out[...] = value_change
    coef_out[...] = coef
    rank = key_up.shape[0]
    ups = ADAPTER_SCALE * jnp.concatenate(
        [
            first_product(reduced[...], key_change)[:rank],
            first_product(reduced[...], value_change)[rank:],
        ],
        axis=0,
    )
    downs = ADAPTER_SCALE * first_product(coef, tokens[...])
    z_count, mp_count, rows, chunk_width = shares_out.shape
    width = downs.shape[1] // mp_count
    up_end = width + ups.shape[1]
    deltas = jnp.concatenate(
        [
            jnp.concatenate(
                [delta[at : at + 1], delta[at + 1 : at + 2]], axis=1
            )
            for at in range(0, subs * group, 2)
        ],
        axis=0,
    )
    for other in range(mp_count):
        mine = lax.axis_index("mp") == other
        kept_ups = jnp.where(mine, ups, 0.0)
        kept_deltas = jnp.where(mine, deltas, 0.0).astype(jnp.bfloat16)
        for z in range(z_count):
            ranks = slice(z * rows, (z + 1) * rows)
            shares_out[z, other, :, :width] = downs[
                ranks, other * width : (other + 1) * width
            ].astype(jnp.bfloat16)
            shares_out[z, other, :, width:up_end] = kept_ups[ranks].astype(jnp.bfloat16)
            shares_out[z, other, :, up_end:] = kept_deltas

def portion_kernel(key_change, value_change, coef, key_weight, value_weight, down, out):
    width = 4 * LANES
    for start in range(0, out.shape[1], width):
        features = slice(start, start + width)
        portion = final_product(key_change[...], key_weight[features]) + final_product(
            value_change[...], value_weight[features]
        )
        portion = portion + ADAPTER_SCALE * jnp.dot(
            coef[...], down[:, features], preferred_element_type=jnp.float32
        )
        out[:, features] = portion.astype(jnp.bfloat16)


def home_kernel(subs, received, loss, wq_plane, sums_out, last_out):
    z_count, mp_count, rows, _ = received.shape
    copies, _, sum_width = sums_out.shape
    sum_width = sum_width - loss.shape[1]
    total = None
    deltas = []
    for z in range(z_count):
        column = None
        for other in range(mp_count):
            part = received[z, other].astype(jnp.float32)
            column = part if column is None else column + part
        delta = column[:, sum_width:]
        deltas = deltas + [
            jnp.concatenate([delta[at : at + 1], delta[at + 1 : at + 2]], axis=1)
            for at in range(0, rows, 2)
        ]
        column = column[:, :sum_width]
        total = column if total is None else total + column
    for copy in range(copies):
        sums_out[copy, :, :sum_width] = total
        sums_out[copy, :, sum_width:] = loss[:rows]
    deltas = jnp.concatenate(deltas, axis=0).astype(jnp.bfloat16)
    last = final_product(deltas, wq_plane[...])
    for z in range(z_count):
        last_out[z] = last[z * subs : (z + 1) * subs]


def return_kernel(sums, last, chunks_out, loss_out):
    z_count, mp_count, rows, chunk_width = chunks_out.shape
    total = sums[0]
    for part in range(1, sums.shape[0]):
        total = total + sums[part]
    sum_width = total.shape[1] - loss_out.shape[1]
    loss_out[...] = total[:, sum_width:]
    total = total[:, :sum_width].astype(jnp.bfloat16)
    half = chunk_width - sum_width
    for z in range(z_count):
        value = last[z]
        value = jnp.concatenate(
            [
                value[sub : sub + 1, side * half : (side + 1) * half]
                for sub in range(value.shape[0])
                for side in range(value.shape[1] // half)
            ],
            axis=0,
        )
        for other in range(mp_count):
            chunks_out[z, other, :, :sum_width] = total
            chunks_out[z, other, :, sum_width:] = jnp.where(
                lax.axis_index("z") == other, value, 0.0
            ).astype(jnp.bfloat16)


def local(
    query_emb,
    item_emb,
    pair_index,
    hard_index,
    hidden_in,
    lengths,
    w_query,
    key_weight_matrix,
    value_weight_matrix,
    w_out,
    key_down_matrix,
    key_up_matrix,
    value_down,
    value_up_matrix,
):
    bf16, f32 = jnp.bfloat16, jnp.float32
    x_count = lax.axis_size("x")
    z_count = lax.axis_size("z")
    plane_count = lax.axis_size(PLANE)
    dp_count = z_count * plane_count
    mp_count = lax.axis_size("mp")
    local_rows = query_emb.shape[0]
    batch_size = local_rows * dp_count
    feature_width = query_emb.shape[1]
    sub_count = hidden_in.shape[0]
    seq_len = hidden_in.shape[2]
    token_count = sub_count * seq_len
    full_rows = lax.all_gather(hidden_in, "mp", axis=3, tiled=True)
    model_width = full_rows.shape[3]
    token_inputs = full_rows.reshape(token_count, model_width)
    seq_lengths = lengths[:, 0]
    last_rows = jnp.arange(sub_count, dtype=jnp.int32) * seq_len + seq_lengths - 1

    core = lax.rem(lax.axis_index("mp"), 2)
    pair_rows = 2 * local_rows
    emb_pair = spread(jnp.concatenate([item_emb, query_emb], axis=0), ("h", "mp"))
    emb_pair = emb_pair.reshape(2, mp_count, pair_rows, feature_width)
    item_pair = lax.dynamic_index_in_dim(
        emb_pair[:, :, :local_rows], lax.axis_index("mp"), 1, keepdims=False
    ).reshape(pair_rows, feature_width)
    query_slices = lax.dynamic_index_in_dim(
        emb_pair[:, :, local_rows:], core, 0, keepdims=False
    )
    both = jnp.stack([w_query, w_out.T])
    both, query_slices = lax.optimization_barrier((both, query_slices))
    item_copies = jnp.broadcast_to(item_pair[None], (mp_count,) + item_pair.shape)
    chunks = jnp.concatenate([item_copies, query_slices], axis=1)
    chunks = jnp.broadcast_to(chunks[:, None], (z_count, x_count) + chunks.shape[1:])
    received = swap(chunks.reshape((z_count * x_count,) + chunks.shape[2:]), ("z", "x"))
    query_half = received[:, pair_rows:]
    other_half = lax.ppermute(query_half, "mp", [(a, a ^ 1) for a in range(mp_count)])
    queries_all = jnp.stack(
        [
            jnp.where(core == 0, query_half, other_half),
            jnp.where(core == 0, other_half, query_half),
        ],
        axis=1,
    ).reshape(batch_size, feature_width)
    items_all = (
        received[:, :pair_rows]
        .reshape(z_count, plane_count, local_rows, feature_width)
        .transpose(1, 0, 2, 3)
        .reshape(batch_size, feature_width)
    )
    partial_scores = final_product(query_emb, items_all)
    score_parts = spread(partial_scores, "mp")

    query_width = w_query.shape[1]
    other = lax.ppermute(both, "h", [(0, 1), (1, 0)])
    lower = lax.axis_index("h") == 0
    both = jnp.stack([jnp.where(lower, both, other), jnp.where(lower, other, both)])
    both = lax.all_gather(both, "x", axis=0, tiled=False)
    plane_shape = (feature_width, query_width)
    wq_plane = both[:, :, 0].reshape(plane_shape)
    wo_plane = both[:, :, 1].reshape(plane_shape)

    last_tokens = jnp.concatenate(
        [
            lax.dynamic_slice_in_dim(token_inputs, last_rows[sub], 1, 0)
            for sub in range(sub_count)
        ],
        axis=0,
    )
    last_slices = (
        last_tokens.reshape(sub_count, z_count, x_count, feature_width // x_count)
        .transpose(1, 2, 0, 3)
        .reshape(z_count, x_count * sub_count, feature_width // x_count)
    )

    chunks, residual, loss_part = call(
        functools.partial(residual_kernel, z_count, plane_count),
        (
            jax.ShapeDtypeStruct((dp_count, local_rows, 2 * LANES), bf16),
            jax.ShapeDtypeStruct((local_rows, batch_size), bf16),
            jax.ShapeDtypeStruct((local_rows, LANES), f32),
        ),
        2**24,
    )(score_parts, hard_index.T, pair_index[None], last_slices)
    column_rows = swap(chunks, DP).reshape(batch_size, 2 * LANES)
    adapter_rank = key_down_matrix.shape[1]
    up_width = key_up_matrix.shape[1]
    down_both = jnp.concatenate([key_down_matrix, value_down], axis=1)
    late_tokens, residual = lax.optimization_barrier((token_inputs, residual))
    head_shape = jax.ShapeDtypeStruct((token_count, up_width), bf16)
    low_shape = jax.ShapeDtypeStruct((token_count, 2 * adapter_rank), bf16)
    reduced_pair, key_rows, value_rows = call(
        token_kernel, (low_shape, head_shape, head_shape), 2**30
    )(
        late_tokens,
        key_weight_matrix,
        value_weight_matrix,
        down_both,
        key_up_matrix,
        value_up_matrix,
    )
    column_rows, key_rows, value_rows = lax.optimization_barrier(
        (column_rows, key_rows, value_rows)
    )
    column_grads, parts = call(
        functools.partial(gradient_kernel, z_count, sub_count),
        (
            jax.ShapeDtypeStruct((z_count * local_rows, feature_width), bf16),
            jax.ShapeDtypeStruct((z_count, 2 * sub_count, query_width + LANES), f32),
        ),
        2**26,
    )(column_rows, queries_all, loss_part, wq_plane, wo_plane)
    parts = swap(parts, "z")
    own_grads = lax.dynamic_index_in_dim(
        column_grads.reshape(z_count, local_rows, feature_width),
        lax.axis_index("mp"),
        0,
        keepdims=False,
    )
    item_grad = lax.ppermute(
        own_grads,
        ("z", "mp"),
        [(a * mp_count + b, b * mp_count + a) for a in range(z_count) for b in range(mp_count)],
    )
    query_grad = (jnp.dot(residual, items_all, preferred_element_type=f32) * INV_TEMP).astype(bf16)

    share_rows = 2 * adapter_rank // z_count
    sum_width = feature_width + up_width
    chunk_width = sum_width + sub_count * query_width // share_rows
    key_change, value_change, coef, loss_part, shares = call(
        attention_kernel,
        (
            head_shape,
            head_shape,
            low_shape,
            jax.ShapeDtypeStruct((2 * sub_count, LANES), f32),
            jax.ShapeDtypeStruct((z_count, mp_count, share_rows, chunk_width), bf16),
        ),
        2**26,
    )(
        lengths.T,
        parts,
        key_rows,
        value_rows,
        key_up_matrix,
        value_up_matrix,
        reduced_pair,
        token_inputs,
    )
    grid_shape = shares.shape
    shares = swap(shares.reshape((-1,) + grid_shape[2:]), ("z", "mp")).reshape(grid_shape)

    portion = call(portion_kernel, jax.ShapeDtypeStruct((token_count, model_width), bf16), 2**30)(
        key_change, value_change, coef, key_weight_matrix, value_weight_matrix, down_both.T
    )
    shares, portion = lax.optimization_barrier((shares, portion))
    input_sum = lax.psum_scatter(portion, "mp", scatter_dimension=1, tiled=True).astype(f32)
    sums, last_part = call(
        functools.partial(home_kernel, sub_count),
        (
            jax.ShapeDtypeStruct((plane_count, share_rows, sum_width + LANES), f32),
            jax.ShapeDtypeStruct((z_count, sub_count, feature_width), f32),
        ),
        2**24,
    )(shares, loss_part, wq_plane)
    chunks, loss_sum = call(
        return_kernel,
        (
            jax.ShapeDtypeStruct(grid_shape, bf16),
            jax.ShapeDtypeStruct((share_rows, LANES), f32),
        ),
        2**24,
    )(swap(sums, PLANE), last_part)
    mean_loss = loss_sum[0, 0] / batch_size
    summed = swap(chunks.reshape((-1,) + grid_shape[2:]), ("z", "mp")).reshape(grid_shape)
    own = lax.axis_index("mp")
    up_grad = lax.dynamic_index_in_dim(
        summed[:, :, :, feature_width:sum_width], own, 1, keepdims=False
    )
    up_grad = up_grad.reshape(2 * adapter_rank, up_width).astype(f32)
    last_rows_grad = jnp.sum(
        lax.dynamic_index_in_dim(
            summed[:, :, :, sum_width:], own, 0, keepdims=False
        ).astype(f32),
        axis=0,
    ).reshape(sub_count, feature_width) + item_grad[:sub_count].astype(f32)
    row_ids = jnp.arange(token_count, dtype=jnp.int32)[:, None]
    for sub in range(sub_count):
        input_sum = input_sum + jnp.where(
            row_ids == last_rows[sub], last_rows_grad[sub][None, :], 0.0
        )
    input_grad = input_sum.astype(bf16).reshape(hidden_in.shape)
    down_grad = (
        summed[:, :, :, :feature_width]
        .transpose(0, 2, 1, 3)
        .reshape(2 * adapter_rank, model_width)
        .astype(f32)
        .T
    )
    return (
        mean_loss,
        query_grad,
        item_grad,
        input_grad,
        down_grad[:, :adapter_rank],
        down_grad[:, adapter_rank:],
        up_grad[:adapter_rank],
        up_grad[adapter_rank:],
    )


def solution(mesh):
    fine = Mesh(
        mesh.devices.reshape(8, 4, 2, mesh.devices.shape[1]), ("z", "x", "h", "mp")
    )
    in_specs = (
        P(DP, "mp"),
        P(DP, "mp"),
        P(DP),
        P(DP, None),
        P(None, DP, None, "mp"),
        P(None, DP),
        P(DP, "mp"),
        P(None, "mp"),
        P(None, "mp"),
        P("mp", DP),
        P(),
        P(None, "mp"),
        P(),
        P(None, "mp"),
    )
    out_specs = (
        P(),
        P(DP, "mp"),
        P(DP, "mp"),
        P(None, DP, None, "mp"),
        P(),
        P(),
        P(None, "mp"),
        P(None, "mp"),
    )
    return jax.shard_map(local, mesh=fine, in_specs=in_specs, out_specs=out_specs, check_vma=False)
```

```python
import functools
import math

import jax
import jax.numpy as jnp
from jax import lax
from jax.experimental import pallas as pl
from jax.experimental.pallas import tpu as pltpu
from jax.sharding import Mesh
from jax.sharding import PartitionSpec as P

HEADS = 32
KV_HEADS = 8
HEAD_DIM = 128
LANES = 128

INV_TEMP = 50.0
HARD_NEGATIVE_ADD = 4.0
ADAPTER_SCALE = 2.0

PLANE = ("x", "h")
DP = ("z", "x", "h")


def final_product(left_side, right_side):
    return lax.dot_general(
        left_side, right_side, (((1,), (1,)), ((), ())), preferred_element_type=jnp.float32
    )


def first_product(left_side, right_side):
    return lax.dot_general(
        left_side, right_side, (((0,), (0,)), ((), ())), preferred_element_type=jnp.float32
    )


def spread(block, axes):
    count = lax.axis_size(axes)
    copies = jnp.broadcast_to(block[None], (count,) + block.shape)
    return lax.all_to_all(copies, axes, split_axis=0, concat_axis=0, tiled=True)


def swap(blocks, axes):
    return lax.all_to_all(blocks, axes, split_axis=0, concat_axis=0, tiled=True)


def call(kernel, out_shape, flops, **layout):
    return pl.pallas_call(
        kernel,
        out_shape=out_shape,
        compiler_params=pltpu.CompilerParams(vmem_limit_bytes=56 * 1024 * 1024),
        cost_estimate=pl.CostEstimate(flops=flops, bytes_accessed=2**20, transcendentals=4096),
        **layout,
    )


def upright(line):
    count = line.shape[1]
    row = lax.broadcasted_iota(jnp.int32, (count, count), 0)
    column = lax.broadcasted_iota(jnp.int32, (count, count), 1)
    return jnp.sum(jnp.where(row == column, line, 0), axis=1, keepdims=True)


def residual_kernel(
    z_count, plane_count, parts, hard, pair, tokens, chunks, residual_out, loss_out
):
    rows = parts.shape[1]
    batch_size = parts.shape[2]
    pair_scores = parts[0]
    for part in range(1, parts.shape[0]):
        pair_scores = pair_scores + parts[part]
    column = lax.broadcasted_iota(jnp.int32, (rows, batch_size), 1)
    inner = column % rows
    outer = column // rows
    item = ((outer % z_count) * plane_count + outer // z_count) * rows + inner
    count = jnp.zeros((rows, batch_size), jnp.float32)
    for choice in range(hard.shape[0]):
        count = count + jnp.where(upright(hard[choice : choice + 1]) == item, 1.0, 0.0)
    logits = pair_scores * INV_TEMP + HARD_NEGATIVE_ADD * count
    top = jnp.max(logits, axis=1, keepdims=True)
    log_total = top + jnp.log(jnp.sum(jnp.exp(logits - top), axis=1, keepdims=True))
    target = jnp.where(upright(pair[...]) == item, 1.0, 0.0)
    picked = jnp.sum(target * logits, axis=1, keepdims=True)
    loss = jnp.sum(log_total - picked, axis=0, keepdims=True)
    loss_out[...] = jnp.broadcast_to(loss, loss_out.shape)
    residual = jnp.exp(logits - log_total) - target
    residual_out[...] = residual.astype(jnp.bfloat16)
    width = z_count * rows
    pad = jnp.zeros((rows, LANES - width), jnp.float32)
    for plane in range(plane_count):
        block = jnp.concatenate([residual[:, plane * width : (plane + 1) * width], pad], axis=1)
        block = block.astype(jnp.bfloat16)
        for z in range(z_count):
            chunks[z * plane_count + plane, :, :LANES] = block
            chunks[z * plane_count + plane, :, LANES:] = tokens[z]


def token_kernel(tokens, key_weight, value_weight, down, key_up, value_up, low, keys, values):
    rank = key_up.shape[0]
    lows = jnp.dot(tokens[...], down[...], preferred_element_type=jnp.float32)
    lows = lows.astype(jnp.bfloat16)
    low[...] = lows
    for side, (weight, up, out) in enumerate(
        ((key_weight, key_up, keys), (value_weight, value_up, values))
    ):
        base = jnp.dot(tokens[...], weight[...], preferred_element_type=jnp.float32)
        mine = lows[:, side * rank : (side + 1) * rank]
        rise = jnp.dot(mine, up[...], preferred_element_type=jnp.float32)
        out[...] = (base + ADAPTER_SCALE * rise).astype(jnp.bfloat16)


def gradient_kernel(
    z_count, subs, received, queries, loss, wq_plane, wo_plane, item_out, parts_out
):
    item_rows = item_out.shape[0]
    width = received.shape[1] - LANES
    count = queries.shape[1] // width
    every = lax.dot_general(
        received[:, :LANES],
        queries[...],
        (((0,), (0,)), ((), ())),
        preferred_element_type=jnp.float32,
    )
    grads = (every[:item_rows] * INV_TEMP).astype(jnp.bfloat16)
    item_out[...] = grads
    picks = subs * z_count
    row = lax.broadcasted_iota(jnp.int32, (picks, item_rows), 0)
    column = lax.broadcasted_iota(jnp.int32, (picks, item_rows), 1)
    per_z = item_rows // z_count
    wanted = jnp.where((row // subs) * per_z + row % subs == column, 1.0, 0.0)
    cotangents = jnp.dot(
        wanted.astype(jnp.bfloat16), grads, preferred_element_type=jnp.float32
    )
    senders = received.shape[0] // per_z
    planes = senders // z_count
    row = lax.broadcasted_iota(jnp.int32, (picks, received.shape[0]), 0)
    column = lax.broadcasted_iota(jnp.int32, (picks, received.shape[0]), 1)
    plane = lax.axis_index(PLANE)
    first = ((row // subs) * planes + plane) * per_z + row % subs
    attn = query = None
    for block in range(count):
        cot = cotangents[:, block * width : (block + 1) * width]
        chosen = jnp.where(first + block * subs == column, 1.0, 0.0).astype(jnp.bfloat16)
        token = jnp.dot(chosen, received[:, LANES:], preferred_element_type=jnp.float32)
        rows = slice(block * width, (block + 1) * width)
        wq_rows, wo_rows = wq_plane[rows], wo_plane[rows]
        attn_term = jnp.dot(cot.astype(jnp.bfloat16), wo_rows, preferred_element_type=jnp.float32)
        query_term = jnp.dot(
            token.astype(jnp.bfloat16), wq_rows, preferred_element_type=jnp.float32
        )
        attn = attn_term if attn is None else attn + attn_term
        query = query_term if query is None else query + query_term
    end = attn.shape[1]
    for z in range(z_count):
        parts_out[z, :subs, :end] = attn[z * subs : (z + 1) * subs]
        parts_out[z, subs:, :end] = query[z * subs : (z + 1) * subs]
        parts_out[z, :, end:] = loss[: 2 * subs]


def attention_kernel(
    lengths,
    parts,
    keys,
    values,
    key_up,
    value_up,
    reduced,
    tokens,
    key_change_out,
    value_change_out,
    coef_out,
    loss_out,
    shares_out,
):
    subs = parts.shape[1] // 2
    token_count = keys.shape[0]
    seq_len = token_count // subs
    group = parts.shape[2] // HEAD_DIM - 1
    total = parts[0]
    for part in range(1, parts.shape[0]):
        total = total + parts[part]
    loss_out[...] = total[:, group * HEAD_DIM :]
    both = total.astype(jnp.bfloat16).astype(jnp.float32)

    def heads(first):
        return jnp.concatenate(
            [
                both[first + sub : first + sub + 1, head * HEAD_DIM : (head + 1) * HEAD_DIM]
                for sub in range(subs)
                for head in range(group)
            ],
            axis=0,
        )

    grad_heads = heads(0)
    q_heads = heads(subs)
    score_scale = 1.0 / math.sqrt(HEAD_DIM)
    raw = final_product(q_heads.astype(jnp.bfloat16), keys[...]) * score_scale
    row_sub = lax.broadcasted_iota(jnp.int32, raw.shape, 0) // group
    token = lax.broadcasted_iota(jnp.int32, raw.shape, 1)
    live = jnp.zeros(raw.shape, jnp.bool_)
    for sub in range(subs):
        first = sub * seq_len
        inside = (token >= first) & (token < first + lengths[0, sub])
        live = live | (inside & (row_sub == sub))
    raw = jnp.where(live, raw, -jnp.inf)
    weights = jnp.exp(raw - jnp.max(raw, axis=1, keepdims=True))
    probs = weights / jnp.sum(weights, axis=1, keepdims=True)
    prob_half = probs.astype(jnp.bfloat16).astype(jnp.float32)
    prob_grad = final_product(grad_heads.astype(jnp.bfloat16), values[...])
    score_grad = (
        probs * (prob_grad - jnp.sum(probs * prob_grad, axis=1, keepdims=True)) * score_scale
    )
    score_grad = score_grad.astype(jnp.bfloat16)
    delta = jnp.dot(score_grad, keys[...], preferred_element_type=jnp.float32)
    score_grad = score_grad.astype(jnp.float32)
    key_change = first_product(score_grad, q_heads).astype(jnp.bfloat16)
    value_change = first_product(prob_half, grad_heads).astype(jnp.bfloat16)
    key_coef = final_product(key_change, key_up[...])
    value_coef = final_product(value_change, value_up[...])
    coef = jnp.concatenate([key_coef, value_coef], axis=1).astype(jnp.bfloat16)
    key_change_out[...] = key_change
    value_change_out[...] = value_change
    coef_out[...] = coef
    rank = key_up.shape[0]
    ups = ADAPTER_SCALE * jnp.concatenate(
        [
            first_product(reduced[...], key_change)[:rank],
            first_product(reduced[...], value_change)[rank:],
        ],
        axis=0,
    )
    downs = ADAPTER_SCALE * first_product(coef, tokens[...])
    ranks = downs.shape[0]
    for chunk in range(shares_out.shape[0]):
        features = slice(chunk * LANES, (chunk + 1) * LANES)
        shares_out[chunk, :ranks] = downs[:, features].astype(jnp.bfloat16)
        own_up = jnp.broadcast_to(ups[chunk : chunk + 1], delta.shape)
        shares_out[chunk, ranks:] = jnp.concatenate([delta, own_up], axis=0).astype(jnp.bfloat16)


def portion_kernel(key_change, value_change, coef, key_weight, value_weight, down, out):
    width = 4 * LANES
    for start in range(0, out.shape[1], width):
        features = slice(start, start + width)
        portion = final_product(key_change[...], key_weight[features]) + final_product(
            value_change[...], value_weight[features]
        )
        portion = portion + ADAPTER_SCALE * jnp.dot(
            coef[...], down[:, features], preferred_element_type=jnp.float32
        )
        out[:, features] = portion.astype(jnp.bfloat16)


def home_kernel(z_count, subs, received, loss, wq_plane, out):
    senders, rows, _ = received.shape
    x_count = senders // z_count
    sides = 2 * subs * (wq_plane.shape[1] // LANES)
    ranks = rows - sides
    half = sides // 2
    total = received[0].astype(jnp.float32)
    for sender in range(1, senders):
        total = total + received[sender].astype(jnp.float32)
    deltas = jnp.concatenate(
        [
            received[z * x_count + lax.axis_index("x"), ranks:].astype(jnp.float32)[:half]
            for z in range(z_count)
        ],
        axis=0,
    ).astype(jnp.bfloat16)
    heads = half // subs
    picks = subs * z_count
    row = lax.broadcasted_iota(jnp.int32, (picks, deltas.shape[0]), 0)
    column = lax.broadcasted_iota(jnp.int32, (picks, deltas.shape[0]), 1)
    last = None
    for head in range(heads):
        wanted = jnp.where(row * heads + head == column, 1.0, 0.0).astype(jnp.bfloat16)
        delta = jnp.dot(wanted, deltas, preferred_element_type=jnp.float32).astype(jnp.bfloat16)
        term = final_product(delta, wq_plane[:, head * LANES : (head + 1) * LANES])
        last = term if last is None else last + term
    lines = [total[ranks + half : ranks + half + 1]]
    left = loss[:1]
    for _ in range(3):
        term = left.astype(jnp.bfloat16).astype(jnp.float32)
        lines.append(term)
        left = left - term
    lines.append(jnp.zeros((half - len(lines), LANES), jnp.float32))
    downs = total[:ranks].astype(jnp.bfloat16)
    copies = out.shape[0] // z_count
    for z in range(z_count):
        blocks = [
            last[z * subs + sub : z * subs + sub + 1, side * LANES : (side + 1) * LANES]
            for sub in range(subs)
            for side in range(heads)
        ]
        extra = jnp.concatenate(blocks + lines, axis=0).astype(jnp.bfloat16)
        for copy in range(copies):
            out[copy * z_count + z, :ranks] = downs
            out[copy * z_count + z, ranks:] = extra


def return_kernel(mp_count, received, out, last_out):
    senders, rows, _ = received.shape
    half = last_out.shape[0]
    ranks = rows - 2 * half
    total = received[0, :ranks].astype(jnp.float32)
    for sender in range(1, senders):
        total = total + received[sender, :ranks].astype(jnp.float32)
    lasts = None
    for other in range(mp_count):
        term = received[lax.axis_index("h") * mp_count + other, ranks:].astype(jnp.float32)[:half]
        lasts = term if lasts is None else lasts + term
    last_out[...] = lasts
    lines = None
    for side in range(senders // mp_count):
        term = received[side * mp_count + lax.axis_index("mp"), ranks:].astype(jnp.float32)[half:]
        lines = term if lines is None else lines + term
    left = lines[1:2] + lines[2:3] + lines[3:4]
    parts = [lines[:1]]
    for _ in range(3):
        term = left.astype(jnp.bfloat16).astype(jnp.float32)
        parts.append(term)
        left = left - term
    parts.append(jnp.zeros((2 * half - len(parts), LANES), jnp.float32))
    extra = jnp.concatenate(parts, axis=0).astype(jnp.bfloat16)
    downs = total.astype(jnp.bfloat16)
    for copy in range(out.shape[0]):
        out[copy, :ranks] = downs
        out[copy, ranks:] = extra


def local(
    query_emb,
    item_emb,
    pair_index,
    hard_index,
    hidden_in,
    lengths,
    w_query,
    key_weight_matrix,
    value_weight_matrix,
    w_out,
    key_down_matrix,
    key_up_matrix,
    value_down,
    value_up_matrix,
):
    bf16, f32 = jnp.bfloat16, jnp.float32
    x_count = lax.axis_size("x")
    z_count = lax.axis_size("z")
    plane_count = lax.axis_size(PLANE)
    dp_count = z_count * plane_count
    mp_count = lax.axis_size("mp")
    local_rows = query_emb.shape[0]
    batch_size = local_rows * dp_count
    feature_width = query_emb.shape[1]
    sub_count = hidden_in.shape[0]
    seq_len = hidden_in.shape[2]
    token_count = sub_count * seq_len
    full_rows = lax.all_gather(hidden_in, "mp", axis=3, tiled=True)
    model_width = full_rows.shape[3]
    token_inputs = full_rows.reshape(token_count, model_width)
    seq_lengths = lengths[:, 0]
    last_rows = jnp.arange(sub_count, dtype=jnp.int32) * seq_len + seq_lengths - 1

    core = lax.rem(lax.axis_index("mp"), 2)
    pair_rows = 2 * local_rows
    emb_pair = spread(jnp.concatenate([item_emb, query_emb], axis=0), ("h", "mp"))
    emb_pair = emb_pair.reshape(2, mp_count, pair_rows, feature_width)
    item_pair = lax.dynamic_index_in_dim(
        emb_pair[:, :, :local_rows], lax.axis_index("mp"), 1, keepdims=False
    ).reshape(pair_rows, feature_width)
    query_slices = lax.dynamic_index_in_dim(
        emb_pair[:, :, local_rows:], core, 0, keepdims=False
    )
    both = jnp.stack([w_query, w_out.T])
    both, query_slices = lax.optimization_barrier((both, query_slices))
    item_copies = jnp.broadcast_to(item_pair[None], (mp_count,) + item_pair.shape)
    chunks = jnp.concatenate([item_copies, query_slices], axis=1)
    chunks = jnp.broadcast_to(chunks[:, None], (z_count, x_count) + chunks.shape[1:])
    received = swap(chunks.reshape((z_count * x_count,) + chunks.shape[2:]), ("z", "x"))
    query_half = received[:, pair_rows:]
    other_half = lax.ppermute(query_half, "mp", [(a, a ^ 1) for a in range(mp_count)])
    queries_all = jnp.stack(
        [
            jnp.where(core == 0, query_half, other_half),
            jnp.where(core == 0, other_half, query_half),
        ],
        axis=1,
    ).reshape(batch_size, feature_width)
    items_all = (
        received[:, :pair_rows]
        .reshape(z_count, plane_count, local_rows, feature_width)
        .transpose(1, 0, 2, 3)
        .reshape(batch_size, feature_width)
    )
    partial_scores = final_product(query_emb, items_all)
    score_parts = spread(partial_scores, "mp")

    query_width = w_query.shape[1]
    other = lax.ppermute(both, "h", [(0, 1), (1, 0)])
    lower = lax.axis_index("h") == 0
    both = jnp.stack([jnp.where(lower, both, other), jnp.where(lower, other, both)])
    both = lax.all_gather(both, "x", axis=0, tiled=False)
    plane_shape = (feature_width, query_width)
    wq_plane = both[:, :, 0].reshape(plane_shape)
    wo_plane = both[:, :, 1].reshape(plane_shape)

    last_tokens = jnp.concatenate(
        [
            lax.dynamic_slice_in_dim(token_inputs, last_rows[sub], 1, 0)
            for sub in range(sub_count)
        ],
        axis=0,
    )
    last_slices = (
        last_tokens.reshape(sub_count, z_count, x_count, feature_width // x_count)
        .transpose(1, 2, 0, 3)
        .reshape(z_count, x_count * sub_count, feature_width // x_count)
    )

    chunks, residual, loss_part = call(
        functools.partial(residual_kernel, z_count, plane_count),
        (
            jax.ShapeDtypeStruct((dp_count, local_rows, 2 * LANES), bf16),
            jax.ShapeDtypeStruct((local_rows, batch_size), bf16),
            jax.ShapeDtypeStruct((local_rows, LANES), f32),
        ),
        2**24,
    )(score_parts, hard_index.T, pair_index[None], last_slices)
    column_rows = swap(chunks, DP).reshape(batch_size, 2 * LANES)
    adapter_rank = key_down_matrix.shape[1]
    up_width = key_up_matrix.shape[1]
    down_both = jnp.concatenate([key_down_matrix, value_down], axis=1)
    late_tokens, residual = lax.optimization_barrier((token_inputs, residual))
    head_shape = jax.ShapeDtypeStruct((token_count, up_width), bf16)
    low_shape = jax.ShapeDtypeStruct((token_count, 2 * adapter_rank), bf16)
    reduced_pair, key_rows, value_rows = call(
        token_kernel, (low_shape, head_shape, head_shape), 2**30
    )(
        late_tokens,
        key_weight_matrix,
        value_weight_matrix,
        down_both,
        key_up_matrix,
        value_up_matrix,
    )
    column_rows, key_rows, value_rows = lax.optimization_barrier(
        (column_rows, key_rows, value_rows)
    )
    column_grads, parts = call(
        functools.partial(gradient_kernel, z_count, sub_count),
        (
            jax.ShapeDtypeStruct((z_count * local_rows, feature_width), bf16),
            jax.ShapeDtypeStruct((z_count, 2 * sub_count, query_width + LANES), f32),
        ),
        2**26,
    )(column_rows, queries_all, loss_part, wq_plane, wo_plane)
    parts = swap(parts, "z")
    query_grad = (jnp.dot(residual, items_all, preferred_element_type=f32) * INV_TEMP).astype(bf16)

    ranks = 2 * adapter_rank
    share_shape = (z_count * x_count, ranks + 2 * sub_count * query_width // LANES, LANES)
    key_change, value_change, coef, loss_part, shares = call(
        attention_kernel,
        (
            head_shape,
            head_shape,
            low_shape,
            jax.ShapeDtypeStruct((2 * sub_count, LANES), f32),
            jax.ShapeDtypeStruct(share_shape, bf16),
        ),
        2**26,
    )(
        lengths.T,
        parts,
        key_rows,
        value_rows,
        key_up_matrix,
        value_up_matrix,
        reduced_pair,
        token_inputs,
    )
    shares = swap(shares, ("z", "x"))

    portion = call(portion_kernel, jax.ShapeDtypeStruct((token_count, model_width), bf16), 2**30)(
        key_change, value_change, coef, key_weight_matrix, value_weight_matrix, down_both.T
    )
    input_sum = lax.psum_scatter(portion, "mp", scatter_dimension=1, tiled=True).astype(f32)
    middle = call(
        functools.partial(home_kernel, z_count, sub_count),
        jax.ShapeDtypeStruct((2 * mp_count,) + share_shape[1:], bf16),
        2**26,
    )(shares, loss_part, wq_plane)
    chunks, last_part = call(
        functools.partial(return_kernel, mp_count),
        (
            jax.ShapeDtypeStruct(share_shape, bf16),
            jax.ShapeDtypeStruct((sub_count * query_width // LANES, LANES), f32),
        ),
        2**24,
    )(swap(middle, ("h", "mp")))
    summed = swap(chunks, ("z", "x"))
    up_grad = summed[:, ranks].astype(f32)
    mean_loss = jnp.sum(summed[:x_count, ranks + 1 : ranks + 4, 0].astype(f32)) / batch_size
    own_grads = lax.dynamic_index_in_dim(
        column_grads.reshape(z_count, local_rows, feature_width),
        lax.axis_index("mp"),
        0,
        keepdims=False,
    )
    own_last = last_part.reshape(sub_count, feature_width).astype(bf16)
    at_home = lax.ppermute(
        jnp.concatenate([own_grads, own_last], axis=0),
        ("z", "mp"),
        [(a * mp_count + b, b * mp_count + a) for a in range(z_count) for b in range(mp_count)],
    )
    item_grad = at_home[:local_rows]
    last_rows_grad = at_home[local_rows:].astype(f32) + item_grad[:sub_count].astype(f32)
    row_ids = jnp.arange(token_count, dtype=jnp.int32)[:, None]
    for sub in range(sub_count):
        input_sum = input_sum + jnp.where(
            row_ids == last_rows[sub], last_rows_grad[sub][None, :], 0.0
        )
    input_grad = input_sum.astype(bf16).reshape(hidden_in.shape)
    down_grad = summed[:, :ranks].transpose(1, 0, 2).reshape(ranks, model_width).astype(f32).T
    return (
        mean_loss,
        query_grad,
        item_grad,
        input_grad,
        down_grad[:, :adapter_rank],
        down_grad[:, adapter_rank:],
        up_grad[:adapter_rank],
        up_grad[adapter_rank:],
    )


def solution(mesh):
    fine = Mesh(
        mesh.devices.reshape(8, 4, 2, mesh.devices.shape[1]), ("z", "x", "h", "mp")
    )
    in_specs = (
        P(DP, "mp"),
        P(DP, "mp"),
        P(DP),
        P(DP, None),
        P(None, DP, None, "mp"),
        P(None, DP),
        P(DP, "mp"),
        P(None, "mp"),
        P(None, "mp"),
        P("mp", DP),
        P(),
        P(None, "mp"),
        P(),
        P(None, "mp"),
    )
    out_specs = (
        P(),
        P(DP, "mp"),
        P(DP, "mp"),
        P(None, DP, None, "mp"),
        P(),
        P(),
        P(None, "mp"),
        P(None, "mp"),
    )
    return jax.shard_map(local, mesh=fine, in_specs=in_specs, out_specs=out_specs, check_vma=False)
```

```python
import functools
import math

import jax
import jax.numpy as jnp
from jax import lax
from jax.experimental import pallas as pl
from jax.experimental.pallas import tpu as pltpu
from jax.sharding import Mesh
from jax.sharding import PartitionSpec as P

HEADS = 32
KV_HEADS = 8
HEAD_DIM = 128
LANES = 128

INV_TEMP = 50.0
HARD_NEGATIVE_ADD = 4.0
ADAPTER_SCALE = 2.0

PLANE = ("x", "h")
DP = ("z", "x", "h")


def final_product(left_side, right_side):
    return lax.dot_general(
        left_side, right_side, (((1,), (1,)), ((), ())), preferred_element_type=jnp.float32
    )


def first_product(left_side, right_side):
    return lax.dot_general(
        left_side, right_side, (((0,), (0,)), ((), ())), preferred_element_type=jnp.float32
    )


def spread(block, axes):
    count = lax.axis_size(axes)
    copies = jnp.broadcast_to(block[None], (count,) + block.shape)
    return lax.all_to_all(copies, axes, split_axis=0, concat_axis=0, tiled=True)


def swap(blocks, axes):
    return lax.all_to_all(blocks, axes, split_axis=0, concat_axis=0, tiled=True)


def call(kernel, out_shape, flops, mebibytes=56):
    return pl.pallas_call(
        kernel,
        out_shape=out_shape,
        compiler_params=pltpu.CompilerParams(vmem_limit_bytes=mebibytes * 1024 * 1024),
        cost_estimate=pl.CostEstimate(flops=flops, bytes_accessed=2**20, transcendentals=4096),
    )


def upright(line):
    count = line.shape[1]
    row = lax.broadcasted_iota(jnp.int32, (count, count), 0)
    column = lax.broadcasted_iota(jnp.int32, (count, count), 1)
    return jnp.sum(jnp.where(row == column, line, 0), axis=1, keepdims=True)


def residual_kernel(
    z_count, plane_count, parts, hard, pair, tokens, chunks, residual_out, loss_out
):
    rows = parts.shape[1]
    batch_size = parts.shape[2]
    pair_scores = parts[0]
    for part in range(1, parts.shape[0]):
        pair_scores = pair_scores + parts[part]
    column = lax.broadcasted_iota(jnp.int32, (rows, batch_size), 1)
    inner = column % rows
    outer = column // rows
    item = ((outer % z_count) * plane_count + outer // z_count) * rows + inner
    count = jnp.zeros((rows, batch_size), jnp.float32)
    for choice in range(hard.shape[0]):
        count = count + jnp.where(upright(hard[choice : choice + 1]) == item, 1.0, 0.0)
    logits = pair_scores * INV_TEMP + HARD_NEGATIVE_ADD * count
    top = jnp.max(logits, axis=1, keepdims=True)
    log_total = top + jnp.log(jnp.sum(jnp.exp(logits - top), axis=1, keepdims=True))
    target = jnp.where(upright(pair[...]) == item, 1.0, 0.0)
    picked = jnp.sum(target * logits, axis=1, keepdims=True)
    loss = jnp.sum(log_total - picked, axis=0, keepdims=True)
    loss_out[...] = jnp.broadcast_to(loss, loss_out.shape)
    residual = jnp.exp(logits - log_total) - target
    residual_out[...] = residual.astype(jnp.bfloat16)
    width = z_count * rows
    pad = jnp.zeros((rows, LANES - width), jnp.float32)
    for plane in range(plane_count):
        block = jnp.concatenate([residual[:, plane * width : (plane + 1) * width], pad], axis=1)
        block = block.astype(jnp.bfloat16)
        for z in range(z_count):
            chunks[z * plane_count + plane, :, :LANES] = block
            chunks[z * plane_count + plane, :, LANES:] = tokens[z]


def token_kernel(tokens, key_weight, value_weight, down, key_up, value_up, low, keys, values):
    rank = key_up.shape[0]
    lows = jnp.dot(tokens[...], down[...], preferred_element_type=jnp.float32)
    lows = lows.astype(jnp.bfloat16)
    low[...] = lows
    for side, (weight, up, out) in enumerate(
        ((key_weight, key_up, keys), (value_weight, value_up, values))
    ):
        base = jnp.dot(tokens[...], weight[...], preferred_element_type=jnp.float32)
        mine = lows[:, side * rank : (side + 1) * rank]
        rise = jnp.dot(mine, up[...], preferred_element_type=jnp.float32)
        out[...] = (base + ADAPTER_SCALE * rise).astype(jnp.bfloat16)


def gradient_kernel(
    z_count, subs, received, queries, loss, wq_plane, wo_plane, item_out, parts_out
):
    item_rows = item_out.shape[0]
    width = received.shape[1] - LANES
    count = queries.shape[1] // width
    every = lax.dot_general(
        received[:, :LANES],
        queries[...],
        (((0,), (0,)), ((), ())),
        preferred_element_type=jnp.float32,
    )
    grads = (every[:item_rows] * INV_TEMP).astype(jnp.bfloat16)
    item_out[...] = grads
    picks = subs * z_count
    row = lax.broadcasted_iota(jnp.int32, (picks, item_rows), 0)
    column = lax.broadcasted_iota(jnp.int32, (picks, item_rows), 1)
    per_z = item_rows // z_count
    wanted = jnp.where((row // subs) * per_z + row % subs == column, 1.0, 0.0)
    cotangents = jnp.dot(
        wanted.astype(jnp.bfloat16), grads, preferred_element_type=jnp.float32
    )
    senders = received.shape[0] // per_z
    planes = senders // z_count
    row = lax.broadcasted_iota(jnp.int32, (picks, received.shape[0]), 0)
    column = lax.broadcasted_iota(jnp.int32, (picks, received.shape[0]), 1)
    plane = lax.axis_index(PLANE)
    first = ((row // subs) * planes + plane) * per_z + row % subs
    attn = query = None
    for block in range(count):
        cot = cotangents[:, block * width : (block + 1) * width]
        chosen = jnp.where(first + block * subs == column, 1.0, 0.0).astype(jnp.bfloat16)
        token = jnp.dot(chosen, received[:, LANES:], preferred_element_type=jnp.float32)
        rows = slice(block * width, (block + 1) * width)
        wq_rows, wo_rows = wq_plane[rows], wo_plane[rows]
        attn_term = jnp.dot(cot.astype(jnp.bfloat16), wo_rows, preferred_element_type=jnp.float32)
        query_term = jnp.dot(
            token.astype(jnp.bfloat16), wq_rows, preferred_element_type=jnp.float32
        )
        attn = attn_term if attn is None else attn + attn_term
        query = query_term if query is None else query + query_term
    end = attn.shape[1]
    for z in range(z_count):
        parts_out[z, :subs, :end] = attn[z * subs : (z + 1) * subs]
        parts_out[z, subs:, :end] = query[z * subs : (z + 1) * subs]
        parts_out[z, :, end:] = loss[: 2 * subs]


def attention_kernel(
    lengths,
    parts,
    keys,
    values,
    key_up,
    value_up,
    reduced,
    tokens,
    key_change_out,
    value_change_out,
    coef_out,
    loss_out,
    shares_out,
):
    subs = parts.shape[1] // 2
    token_count = keys.shape[0]
    seq_len = token_count // subs
    group = parts.shape[2] // HEAD_DIM - 1
    total = parts[0]
    for part in range(1, parts.shape[0]):
        total = total + parts[part]
    loss_out[...] = total[:, group * HEAD_DIM :]
    both = total.astype(jnp.bfloat16).astype(jnp.float32)

    def heads(first):
        return jnp.concatenate(
            [
                both[first + sub : first + sub + 1, head * HEAD_DIM : (head + 1) * HEAD_DIM]
                for sub in range(subs)
                for head in range(group)
            ],
            axis=0,
        )

    grad_heads = heads(0)
    q_heads = heads(subs)
    score_scale = 1.0 / math.sqrt(HEAD_DIM)
    raw = final_product(q_heads.astype(jnp.bfloat16), keys[...]) * score_scale
    row_sub = lax.broadcasted_iota(jnp.int32, raw.shape, 0) // group
    token = lax.broadcasted_iota(jnp.int32, raw.shape, 1)
    live = jnp.zeros(raw.shape, jnp.bool_)
    for sub in range(subs):
        first = sub * seq_len
        inside = (token >= first) & (token < first + lengths[0, sub])
        live = live | (inside & (row_sub == sub))
    raw = jnp.where(live, raw, -jnp.inf)
    weights = jnp.exp(raw - jnp.max(raw, axis=1, keepdims=True))
    probs = weights / jnp.sum(weights, axis=1, keepdims=True)
    prob_half = probs.astype(jnp.bfloat16).astype(jnp.float32)
    prob_grad = final_product(grad_heads.astype(jnp.bfloat16), values[...])
    score_grad = (
        probs * (prob_grad - jnp.sum(probs * prob_grad, axis=1, keepdims=True)) * score_scale
    )
    score_grad = score_grad.astype(jnp.bfloat16)
    delta = jnp.dot(score_grad, keys[...], preferred_element_type=jnp.float32)
    score_grad = score_grad.astype(jnp.float32)
    key_change = first_product(score_grad, q_heads).astype(jnp.bfloat16)
    value_change = first_product(prob_half, grad_heads).astype(jnp.bfloat16)
    key_coef = final_product(key_change, key_up[...])
    value_coef = final_product(value_change, value_up[...])
    coef = jnp.concatenate([key_coef, value_coef], axis=1).astype(jnp.bfloat16)
    key_change_out[...] = key_change
    value_change_out[...] = value_change
    coef_out[...] = coef
    rank = key_up.shape[0]
    ups = ADAPTER_SCALE * jnp.concatenate(
        [
            first_product(reduced[...], key_change)[:rank],
            first_product(reduced[...], value_change)[rank:],
        ],
        axis=0,
    )
    downs = ADAPTER_SCALE * first_product(coef, tokens[...])
    ranks = downs.shape[0]
    for chunk in range(shares_out.shape[0]):
        features = slice(chunk * LANES, (chunk + 1) * LANES)
        shares_out[chunk, :ranks] = downs[:, features].astype(jnp.bfloat16)
        own_up = jnp.broadcast_to(ups[chunk : chunk + 1], delta.shape)
        shares_out[chunk, ranks:] = jnp.concatenate([delta, own_up], axis=0).astype(jnp.bfloat16)


def portion_kernel(key_change, value_change, coef, key_weight, value_weight, down, out):
    width = 4 * LANES
    for start in range(0, out.shape[1], width):
        features = slice(start, start + width)
        portion = final_product(key_change[...], key_weight[features]) + final_product(
            value_change[...], value_weight[features]
        )
        portion = portion + ADAPTER_SCALE * jnp.dot(
            coef[...], down[:, features], preferred_element_type=jnp.float32
        )
        out[:, features] = portion.astype(jnp.bfloat16)


def home_kernel(z_count, subs, received, loss, wq_plane, out):
    senders, rows, _ = received.shape
    x_count = senders // z_count
    sides = 2 * subs * (wq_plane.shape[1] // LANES)
    ranks = rows - sides
    half = sides // 2
    total = received[0].astype(jnp.float32)
    for sender in range(1, senders):
        total = total + received[sender].astype(jnp.float32)
    deltas = jnp.concatenate(
        [
            received[z * x_count + lax.axis_index("x"), ranks:].astype(jnp.float32)[:half]
            for z in range(z_count)
        ],
        axis=0,
    ).astype(jnp.bfloat16)
    heads = half // subs
    picks = subs * z_count
    row = lax.broadcasted_iota(jnp.int32, (picks, deltas.shape[0]), 0)
    column = lax.broadcasted_iota(jnp.int32, (picks, deltas.shape[0]), 1)
    last = None
    for head in range(heads):
        wanted = jnp.where(row * heads + head == column, 1.0, 0.0).astype(jnp.bfloat16)
        delta = jnp.dot(wanted, deltas, preferred_element_type=jnp.float32).astype(jnp.bfloat16)
        term = final_product(delta, wq_plane[:, head * LANES : (head + 1) * LANES])
        last = term if last is None else last + term
    lines = [total[ranks + half : ranks + half + 1]]
    left = loss[:1]
    for _ in range(3):
        term = left.astype(jnp.bfloat16).astype(jnp.float32)
        lines.append(term)
        left = left - term
    lines.append(jnp.zeros((half - len(lines), LANES), jnp.float32))
    downs = total[:ranks].astype(jnp.bfloat16)
    copies = out.shape[0] // z_count
    for z in range(z_count):
        blocks = [
            last[z * subs + sub : z * subs + sub + 1, side * LANES : (side + 1) * LANES]
            for sub in range(subs)
            for side in range(heads)
        ]
        extra = jnp.concatenate(blocks + lines, axis=0).astype(jnp.bfloat16)
        for copy in range(copies):
            out[copy * z_count + z, :ranks] = downs
            out[copy * z_count + z, ranks:] = extra


def return_kernel(mp_count, received, out, last_out):
    senders, rows, _ = received.shape
    half = last_out.shape[0]
    ranks = rows - 2 * half
    total = received[0, :ranks].astype(jnp.float32)
    for sender in range(1, senders):
        total = total + received[sender, :ranks].astype(jnp.float32)
    lasts = None
    for other in range(mp_count):
        term = received[lax.axis_index("h") * mp_count + other, ranks:].astype(jnp.float32)[:half]
        lasts = term if lasts is None else lasts + term
    last_out[...] = lasts
    lines = None
    for side in range(senders // mp_count):
        term = received[side * mp_count + lax.axis_index("mp"), ranks:].astype(jnp.float32)[half:]
        lines = term if lines is None else lines + term
    left = lines[1:2] + lines[2:3] + lines[3:4]
    parts = [lines[:1]]
    for _ in range(3):
        term = left.astype(jnp.bfloat16).astype(jnp.float32)
        parts.append(term)
        left = left - term
    parts.append(jnp.zeros((2 * half - len(parts), LANES), jnp.float32))
    extra = jnp.concatenate(parts, axis=0).astype(jnp.bfloat16)
    downs = total.astype(jnp.bfloat16)
    for copy in range(out.shape[0]):
        out[copy, :ranks] = downs
        out[copy, ranks:] = extra


def local(
    query_emb,
    item_emb,
    pair_index,
    hard_index,
    hidden_in,
    lengths,
    w_query,
    key_weight_matrix,
    value_weight_matrix,
    w_out,
    key_down_matrix,
    key_up_matrix,
    value_down,
    value_up_matrix,
):
    bf16, f32 = jnp.bfloat16, jnp.float32
    x_count = lax.axis_size("x")
    z_count = lax.axis_size("z")
    plane_count = lax.axis_size(PLANE)
    dp_count = z_count * plane_count
    mp_count = lax.axis_size("mp")
    local_rows = query_emb.shape[0]
    batch_size = local_rows * dp_count
    feature_width = query_emb.shape[1]
    sub_count = hidden_in.shape[0]
    seq_len = hidden_in.shape[2]
    token_count = sub_count * seq_len
    full_rows = lax.all_gather(hidden_in, "mp", axis=3, tiled=True)
    model_width = full_rows.shape[3]
    token_inputs = full_rows.reshape(token_count, model_width)
    seq_lengths = lengths[:, 0]
    last_rows = jnp.arange(sub_count, dtype=jnp.int32) * seq_len + seq_lengths - 1

    core = lax.rem(lax.axis_index("mp"), 2)
    pair_rows = 2 * local_rows
    emb_pair = spread(jnp.concatenate([item_emb, query_emb], axis=0), ("h", "mp"))
    emb_pair = emb_pair.reshape(2, mp_count, pair_rows, feature_width)
    item_pair = lax.dynamic_index_in_dim(
        emb_pair[:, :, :local_rows], lax.axis_index("mp"), 1, keepdims=False
    ).reshape(pair_rows, feature_width)
    query_slices = lax.dynamic_index_in_dim(
        emb_pair[:, :, local_rows:], core, 0, keepdims=False
    )
    both = jnp.stack([w_query, w_out.T])
    both, query_slices = lax.optimization_barrier((both, query_slices))
    item_copies = jnp.broadcast_to(item_pair[None], (mp_count,) + item_pair.shape)
    chunks = jnp.concatenate([item_copies, query_slices], axis=1)
    chunks = jnp.broadcast_to(chunks[:, None], (z_count, x_count) + chunks.shape[1:])
    received = swap(chunks.reshape((z_count * x_count,) + chunks.shape[2:]), ("z", "x"))
    query_half = received[:, pair_rows:]
    other_half = lax.ppermute(query_half, "mp", [(a, a ^ 1) for a in range(mp_count)])
    queries_all = jnp.stack(
        [
            jnp.where(core == 0, query_half, other_half),
            jnp.where(core == 0, other_half, query_half),
        ],
        axis=1,
    ).reshape(batch_size, feature_width)
    items_all = (
        received[:, :pair_rows]
        .reshape(z_count, plane_count, local_rows, feature_width)
        .transpose(1, 0, 2, 3)
        .reshape(batch_size, feature_width)
    )
    partial_scores = final_product(query_emb, items_all)
    score_parts = spread(partial_scores, "mp")

    query_width = w_query.shape[1]
    other = lax.ppermute(both, "h", [(0, 1), (1, 0)])
    lower = lax.axis_index("h") == 0
    both = jnp.stack([jnp.where(lower, both, other), jnp.where(lower, other, both)])
    both = lax.all_gather(both, "x", axis=0, tiled=False)
    plane_shape = (feature_width, query_width)
    wq_plane = both[:, :, 0].reshape(plane_shape)
    wo_plane = both[:, :, 1].reshape(plane_shape)

    last_tokens = jnp.concatenate(
        [
            lax.dynamic_slice_in_dim(token_inputs, last_rows[sub], 1, 0)
            for sub in range(sub_count)
        ],
        axis=0,
    )
    last_slices = (
        last_tokens.reshape(sub_count, z_count, x_count, feature_width // x_count)
        .transpose(1, 2, 0, 3)
        .reshape(z_count, x_count * sub_count, feature_width // x_count)
    )

    chunks, residual, loss_part = call(
        functools.partial(residual_kernel, z_count, plane_count),
        (
            jax.ShapeDtypeStruct((dp_count, local_rows, 2 * LANES), bf16),
            jax.ShapeDtypeStruct((local_rows, batch_size), bf16),
            jax.ShapeDtypeStruct((local_rows, LANES), f32),
        ),
        2**24,
        8,
    )(score_parts, hard_index.T, pair_index[None], last_slices)
    column_rows = swap(chunks, DP).reshape(batch_size, 2 * LANES)
    adapter_rank = key_down_matrix.shape[1]
    up_width = key_up_matrix.shape[1]
    down_both = jnp.concatenate([key_down_matrix, value_down], axis=1)
    late_tokens, column_rows = lax.optimization_barrier((token_inputs, column_rows))
    head_shape = jax.ShapeDtypeStruct((token_count, up_width), bf16)
    low_shape = jax.ShapeDtypeStruct((token_count, 2 * adapter_rank), bf16)
    reduced_pair, key_rows, value_rows = call(
        token_kernel, (low_shape, head_shape, head_shape), 2**30
    )(
        late_tokens,
        key_weight_matrix,
        value_weight_matrix,
        down_both,
        key_up_matrix,
        value_up_matrix,
    )
    column_grads, parts = call(
        functools.partial(gradient_kernel, z_count, sub_count),
        (
            jax.ShapeDtypeStruct((z_count * local_rows, feature_width), bf16),
            jax.ShapeDtypeStruct((z_count, 2 * sub_count, query_width + LANES), f32),
        ),
        2**26,
        8,
    )(column_rows, queries_all, loss_part, wq_plane, wo_plane)
    parts = swap(parts, "z")
    query_grad = (jnp.dot(residual, items_all, preferred_element_type=f32) * INV_TEMP).astype(bf16)

    ranks = 2 * adapter_rank
    share_shape = (z_count * x_count, ranks + 2 * sub_count * query_width // LANES, LANES)
    key_change, value_change, coef, loss_part, shares = call(
        attention_kernel,
        (
            head_shape,
            head_shape,
            low_shape,
            jax.ShapeDtypeStruct((2 * sub_count, LANES), f32),
            jax.ShapeDtypeStruct(share_shape, bf16),
        ),
        2**26,
    )(
        lengths.T,
        parts,
        key_rows,
        value_rows,
        key_up_matrix,
        value_up_matrix,
        reduced_pair,
        token_inputs,
    )
    shares = swap(shares, ("z", "x"))

    portion = call(portion_kernel, jax.ShapeDtypeStruct((token_count, model_width), bf16), 2**30)(
        key_change, value_change, coef, key_weight_matrix, value_weight_matrix, down_both.T
    )
    input_sum = lax.psum_scatter(portion, "mp", scatter_dimension=1, tiled=True).astype(f32)
    middle = call(
        functools.partial(home_kernel, z_count, sub_count),
        jax.ShapeDtypeStruct((2 * mp_count,) + share_shape[1:], bf16),
        2**26,
        8,
    )(shares, loss_part, wq_plane)
    chunks, last_part = call(
        functools.partial(return_kernel, mp_count),
        (
            jax.ShapeDtypeStruct(share_shape, bf16),
            jax.ShapeDtypeStruct((sub_count * query_width // LANES, LANES), f32),
        ),
        2**24,
        8,
    )(swap(middle, ("h", "mp")))
    summed = swap(chunks, ("z", "x"))
    own_grads = lax.dynamic_index_in_dim(
        column_grads.reshape(z_count, local_rows, feature_width),
        lax.axis_index("mp"),
        0,
        keepdims=False,
    )
    own_last = last_part.reshape(sub_count, feature_width).astype(bf16)
    at_home = lax.ppermute(
        jnp.concatenate([own_grads, own_last], axis=0),
        ("z", "mp"),
        [(a * mp_count + b, b * mp_count + a) for a in range(z_count) for b in range(mp_count)],
    )
    item_grad = at_home[:local_rows]
    last_rows_grad = at_home[local_rows:].astype(f32) + item_grad[:sub_count].astype(f32)
    row_ids = jnp.arange(token_count, dtype=jnp.int32)[:, None]
    for sub in range(sub_count):
        input_sum = input_sum + jnp.where(
            row_ids == last_rows[sub], last_rows_grad[sub][None, :], 0.0
        )
    input_grad = input_sum.astype(bf16).reshape(hidden_in.shape)
    summed, input_grad = lax.optimization_barrier((summed, input_grad))
    up_grad = summed[:, ranks].astype(f32)
    mean_loss = jnp.sum(summed[:x_count, ranks + 1 : ranks + 4, 0].astype(f32)) / batch_size
    down_grad = summed[:, :ranks].transpose(1, 0, 2).reshape(ranks, model_width).astype(f32).T
    return (
        mean_loss,
        query_grad,
        item_grad,
        input_grad,
        down_grad[:, :adapter_rank],
        down_grad[:, adapter_rank:],
        up_grad[:adapter_rank],
        up_grad[adapter_rank:],
    )


def solution(mesh):
    fine = Mesh(
        mesh.devices.reshape(8, 4, 2, mesh.devices.shape[1]), ("z", "x", "h", "mp")
    )
    in_specs = (
        P(DP, "mp"),
        P(DP, "mp"),
        P(DP),
        P(DP, None),
        P(None, DP, None, "mp"),
        P(None, DP),
        P(DP, "mp"),
        P(None, "mp"),
        P(None, "mp"),
        P("mp", DP),
        P(),
        P(None, "mp"),
        P(),
        P(None, "mp"),
    )
    out_specs = (
        P(),
        P(DP, "mp"),
        P(DP, "mp"),
        P(None, DP, None, "mp"),
        P(),
        P(),
        P(None, "mp"),
        P(None, "mp"),
    )
    return jax.shard_map(local, mesh=fine, in_specs=in_specs, out_specs=out_specs, check_vma=False)
```

```python
import functools
import math

import jax
import jax.numpy as jnp
from jax import lax
from jax.experimental import pallas as pl
from jax.experimental.pallas import tpu as pltpu
from jax.sharding import Mesh
from jax.sharding import PartitionSpec as P

HEADS = 32
KV_HEADS = 8
HEAD_DIM = 128
LANES = 128

INV_TEMP = 50.0
HARD_NEGATIVE_ADD = 4.0
ADAPTER_SCALE = 2.0

PLANE = ("x", "h")
DP = ("z", "x", "h")


def final_product(left_side, right_side):
    return lax.dot_general(
        left_side, right_side, (((1,), (1,)), ((), ())), preferred_element_type=jnp.float32
    )


def first_product(left_side, right_side):
    return lax.dot_general(
        left_side, right_side, (((0,), (0,)), ((), ())), preferred_element_type=jnp.float32
    )


def spread(block, axes):
    count = lax.axis_size(axes)
    copies = jnp.broadcast_to(block[None], (count,) + block.shape)
    return lax.all_to_all(copies, axes, split_axis=0, concat_axis=0, tiled=True)


def swap(blocks, axes):
    return lax.all_to_all(blocks, axes, split_axis=0, concat_axis=0, tiled=True)


def call(kernel, out_shape, flops, mebibytes=56):
    return pl.pallas_call(
        kernel,
        out_shape=out_shape,
        compiler_params=pltpu.CompilerParams(vmem_limit_bytes=mebibytes * 1024 * 1024),
        cost_estimate=pl.CostEstimate(flops=flops, bytes_accessed=2**20, transcendentals=4096),
    )


def upright(line):
    count = line.shape[1]
    row = lax.broadcasted_iota(jnp.int32, (count, count), 0)
    column = lax.broadcasted_iota(jnp.int32, (count, count), 1)
    return jnp.sum(jnp.where(row == column, line, 0), axis=1, keepdims=True)


def residual_kernel(
    z_count, plane_count, parts, hard, pair, tokens, chunks, residual_out, loss_out
):
    rows = parts.shape[1]
    batch_size = parts.shape[2]
    pair_scores = parts[0]
    for part in range(1, parts.shape[0]):
        pair_scores = pair_scores + parts[part]
    column = lax.broadcasted_iota(jnp.int32, (rows, batch_size), 1)
    inner = column % rows
    outer = column // rows
    item = ((outer % z_count) * plane_count + outer // z_count) * rows + inner
    count = jnp.zeros((rows, batch_size), jnp.float32)
    for choice in range(hard.shape[0]):
        count = count + jnp.where(upright(hard[choice : choice + 1]) == item, 1.0, 0.0)
    logits = pair_scores * INV_TEMP + HARD_NEGATIVE_ADD * count
    top = jnp.max(logits, axis=1, keepdims=True)
    log_total = top + jnp.log(jnp.sum(jnp.exp(logits - top), axis=1, keepdims=True))
    target = jnp.where(upright(pair[...]) == item, 1.0, 0.0)
    picked = jnp.sum(target * logits, axis=1, keepdims=True)
    loss = jnp.sum(log_total - picked, axis=0, keepdims=True)
    loss_out[...] = jnp.broadcast_to(loss, loss_out.shape)
    residual = jnp.exp(logits - log_total) - target
    residual_out[...] = residual.astype(jnp.bfloat16)
    width = z_count * rows
    pad = jnp.zeros((rows, LANES - width), jnp.float32)
    for plane in range(plane_count):
        block = jnp.concatenate([residual[:, plane * width : (plane + 1) * width], pad], axis=1)
        block = block.astype(jnp.bfloat16)
        for z in range(z_count):
            chunks[z * plane_count + plane, :, :LANES] = block
            chunks[z * plane_count + plane, :, LANES:] = tokens[z]


def token_kernel(tokens, key_weight, value_weight, down, key_up, value_up, low, keys, values):
    rank = key_up.shape[0]
    lows = jnp.dot(tokens[...], down[...], preferred_element_type=jnp.float32)
    lows = lows.astype(jnp.bfloat16)
    low[...] = lows
    for side, (weight, up, out) in enumerate(
        ((key_weight, key_up, keys), (value_weight, value_up, values))
    ):
        base = jnp.dot(tokens[...], weight[...], preferred_element_type=jnp.float32)
        mine = lows[:, side * rank : (side + 1) * rank]
        rise = jnp.dot(mine, up[...], preferred_element_type=jnp.float32)
        out[...] = (base + ADAPTER_SCALE * rise).astype(jnp.bfloat16)


def gradient_kernel(
    z_count, subs, received, queries, loss, wq_plane, wo_plane, item_out, parts_out
):
    item_rows = item_out.shape[0]
    width = received.shape[1] - LANES
    count = queries.shape[1] // width
    every = lax.dot_general(
        received[:, :LANES],
        queries[...],
        (((0,), (0,)), ((), ())),
        preferred_element_type=jnp.float32,
    )
    grads = (every[:item_rows] * INV_TEMP).astype(jnp.bfloat16)
    item_out[...] = grads
    picks = subs * z_count
    row = lax.broadcasted_iota(jnp.int32, (picks, item_rows), 0)
    column = lax.broadcasted_iota(jnp.int32, (picks, item_rows), 1)
    per_z = item_rows // z_count
    wanted = jnp.where((row // subs) * per_z + row % subs == column, 1.0, 0.0)
    cotangents = jnp.dot(
        wanted.astype(jnp.bfloat16), grads, preferred_element_type=jnp.float32
    )
    senders = received.shape[0] // per_z
    planes = senders // z_count
    row = lax.broadcasted_iota(jnp.int32, (picks, received.shape[0]), 0)
    column = lax.broadcasted_iota(jnp.int32, (picks, received.shape[0]), 1)
    plane = lax.axis_index(PLANE)
    first = ((row // subs) * planes + plane) * per_z + row % subs
    attn = query = None
    for block in range(count):
        cot = cotangents[:, block * width : (block + 1) * width]
        chosen = jnp.where(first + block * subs == column, 1.0, 0.0).astype(jnp.bfloat16)
        token = jnp.dot(chosen, received[:, LANES:], preferred_element_type=jnp.float32)
        rows = slice(block * width, (block + 1) * width)
        wq_rows, wo_rows = wq_plane[rows], wo_plane[rows]
        attn_term = jnp.dot(cot.astype(jnp.bfloat16), wo_rows, preferred_element_type=jnp.float32)
        query_term = jnp.dot(
            token.astype(jnp.bfloat16), wq_rows, preferred_element_type=jnp.float32
        )
        attn = attn_term if attn is None else attn + attn_term
        query = query_term if query is None else query + query_term
    end = attn.shape[1]
    for z in range(z_count):
        parts_out[z, :subs, :end] = attn[z * subs : (z + 1) * subs]
        parts_out[z, subs:, :end] = query[z * subs : (z + 1) * subs]
        parts_out[z, :, end:] = loss[: 2 * subs]


def attention_kernel(
    lengths,
    parts,
    keys,
    values,
    key_up,
    value_up,
    reduced,
    tokens,
    key_change_out,
    value_change_out,
    coef_out,
    loss_out,
    shares_out,
):
    subs = parts.shape[1] // 2
    token_count = keys.shape[0]
    seq_len = token_count // subs
    group = parts.shape[2] // HEAD_DIM - 1
    total = parts[0]
    for part in range(1, parts.shape[0]):
        total = total + parts[part]
    loss_out[...] = total[:, group * HEAD_DIM :]
    both = total.astype(jnp.bfloat16).astype(jnp.float32)

    def heads(first):
        return jnp.concatenate(
            [
                both[first + sub : first + sub + 1, head * HEAD_DIM : (head + 1) * HEAD_DIM]
                for sub in range(subs)
                for head in range(group)
            ],
            axis=0,
        )

    grad_heads = heads(0)
    q_heads = heads(subs)
    score_scale = 1.0 / math.sqrt(HEAD_DIM)
    raw = final_product(q_heads.astype(jnp.bfloat16), keys[...]) * score_scale
    row_sub = lax.broadcasted_iota(jnp.int32, raw.shape, 0) // group
    token = lax.broadcasted_iota(jnp.int32, raw.shape, 1)
    live = jnp.zeros(raw.shape, jnp.bool_)
    for sub in range(subs):
        first = sub * seq_len
        inside = (token >= first) & (token < first + lengths[0, sub])
        live = live | (inside & (row_sub == sub))
    raw = jnp.where(live, raw, -jnp.inf)
    weights = jnp.exp(raw - jnp.max(raw, axis=1, keepdims=True))
    probs = weights / jnp.sum(weights, axis=1, keepdims=True)
    prob_half = probs.astype(jnp.bfloat16).astype(jnp.float32)
    prob_grad = final_product(grad_heads.astype(jnp.bfloat16), values[...])
    score_grad = (
        probs * (prob_grad - jnp.sum(probs * prob_grad, axis=1, keepdims=True)) * score_scale
    )
    score_grad = score_grad.astype(jnp.bfloat16)
    delta = jnp.dot(score_grad, keys[...], preferred_element_type=jnp.float32)
    score_grad = score_grad.astype(jnp.float32)
    key_change = first_product(score_grad, q_heads).astype(jnp.bfloat16)
    value_change = first_product(prob_half, grad_heads).astype(jnp.bfloat16)
    key_coef = final_product(key_change, key_up[...])
    value_coef = final_product(value_change, value_up[...])
    coef = jnp.concatenate([key_coef, value_coef], axis=1).astype(jnp.bfloat16)
    key_change_out[...] = key_change
    value_change_out[...] = value_change
    coef_out[...] = coef
    rank = key_up.shape[0]
    ups = ADAPTER_SCALE * jnp.concatenate(
        [
            first_product(reduced[...], key_change)[:rank],
            first_product(reduced[...], value_change)[rank:],
        ],
        axis=0,
    )
    downs = ADAPTER_SCALE * first_product(coef, tokens[...])
    ranks = downs.shape[0]
    for chunk in range(shares_out.shape[0]):
        features = slice(chunk * LANES, (chunk + 1) * LANES)
        shares_out[chunk, :ranks] = downs[:, features].astype(jnp.bfloat16)
        own_up = jnp.broadcast_to(ups[chunk : chunk + 1], delta.shape)
        shares_out[chunk, ranks:] = jnp.concatenate([delta, own_up], axis=0).astype(jnp.bfloat16)


def portion_kernel(key_change, value_change, coef, key_weight, value_weight, down, out):
    width = 4 * LANES
    for start in range(0, out.shape[1], width):
        features = slice(start, start + width)
        portion = final_product(key_change[...], key_weight[features]) + final_product(
            value_change[...], value_weight[features]
        )
        portion = portion + ADAPTER_SCALE * jnp.dot(
            coef[...], down[:, features], preferred_element_type=jnp.float32
        )
        out[:, features] = portion.astype(jnp.bfloat16)


def home_kernel(z_count, subs, received, loss, wq_plane, out):
    senders, rows, _ = received.shape
    x_count = senders // z_count
    sides = 2 * subs * (wq_plane.shape[1] // LANES)
    ranks = rows - sides
    half = sides // 2
    total = received[0].astype(jnp.float32)
    for sender in range(1, senders):
        total = total + received[sender].astype(jnp.float32)
    deltas = jnp.concatenate(
        [
            received[z * x_count + lax.axis_index("x"), ranks:].astype(jnp.float32)[:half]
            for z in range(z_count)
        ],
        axis=0,
    ).astype(jnp.bfloat16)
    heads = half // subs
    picks = subs * z_count
    row = lax.broadcasted_iota(jnp.int32, (picks, deltas.shape[0]), 0)
    column = lax.broadcasted_iota(jnp.int32, (picks, deltas.shape[0]), 1)
    last = None
    for head in range(heads):
        wanted = jnp.where(row * heads + head == column, 1.0, 0.0).astype(jnp.bfloat16)
        delta = jnp.dot(wanted, deltas, preferred_element_type=jnp.float32).astype(jnp.bfloat16)
        term = final_product(delta, wq_plane[:, head * LANES : (head + 1) * LANES])
        last = term if last is None else last + term
    lines = [total[ranks + half : ranks + half + 1]]
    left = loss[:1]
    for _ in range(3):
        term = left.astype(jnp.bfloat16).astype(jnp.float32)
        lines.append(term)
        left = left - term
    lines.append(jnp.zeros((half - len(lines), LANES), jnp.float32))
    downs = total[:ranks].astype(jnp.bfloat16)
    copies = out.shape[0] // z_count
    for z in range(z_count):
        blocks = [
            last[z * subs + sub : z * subs + sub + 1, side * LANES : (side + 1) * LANES]
            for sub in range(subs)
            for side in range(heads)
        ]
        extra = jnp.concatenate(blocks + lines, axis=0).astype(jnp.bfloat16)
        for copy in range(copies):
            out[copy * z_count + z, :ranks] = downs
            out[copy * z_count + z, ranks:] = extra


def return_kernel(mp_count, received, out, last_out):
    senders, rows, _ = received.shape
    half = last_out.shape[0]
    ranks = rows - 2 * half
    total = received[0, :ranks].astype(jnp.float32)
    for sender in range(1, senders):
        total = total + received[sender, :ranks].astype(jnp.float32)
    lasts = None
    for other in range(mp_count):
        term = received[lax.axis_index("h") * mp_count + other, ranks:].astype(jnp.float32)[:half]
        lasts = term if lasts is None else lasts + term
    last_out[...] = lasts
    lines = None
    for side in range(senders // mp_count):
        term = received[side * mp_count + lax.axis_index("mp"), ranks:].astype(jnp.float32)[half:]
        lines = term if lines is None else lines + term
    left = lines[1:2] + lines[2:3] + lines[3:4]
    parts = [lines[:1]]
    for _ in range(3):
        term = left.astype(jnp.bfloat16).astype(jnp.float32)
        parts.append(term)
        left = left - term
    parts.append(jnp.zeros((2 * half - len(parts), LANES), jnp.float32))
    extra = jnp.concatenate(parts, axis=0).astype(jnp.bfloat16)
    downs = total.astype(jnp.bfloat16)
    for copy in range(out.shape[0]):
        out[copy, :ranks] = downs
        out[copy, ranks:] = extra


def local(
    query_emb,
    item_emb,
    pair_index,
    hard_index,
    hidden_in,
    lengths,
    w_query,
    key_weight_matrix,
    value_weight_matrix,
    w_out,
    key_down_matrix,
    key_up_matrix,
    value_down,
    value_up_matrix,
):
    bf16, f32 = jnp.bfloat16, jnp.float32
    x_count = lax.axis_size("x")
    z_count = lax.axis_size("z")
    plane_count = lax.axis_size(PLANE)
    dp_count = z_count * plane_count
    mp_count = lax.axis_size("mp")
    local_rows = query_emb.shape[0]
    batch_size = local_rows * dp_count
    feature_width = query_emb.shape[1]
    sub_count = hidden_in.shape[0]
    seq_len = hidden_in.shape[2]
    token_count = sub_count * seq_len
    full_rows = lax.all_gather(hidden_in, "mp", axis=3, tiled=True)
    model_width = full_rows.shape[3]
    token_inputs = full_rows.reshape(token_count, model_width)
    seq_lengths = lengths[:, 0]
    last_rows = jnp.arange(sub_count, dtype=jnp.int32) * seq_len + seq_lengths - 1

    core = lax.rem(lax.axis_index("mp"), 2)
    pair_rows = 2 * local_rows
    emb_pair = spread(jnp.concatenate([item_emb, query_emb], axis=0), ("h", "mp"))
    emb_pair = emb_pair.reshape(2, mp_count, pair_rows, feature_width)
    item_pair = lax.dynamic_index_in_dim(
        emb_pair[:, :, :local_rows], lax.axis_index("mp"), 1, keepdims=False
    ).reshape(pair_rows, feature_width)
    query_slices = lax.dynamic_index_in_dim(
        emb_pair[:, :, local_rows:], core, 0, keepdims=False
    )
    both = jnp.stack([w_query, w_out.T])
    both, query_slices = lax.optimization_barrier((both, query_slices))
    item_copies = jnp.broadcast_to(item_pair[None], (mp_count,) + item_pair.shape)
    chunks = jnp.concatenate([item_copies, query_slices], axis=1)
    chunks = jnp.broadcast_to(chunks[:, None], (z_count, x_count) + chunks.shape[1:])
    received = swap(chunks.reshape((z_count * x_count,) + chunks.shape[2:]), ("z", "x"))
    query_half = received[:, pair_rows:]
    other_half = lax.ppermute(query_half, "mp", [(a, a ^ 1) for a in range(mp_count)])
    queries_all = jnp.stack(
        [
            jnp.where(core == 0, query_half, other_half),
            jnp.where(core == 0, other_half, query_half),
        ],
        axis=1,
    ).reshape(batch_size, feature_width)
    items_all = (
        received[:, :pair_rows]
        .reshape(z_count, plane_count, local_rows, feature_width)
        .transpose(1, 0, 2, 3)
        .reshape(batch_size, feature_width)
    )
    partial_scores = final_product(query_emb, items_all)
    score_parts = spread(partial_scores, "mp")

    query_width = w_query.shape[1]
    other = lax.ppermute(both, "h", [(0, 1), (1, 0)])
    lower = lax.axis_index("h") == 0
    both = jnp.stack([jnp.where(lower, both, other), jnp.where(lower, other, both)])
    both = lax.all_gather(both, "x", axis=0, tiled=False)
    plane_shape = (feature_width, query_width)
    wq_plane = both[:, :, 0].reshape(plane_shape)
    wo_plane = both[:, :, 1].reshape(plane_shape)

    last_tokens = jnp.concatenate(
        [
            lax.dynamic_slice_in_dim(token_inputs, last_rows[sub], 1, 0)
            for sub in range(sub_count)
        ],
        axis=0,
    )
    last_slices = (
        last_tokens.reshape(sub_count, z_count, x_count, feature_width // x_count)
        .transpose(1, 2, 0, 3)
        .reshape(z_count, x_count * sub_count, feature_width // x_count)
    )

    chunks, residual, loss_part = call(
        functools.partial(residual_kernel, z_count, plane_count),
        (
            jax.ShapeDtypeStruct((dp_count, local_rows, 2 * LANES), bf16),
            jax.ShapeDtypeStruct((local_rows, batch_size), bf16),
            jax.ShapeDtypeStruct((local_rows, LANES), f32),
        ),
        2**24,
        8,
    )(score_parts, hard_index.T, pair_index[None], last_slices)
    column_rows = swap(chunks, DP).reshape(batch_size, 2 * LANES)
    adapter_rank = key_down_matrix.shape[1]
    up_width = key_up_matrix.shape[1]
    down_both = jnp.concatenate([key_down_matrix, value_down], axis=1)
    late_tokens, column_rows = lax.optimization_barrier((token_inputs, column_rows))
    head_shape = jax.ShapeDtypeStruct((token_count, up_width), bf16)
    low_shape = jax.ShapeDtypeStruct((token_count, 2 * adapter_rank), bf16)
    reduced_pair, key_rows, value_rows = call(
        token_kernel, (low_shape, head_shape, head_shape), 2**30
    )(
        late_tokens,
        key_weight_matrix,
        value_weight_matrix,
        down_both,
        key_up_matrix,
        value_up_matrix,
    )
    column_grads, parts = call(
        functools.partial(gradient_kernel, z_count, sub_count),
        (
            jax.ShapeDtypeStruct((z_count * local_rows, feature_width), bf16),
            jax.ShapeDtypeStruct((z_count, 2 * sub_count, query_width + LANES), f32),
        ),
        2**26,
        8,
    )(column_rows, queries_all, loss_part, wq_plane, wo_plane)
    parts = swap(parts, "z")
    query_grad = (jnp.dot(residual, items_all, preferred_element_type=f32) * INV_TEMP).astype(bf16)

    ranks = 2 * adapter_rank
    share_shape = (z_count * x_count, ranks + 2 * sub_count * query_width // LANES, LANES)
    key_change, value_change, coef, loss_part, shares = call(
        attention_kernel,
        (
            head_shape,
            head_shape,
            low_shape,
            jax.ShapeDtypeStruct((2 * sub_count, LANES), f32),
            jax.ShapeDtypeStruct(share_shape, bf16),
        ),
        2**26,
    )(
        lengths.T,
        parts,
        key_rows,
        value_rows,
        key_up_matrix,
        value_up_matrix,
        reduced_pair,
        token_inputs,
    )
    shares = swap(shares, ("z", "x"))

    portion = call(portion_kernel, jax.ShapeDtypeStruct((token_count, model_width), bf16), 2**30)(
        key_change, value_change, coef, key_weight_matrix, value_weight_matrix, down_both.T
    )
    shares, portion = lax.optimization_barrier((shares, portion))
    input_sum = lax.psum_scatter(portion, "mp", scatter_dimension=1, tiled=True).astype(f32)
    middle = call(
        functools.partial(home_kernel, z_count, sub_count),
        jax.ShapeDtypeStruct((2 * mp_count,) + share_shape[1:], bf16),
        2**26,
        8,
    )(shares, loss_part, wq_plane)
    chunks, last_part = call(
        functools.partial(return_kernel, mp_count),
        (
            jax.ShapeDtypeStruct(share_shape, bf16),
            jax.ShapeDtypeStruct((sub_count * query_width // LANES, LANES), f32),
        ),
        2**24,
        8,
    )(swap(middle, ("h", "mp")))
    summed = swap(chunks, ("z", "x"))
    own_grads = lax.dynamic_index_in_dim(
        column_grads.reshape(z_count, local_rows, feature_width),
        lax.axis_index("mp"),
        0,
        keepdims=False,
    )
    own_last = last_part.reshape(sub_count, feature_width).astype(bf16)
    at_home = lax.ppermute(
        jnp.concatenate([own_grads, own_last], axis=0),
        ("z", "mp"),
        [(a * mp_count + b, b * mp_count + a) for a in range(z_count) for b in range(mp_count)],
    )
    item_grad = at_home[:local_rows]
    last_rows_grad = at_home[local_rows:].astype(f32) + item_grad[:sub_count].astype(f32)
    row_ids = jnp.arange(token_count, dtype=jnp.int32)[:, None]
    for sub in range(sub_count):
        input_sum = input_sum + jnp.where(
            row_ids == last_rows[sub], last_rows_grad[sub][None, :], 0.0
        )
    input_grad = input_sum.astype(bf16).reshape(hidden_in.shape)
    summed, input_grad = lax.optimization_barrier((summed, input_grad))
    up_grad = summed[:, ranks].astype(f32)
    mean_loss = jnp.sum(summed[:x_count, ranks + 1 : ranks + 4, 0].astype(f32)) / batch_size
    down_grad = summed[:, :ranks].transpose(1, 0, 2).reshape(ranks, model_width).astype(f32).T
    return (
        mean_loss,
        query_grad,
        item_grad,
        input_grad,
        down_grad[:, :adapter_rank],
        down_grad[:, adapter_rank:],
        up_grad[:adapter_rank],
        up_grad[adapter_rank:],
    )


def solution(mesh):
    fine = Mesh(
        mesh.devices.reshape(8, 4, 2, mesh.devices.shape[1]), ("z", "x", "h", "mp")
    )
    in_specs = (
        P(DP, "mp"),
        P(DP, "mp"),
        P(DP),
        P(DP, None),
        P(None, DP, None, "mp"),
        P(None, DP),
        P(DP, "mp"),
        P(None, "mp"),
        P(None, "mp"),
        P("mp", DP),
        P(),
        P(None, "mp"),
        P(),
        P(None, "mp"),
    )
    out_specs = (
        P(),
        P(DP, "mp"),
        P(DP, "mp"),
        P(None, DP, None, "mp"),
        P(),
        P(),
        P(None, "mp"),
        P(None, "mp"),
    )
    return jax.shard_map(local, mesh=fine, in_specs=in_specs, out_specs=out_specs, check_vma=False)
```

```python
import functools
import math

import jax
import jax.numpy as jnp
from jax import lax
from jax.experimental import pallas as pl
from jax.experimental.pallas import tpu as pltpu
from jax.sharding import Mesh
from jax.sharding import PartitionSpec as P

HEADS = 32
KV_HEADS = 8
HEAD_DIM = 128
LANES = 128

INV_TEMP = 50.0
HARD_NEGATIVE_ADD = 4.0
ADAPTER_SCALE = 2.0

PLANE = ("x", "h")
DP = ("z", "x", "h")


def final_product(left_side, right_side):
    return lax.dot_general(
        left_side, right_side, (((1,), (1,)), ((), ())), preferred_element_type=jnp.float32
    )


def first_product(left_side, right_side):
    return lax.dot_general(
        left_side, right_side, (((0,), (0,)), ((), ())), preferred_element_type=jnp.float32
    )


def spread(block, axes):
    count = lax.axis_size(axes)
    copies = jnp.broadcast_to(block[None], (count,) + block.shape)
    return lax.all_to_all(copies, axes, split_axis=0, concat_axis=0, tiled=True)


def swap(blocks, axes):
    return lax.all_to_all(blocks, axes, split_axis=0, concat_axis=0, tiled=True)


def call(kernel, out_shape, flops, mebibytes=56):
    return pl.pallas_call(
        kernel,
        out_shape=out_shape,
        compiler_params=pltpu.CompilerParams(vmem_limit_bytes=mebibytes * 1024 * 1024),
        cost_estimate=pl.CostEstimate(flops=flops, bytes_accessed=2**20, transcendentals=4096),
    )


def upright(line):
    count = line.shape[1]
    row = lax.broadcasted_iota(jnp.int32, (count, count), 0)
    column = lax.broadcasted_iota(jnp.int32, (count, count), 1)
    return jnp.sum(jnp.where(row == column, line, 0), axis=1, keepdims=True)


def residual_kernel(
    z_count, plane_count, parts, hard, pair, tokens, chunks, residual_out, loss_out
):
    rows = parts.shape[1]
    batch_size = parts.shape[2]
    pair_scores = parts[0]
    for part in range(1, parts.shape[0]):
        pair_scores = pair_scores + parts[part]
    column = lax.broadcasted_iota(jnp.int32, (rows, batch_size), 1)
    inner = column % rows
    outer = column // rows
    item = ((outer % z_count) * plane_count + outer // z_count) * rows + inner
    count = jnp.zeros((rows, batch_size), jnp.float32)
    for choice in range(hard.shape[0]):
        count = count + jnp.where(upright(hard[choice : choice + 1]) == item, 1.0, 0.0)
    logits = pair_scores * INV_TEMP + HARD_NEGATIVE_ADD * count
    top = jnp.max(logits, axis=1, keepdims=True)
    log_total = top + jnp.log(jnp.sum(jnp.exp(logits - top), axis=1, keepdims=True))
    target = jnp.where(upright(pair[...]) == item, 1.0, 0.0)
    picked = jnp.sum(target * logits, axis=1, keepdims=True)
    loss = jnp.sum(log_total - picked, axis=0, keepdims=True)
    loss_out[...] = jnp.broadcast_to(loss, loss_out.shape)
    residual = jnp.exp(logits - log_total) - target
    residual_out[...] = residual.astype(jnp.bfloat16)
    width = z_count * rows
    pad = jnp.zeros((rows, LANES - width), jnp.float32)
    for plane in range(plane_count):
        block = jnp.concatenate([residual[:, plane * width : (plane + 1) * width], pad], axis=1)
        block = block.astype(jnp.bfloat16)
        for z in range(z_count):
            chunks[z * plane_count + plane, :, :LANES] = block
            chunks[z * plane_count + plane, :, LANES:] = tokens[z]


def token_kernel(tokens, key_weight, value_weight, down, key_up, value_up, low, keys, values):
    rank = key_up.shape[0]
    lows = jnp.dot(tokens[...], down[...], preferred_element_type=jnp.float32)
    lows = lows.astype(jnp.bfloat16)
    low[...] = lows
    for side, (weight, up, out) in enumerate(
        ((key_weight, key_up, keys), (value_weight, value_up, values))
    ):
        base = jnp.dot(tokens[...], weight[...], preferred_element_type=jnp.float32)
        mine = lows[:, side * rank : (side + 1) * rank]
        rise = jnp.dot(mine, up[...], preferred_element_type=jnp.float32)
        out[...] = (base + ADAPTER_SCALE * rise).astype(jnp.bfloat16)


def gradient_kernel(
    z_count, subs, received, queries, loss, wq_plane, wo_plane, item_out, parts_out
):
    item_rows = item_out.shape[0]
    width = received.shape[1] - LANES
    count = queries.shape[1] // width
    every = lax.dot_general(
        received[:, :LANES],
        queries[...],
        (((0,), (0,)), ((), ())),
        preferred_element_type=jnp.float32,
    )
    grads = (every[:item_rows] * INV_TEMP).astype(jnp.bfloat16)
    item_out[...] = grads
    picks = subs * z_count
    row = lax.broadcasted_iota(jnp.int32, (picks, item_rows), 0)
    column = lax.broadcasted_iota(jnp.int32, (picks, item_rows), 1)
    per_z = item_rows // z_count
    wanted = jnp.where((row // subs) * per_z + row % subs == column, 1.0, 0.0)
    cotangents = jnp.dot(
        wanted.astype(jnp.bfloat16), grads, preferred_element_type=jnp.float32
    )
    senders = received.shape[0] // per_z
    planes = senders // z_count
    row = lax.broadcasted_iota(jnp.int32, (picks, received.shape[0]), 0)
    column = lax.broadcasted_iota(jnp.int32, (picks, received.shape[0]), 1)
    plane = lax.axis_index(PLANE)
    first = ((row // subs) * planes + plane) * per_z + row % subs
    attn = query = None
    for block in range(count):
        cot = cotangents[:, block * width : (block + 1) * width]
        chosen = jnp.where(first + block * subs == column, 1.0, 0.0).astype(jnp.bfloat16)
        token = jnp.dot(chosen, received[:, LANES:], preferred_element_type=jnp.float32)
        rows = slice(block * width, (block + 1) * width)
        wq_rows, wo_rows = wq_plane[rows], wo_plane[rows]
        attn_term = jnp.dot(cot.astype(jnp.bfloat16), wo_rows, preferred_element_type=jnp.float32)
        query_term = jnp.dot(
            token.astype(jnp.bfloat16), wq_rows, preferred_element_type=jnp.float32
        )
        attn = attn_term if attn is None else attn + attn_term
        query = query_term if query is None else query + query_term
    end = attn.shape[1]
    for z in range(z_count):
        parts_out[z, :subs, :end] = attn[z * subs : (z + 1) * subs]
        parts_out[z, subs:, :end] = query[z * subs : (z + 1) * subs]
        parts_out[z, :, end:] = loss[: 2 * subs]


def attention_kernel(
    lengths,
    parts,
    keys,
    values,
    key_up,
    value_up,
    reduced,
    tokens,
    key_change_out,
    value_change_out,
    coef_out,
    loss_out,
    shares_out,
):
    subs = parts.shape[1] // 2
    token_count = keys.shape[0]
    seq_len = token_count // subs
    group = parts.shape[2] // HEAD_DIM - 1
    total = parts[0]
    for part in range(1, parts.shape[0]):
        total = total + parts[part]
    loss_out[...] = total[:, group * HEAD_DIM :]
    both = total.astype(jnp.bfloat16).astype(jnp.float32)

    def heads(first):
        return jnp.concatenate(
            [
                both[first + sub : first + sub + 1, head * HEAD_DIM : (head + 1) * HEAD_DIM]
                for sub in range(subs)
                for head in range(group)
            ],
            axis=0,
        )

    grad_heads = heads(0)
    q_heads = heads(subs)
    score_scale = 1.0 / math.sqrt(HEAD_DIM)
    raw = final_product(q_heads.astype(jnp.bfloat16), keys[...]) * score_scale
    row_sub = lax.broadcasted_iota(jnp.int32, raw.shape, 0) // group
    token = lax.broadcasted_iota(jnp.int32, raw.shape, 1)
    live = jnp.zeros(raw.shape, jnp.bool_)
    for sub in range(subs):
        first = sub * seq_len
        inside = (token >= first) & (token < first + lengths[0, sub])
        live = live | (inside & (row_sub == sub))
    raw = jnp.where(live, raw, -jnp.inf)
    weights = jnp.exp(raw - jnp.max(raw, axis=1, keepdims=True))
    probs = weights / jnp.sum(weights, axis=1, keepdims=True)
    prob_half = probs.astype(jnp.bfloat16).astype(jnp.float32)
    prob_grad = final_product(grad_heads.astype(jnp.bfloat16), values[...])
    score_grad = (
        probs * (prob_grad - jnp.sum(probs * prob_grad, axis=1, keepdims=True)) * score_scale
    )
    score_grad = score_grad.astype(jnp.bfloat16)
    delta = jnp.dot(score_grad, keys[...], preferred_element_type=jnp.float32)
    score_grad = score_grad.astype(jnp.float32)
    key_change = first_product(score_grad, q_heads).astype(jnp.bfloat16)
    value_change = first_product(prob_half, grad_heads).astype(jnp.bfloat16)
    key_coef = final_product(key_change, key_up[...])
    value_coef = final_product(value_change, value_up[...])
    coef = jnp.concatenate([key_coef, value_coef], axis=1).astype(jnp.bfloat16)
    key_change_out[...] = key_change
    value_change_out[...] = value_change
    coef_out[...] = coef
    rank = key_up.shape[0]
    ups = ADAPTER_SCALE * jnp.concatenate(
        [
            first_product(reduced[...], key_change)[:rank],
            first_product(reduced[...], value_change)[rank:],
        ],
        axis=0,
    )
    downs = ADAPTER_SCALE * first_product(coef, tokens[...])
    ranks = downs.shape[0]
    for chunk in range(shares_out.shape[0]):
        features = slice(chunk * LANES, (chunk + 1) * LANES)
        shares_out[chunk, :ranks] = downs[:, features].astype(jnp.bfloat16)
        own_up = jnp.broadcast_to(ups[chunk : chunk + 1], delta.shape)
        shares_out[chunk, ranks:] = jnp.concatenate([delta, own_up], axis=0).astype(jnp.bfloat16)


def portion_kernel(key_change, value_change, coef, key_weight, value_weight, down, out):
    width = 4 * LANES
    for start in range(0, out.shape[1], width):
        features = slice(start, start + width)
        portion = final_product(key_change[...], key_weight[features]) + final_product(
            value_change[...], value_weight[features]
        )
        portion = portion + ADAPTER_SCALE * jnp.dot(
            coef[...], down[:, features], preferred_element_type=jnp.float32
        )
        out[:, features] = portion.astype(jnp.bfloat16)


def home_kernel(z_count, subs, received, loss, wq_plane, out):
    senders, rows, _ = received.shape
    x_count = senders // z_count
    sides = 2 * subs * (wq_plane.shape[1] // LANES)
    ranks = rows - sides
    half = sides // 2
    total = received[0].astype(jnp.float32)
    for sender in range(1, senders):
        total = total + received[sender].astype(jnp.float32)
    deltas = jnp.concatenate(
        [
            received[z * x_count + lax.axis_index("x"), ranks:].astype(jnp.float32)[:half]
            for z in range(z_count)
        ],
        axis=0,
    ).astype(jnp.bfloat16)
    heads = half // subs
    picks = subs * z_count
    row = lax.broadcasted_iota(jnp.int32, (picks, deltas.shape[0]), 0)
    column = lax.broadcasted_iota(jnp.int32, (picks, deltas.shape[0]), 1)
    last = None
    for head in range(heads):
        wanted = jnp.where(row * heads + head == column, 1.0, 0.0).astype(jnp.bfloat16)
        delta = jnp.dot(wanted, deltas, preferred_element_type=jnp.float32).astype(jnp.bfloat16)
        term = final_product(delta, wq_plane[:, head * LANES : (head + 1) * LANES])
        last = term if last is None else last + term
    lines = [total[ranks + half : ranks + half + 1]]
    left = loss[:1]
    for _ in range(3):
        term = left.astype(jnp.bfloat16).astype(jnp.float32)
        lines.append(term)
        left = left - term
    lines.append(jnp.zeros((half - len(lines), LANES), jnp.float32))
    downs = total[:ranks].astype(jnp.bfloat16)
    copies = out.shape[0] // z_count
    for z in range(z_count):
        blocks = [
            last[z * subs + sub : z * subs + sub + 1, side * LANES : (side + 1) * LANES]
            for sub in range(subs)
            for side in range(heads)
        ]
        extra = jnp.concatenate(blocks + lines, axis=0).astype(jnp.bfloat16)
        for copy in range(copies):
            out[copy * z_count + z, :ranks] = downs
            out[copy * z_count + z, ranks:] = extra


def return_kernel(mp_count, received, out, last_out):
    senders, rows, _ = received.shape
    half = last_out.shape[0]
    ranks = rows - 2 * half
    total = received[0, :ranks].astype(jnp.float32)
    for sender in range(1, senders):
        total = total + received[sender, :ranks].astype(jnp.float32)
    lasts = None
    for other in range(mp_count):
        term = received[lax.axis_index("h") * mp_count + other, ranks:].astype(jnp.float32)[:half]
        lasts = term if lasts is None else lasts + term
    last_out[...] = lasts
    lines = None
    for side in range(senders // mp_count):
        term = received[side * mp_count + lax.axis_index("mp"), ranks:].astype(jnp.float32)[half:]
        lines = term if lines is None else lines + term
    left = lines[1:2] + lines[2:3] + lines[3:4]
    parts = [lines[:1]]
    for _ in range(3):
        term = left.astype(jnp.bfloat16).astype(jnp.float32)
        parts.append(term)
        left = left - term
    parts.append(jnp.zeros((2 * half - len(parts), LANES), jnp.float32))
    extra = jnp.concatenate(parts, axis=0).astype(jnp.bfloat16)
    downs = total.astype(jnp.bfloat16)
    for copy in range(out.shape[0]):
        out[copy, :ranks] = downs
        out[copy, ranks:] = extra


def local(
    query_emb,
    item_emb,
    pair_index,
    hard_index,
    hidden_in,
    lengths,
    w_query,
    key_weight_matrix,
    value_weight_matrix,
    w_out,
    key_down_matrix,
    key_up_matrix,
    value_down,
    value_up_matrix,
):
    bf16, f32 = jnp.bfloat16, jnp.float32
    x_count = lax.axis_size("x")
    z_count = lax.axis_size("z")
    plane_count = lax.axis_size(PLANE)
    dp_count = z_count * plane_count
    mp_count = lax.axis_size("mp")
    local_rows = query_emb.shape[0]
    batch_size = local_rows * dp_count
    feature_width = query_emb.shape[1]
    sub_count = hidden_in.shape[0]
    seq_len = hidden_in.shape[2]
    token_count = sub_count * seq_len
    full_rows = lax.all_gather(hidden_in, "mp", axis=3, tiled=True)
    model_width = full_rows.shape[3]
    token_inputs = full_rows.reshape(token_count, model_width)
    seq_lengths = lengths[:, 0]
    last_rows = jnp.arange(sub_count, dtype=jnp.int32) * seq_len + seq_lengths - 1

    core = lax.rem(lax.axis_index("mp"), 2)
    pair_rows = 2 * local_rows
    emb_pair = spread(jnp.concatenate([item_emb, query_emb], axis=0), ("h", "mp"))
    emb_pair = emb_pair.reshape(2, mp_count, pair_rows, feature_width)
    item_pair = lax.dynamic_index_in_dim(
        emb_pair[:, :, :local_rows], lax.axis_index("mp"), 1, keepdims=False
    ).reshape(pair_rows, feature_width)
    query_slices = lax.dynamic_index_in_dim(
        emb_pair[:, :, local_rows:], core, 0, keepdims=False
    )
    both = jnp.stack([w_query, w_out.T])
    both, query_slices = lax.optimization_barrier((both, query_slices))
    item_copies = jnp.broadcast_to(item_pair[None], (mp_count,) + item_pair.shape)
    chunks = jnp.concatenate([item_copies, query_slices], axis=1)
    chunks = jnp.broadcast_to(chunks[:, None], (z_count, x_count) + chunks.shape[1:])
    received = swap(chunks.reshape((z_count * x_count,) + chunks.shape[2:]), ("z", "x"))
    query_half = received[:, pair_rows:]
    other_half = lax.ppermute(query_half, "mp", [(a, a ^ 1) for a in range(mp_count)])
    queries_all = jnp.stack(
        [
            jnp.where(core == 0, query_half, other_half),
            jnp.where(core == 0, other_half, query_half),
        ],
        axis=1,
    ).reshape(batch_size, feature_width)
    items_all = (
        received[:, :pair_rows]
        .reshape(z_count, plane_count, local_rows, feature_width)
        .transpose(1, 0, 2, 3)
        .reshape(batch_size, feature_width)
    )
    partial_scores = final_product(query_emb, items_all)
    score_parts = spread(partial_scores, "mp")

    query_width = w_query.shape[1]
    other = lax.ppermute(both, "h", [(0, 1), (1, 0)])
    lower = lax.axis_index("h") == 0
    both = jnp.stack([jnp.where(lower, both, other), jnp.where(lower, other, both)])
    both = lax.all_gather(both, "x", axis=0, tiled=False)
    plane_shape = (feature_width, query_width)
    wq_plane = both[:, :, 0].reshape(plane_shape)
    wo_plane = both[:, :, 1].reshape(plane_shape)

    last_tokens = jnp.concatenate(
        [
            lax.dynamic_slice_in_dim(token_inputs, last_rows[sub], 1, 0)
            for sub in range(sub_count)
        ],
        axis=0,
    )
    last_slices = (
        last_tokens.reshape(sub_count, z_count, x_count, feature_width // x_count)
        .transpose(1, 2, 0, 3)
        .reshape(z_count, x_count * sub_count, feature_width // x_count)
    )

    chunks, residual, loss_part = call(
        functools.partial(residual_kernel, z_count, plane_count),
        (
            jax.ShapeDtypeStruct((dp_count, local_rows, 2 * LANES), bf16),
            jax.ShapeDtypeStruct((local_rows, batch_size), bf16),
            jax.ShapeDtypeStruct((local_rows, LANES), f32),
        ),
        2**24,
        8,
    )(score_parts, hard_index.T, pair_index[None], last_slices)
    column_rows = swap(chunks, DP).reshape(batch_size, 2 * LANES)
    adapter_rank = key_down_matrix.shape[1]
    up_width = key_up_matrix.shape[1]
    down_both = jnp.concatenate([key_down_matrix, value_down], axis=1)
    late_tokens, column_rows = lax.optimization_barrier((token_inputs, column_rows))
    head_shape = jax.ShapeDtypeStruct((token_count, up_width), bf16)
    low_shape = jax.ShapeDtypeStruct((token_count, 2 * adapter_rank), bf16)
    reduced_pair, key_rows, value_rows = call(
        token_kernel, (low_shape, head_shape, head_shape), 2**30
    )(
        late_tokens,
        key_weight_matrix,
        value_weight_matrix,
        down_both,
        key_up_matrix,
        value_up_matrix,
    )
    column_grads, parts = call(
        functools.partial(gradient_kernel, z_count, sub_count),
        (
            jax.ShapeDtypeStruct((z_count * local_rows, feature_width), bf16),
            jax.ShapeDtypeStruct((z_count, 2 * sub_count, query_width + LANES), f32),
        ),
        2**26,
        8,
    )(column_rows, queries_all, loss_part, wq_plane, wo_plane)
    parts = swap(parts, "z")
    query_grad = (jnp.dot(residual, items_all, preferred_element_type=f32) * INV_TEMP).astype(bf16)

    ranks = 2 * adapter_rank
    share_shape = (z_count * x_count, ranks + 2 * sub_count * query_width // LANES, LANES)
    key_change, value_change, coef, loss_part, shares = call(
        attention_kernel,
        (
            head_shape,
            head_shape,
            low_shape,
            jax.ShapeDtypeStruct((2 * sub_count, LANES), f32),
            jax.ShapeDtypeStruct(share_shape, bf16),
        ),
        2**26,
    )(
        lengths.T,
        parts,
        key_rows,
        value_rows,
        key_up_matrix,
        value_up_matrix,
        reduced_pair,
        token_inputs,
    )
    shares = swap(shares, ("z", "x"))

    portion = call(portion_kernel, jax.ShapeDtypeStruct((token_count, model_width), bf16), 2**30)(
        key_change, value_change, coef, key_weight_matrix, value_weight_matrix, down_both.T
    )
    shares, portion = lax.optimization_barrier((shares, portion))
    input_sum = lax.psum_scatter(portion, "mp", scatter_dimension=1, tiled=True).astype(f32)
    middle = call(
        functools.partial(home_kernel, z_count, sub_count),
        jax.ShapeDtypeStruct((2 * mp_count,) + share_shape[1:], bf16),
        2**26,
        8,
    )(shares, loss_part, wq_plane)
    chunks, last_part = call(
        functools.partial(return_kernel, mp_count),
        (
            jax.ShapeDtypeStruct(share_shape, bf16),
            jax.ShapeDtypeStruct((sub_count * query_width // LANES, LANES), f32),
        ),
        2**24,
        8,
    )(swap(middle, ("h", "mp")))
    summed = swap(chunks, ("z", "x"))
    own_grads = lax.dynamic_index_in_dim(
        column_grads.reshape(z_count, local_rows, feature_width),
        lax.axis_index("mp"),
        0,
        keepdims=False,
    )
    own_last = last_part.reshape(sub_count, feature_width).astype(bf16)
    at_home = lax.ppermute(
        jnp.concatenate([own_grads, own_last], axis=0),
        ("z", "mp"),
        [(a * mp_count + b, b * mp_count + a) for a in range(z_count) for b in range(mp_count)],
    )
    item_grad = at_home[:local_rows]
    last_rows_grad = at_home[local_rows:].astype(f32) + item_grad[:sub_count].astype(f32)
    row_ids = jnp.arange(token_count, dtype=jnp.int32)[:, None]
    for sub in range(sub_count):
        input_sum = input_sum + jnp.where(
            row_ids == last_rows[sub], last_rows_grad[sub][None, :], 0.0
        )
    input_grad = input_sum.astype(bf16).reshape(hidden_in.shape)
    up_grad = summed[:, ranks].astype(f32)
    mean_loss = jnp.sum(summed[:x_count, ranks + 1 : ranks + 4, 0].astype(f32)) / batch_size
    down_grad = summed[:, :ranks].transpose(1, 0, 2).reshape(ranks, model_width).astype(f32).T
    return (
        mean_loss,
        query_grad,
        item_grad,
        input_grad,
        down_grad[:, :adapter_rank],
        down_grad[:, adapter_rank:],
        up_grad[:adapter_rank],
        up_grad[adapter_rank:],
    )


def solution(mesh):
    fine = Mesh(
        mesh.devices.reshape(8, 4, 2, mesh.devices.shape[1]), ("z", "x", "h", "mp")
    )
    in_specs = (
        P(DP, "mp"),
        P(DP, "mp"),
        P(DP),
        P(DP, None),
        P(None, DP, None, "mp"),
        P(None, DP),
        P(DP, "mp"),
        P(None, "mp"),
        P(None, "mp"),
        P("mp", DP),
        P(),
        P(None, "mp"),
        P(),
        P(None, "mp"),
    )
    out_specs = (
        P(),
        P(DP, "mp"),
        P(DP, "mp"),
        P(None, DP, None, "mp"),
        P(),
        P(),
        P(None, "mp"),
        P(None, "mp"),
    )
    return jax.shard_map(local, mesh=fine, in_specs=in_specs, out_specs=out_specs, check_vma=False)
```
